128 devices in a mesh: dp: 8 (over z_lo, x), vocab: 16 (over z_hi, y, core).
Axes of the slice: x: 4, y: 4, z: 4 (z_hi: 2, z_lo: 2; z = z_hi * 2 + z_lo), core: 2. Of those that a mesh axis runs over, the one named last changes fastest.
Arguments:
- hidden: bfloat16 [2048, 2048], P('dp'), may hold values from -40 to 40
- norm_gain: float32 [2048], replicated, may hold values from 0.1 to 1.9
- head_weight: bfloat16 [2048, 64128], P(None, 'vocab'), may hold values from -1.0617864 to 1.0617864
- teacher: bfloat16 [2048, 64128], P(('dp', 'vocab')), may hold values from -40 to 256
- labels: int32 [2048], P('dp'), may hold values from 0 to 64127
- cotangent: float32 [2048], P('dp'), may hold values from 2 to 16
Outputs:
- hidden_grad: bfloat16 [2048, 2048], P('dp', 'vocab')
- per_token_loss: float32 [2048], P('dp')
The draws below stay inside these ranges and needn't reach their ends.
All inputs are finite; a program needn't handle non-finite values.
Results may differ from the reference program's by a relative error of at most 0.0093.
Values may be sent and summed in bfloat16 or wider, within the bound.
A program may use at most 128 MiB of HBM per device.

```python
import math
import jax
import jax.numpy as jnp
import numpy as np
from jax import lax

D = 2048
VOCAB = 64128
TOK_DEV = 256
TOKENS = 2048


def draw_hidden(key, part):
    key = jax.random.fold_in(key, 1)
    noise_key, scale_key = jax.random.split(key, 2)
    noise = jnp.clip(jax.random.normal(noise_key, (TOKENS, D), jnp.float32), -6.0, 6.0)
    row_scale = jnp.exp(jax.random.uniform(scale_key, (TOKENS, 1), jnp.float32, -0.7, 0.7))
    values = noise * row_scale
    return values.astype(jnp.bfloat16)


def draw_head_weight(key, part):
    key = jax.random.fold_in(key, 2)
    noise_key, scale_key = jax.random.split(key, 2)
    base = jnp.clip(jax.random.normal(noise_key, (D, VOCAB), jnp.float32), -4.0, 4.0) * (3.0 / math.sqrt(D))
    column_scale = jnp.exp(jax.random.uniform(scale_key, (1, VOCAB), jnp.float32, -0.4, 0.4))
    values = base * column_scale
    return values.astype(jnp.bfloat16)


def draw_teacher(key, part):
    key = jax.random.fold_in(key, 3)
    noise_key, scale_key, bias_key = jax.random.split(key, 3)
    column_float = lax.broadcasted_iota(jnp.float32, (1, VOCAB), 1)
    bias = jax.random.uniform(bias_key, (1, VOCAB), jnp.float32, -2.0, 2.0) + 2.0 * math.log(3.0) * column_float / VOCAB
    noise = jnp.clip(jax.random.normal(noise_key, (TOKENS, VOCAB), jnp.float32), -6.0, 6.0)
    row_scale = jnp.exp(jax.random.uniform(scale_key, (TOKENS, 1), jnp.float32, -0.5, 0.5))
    values = jnp.clip(3.0 * row_scale * noise + bias, -40.0, 40.0)
    return values.astype(jnp.bfloat16)


def touch_ends(drawn, rng, smallest, largest):
    spot = [jax.random.randint(jax.random.fold_in(rng, axis), (), 0, length) for axis, length in enumerate(drawn.shape)]
    main_axis = drawn.shape.index(max(drawn.shape))
    next_to = spot[:main_axis] + [(spot[main_axis] + 1) % drawn.shape[main_axis]] + spot[main_axis + 1:]
    return drawn.at[tuple(spot)].set(smallest).at[tuple(next_to)].set(largest)


def block_levels(rng, dims, shards, low, largest):
    level = 1.0
    for axis_at, shards_of in shards:
        steps = jax.random.uniform(jax.random.fold_in(jax.random.fold_in(rng, 6), axis_at), (shards_of,), jnp.float32, low / len(shards), largest / len(shards))
        level = level * jnp.repeat(jnp.exp(steps), dims[axis_at] // shards_of).reshape((-1,) + (1,) * (len(dims) - 1 - axis_at))
    return level


def rank_bounds(number_of, lean):
    loads = [(1 << 20) // math.isqrt(standing ** lean) + 1 for standing in range(1, number_of + 1)]
    deviation = 1 + sum(loads) // (1 << 30)
    return np.cumsum(np.array([max(1, weight // deviation) for weight in loads]))


def ranked(key, shape, amount, lean):
    grid = rank_bounds(amount, lean)
    pick = jax.random.randint(jax.random.fold_in(key, 1), shape, 0, int(grid[amount - 1]))
    standing = jnp.searchsorted(jnp.asarray(grid, jnp.int32), pick, side="right")
    return jax.random.permutation(jax.random.fold_in(key, 2), amount)[standing].astype(jnp.int32)


def setup_inputs(seed: int = 0) -> dict:
    key_of = jax.random.split(jax.random.key(seed), 7)
    hidden = draw_hidden(jax.random.fold_in(key_of[6], 71), 0)
    norm_gain = jnp.clip(1.0 + 0.18 * jax.random.normal(key_of[1], (D,), jnp.float32), 0.1, 1.9)
    head_weight = draw_head_weight(jax.random.fold_in(key_of[6], 71), 0)
    teacher = draw_teacher(jax.random.fold_in(key_of[6], 71), 0)
    labels = touch_ends(ranked(key_of[4], (TOKENS,), VOCAB, 2), jax.random.fold_in(key_of[4], 3), 0, VOCAB - 1).astype(jnp.int32)
    cotangent = jnp.clip(jnp.exp(math.log(16.0) - 2.0794415 * jax.random.uniform(key_of[5], (TOKENS,), jnp.float32) ** block_levels(key_of[5], (TOKENS,), ((0, 8),), -0.2, 0.2)), 2.0, 16.0)
    return {"hidden": hidden, "norm_gain": norm_gain, "head_weight": head_weight, "teacher": teacher, "labels": labels, "cotangent": cotangent}


SOFTEN_FACTOR = 2.0
BLEND_WEIGHT = 0.5
EPSILON = 1e-05

def token_block(hidden, norm_gain, head_weight, teacher, labels, cotangent):
    hidden_f = hidden.astype(jnp.float32)
    reciprocal = lax.rsqrt(lax.optimization_barrier(jnp.mean(hidden_f * hidden_f, axis=1)) + EPSILON)
    normed = hidden_f * reciprocal[:, None]
    features = (normed * norm_gain[None, :]).astype(jnp.bfloat16)
    student_logits = jnp.dot(features, head_weight, preferred_element_type=jnp.float32)
    target_label = teacher.astype(jnp.float32)
    student_maximum = lax.optimization_barrier(jnp.max(student_logits, axis=1))
    teacher_maximum = lax.optimization_barrier(jnp.max(target_label, axis=1))
    student_soft_probs = jnp.exp((student_logits - student_maximum[:, None]) / SOFTEN_FACTOR)
    hard_student = jnp.exp(student_logits - student_maximum[:, None])
    teacher_soft_probs = jnp.exp((target_label - teacher_maximum[:, None]) / SOFTEN_FACTOR)
    soft_partition_sum = lax.optimization_barrier(jnp.sum(student_soft_probs, axis=1))
    total_hard = lax.optimization_barrier(jnp.sum(hard_student, axis=1))
    teacher_partition_sum = lax.optimization_barrier(jnp.sum(teacher_soft_probs, axis=1))
    cross_entropy_sum = lax.optimization_barrier(jnp.sum(teacher_soft_probs * (target_label - student_logits), axis=1))
    column_ids = lax.broadcasted_iota(jnp.int32, student_logits.shape, 1)
    is_label = column_ids == labels[:, None]
    selected_logit = lax.optimization_barrier(jnp.sum(jnp.where(is_label, student_logits, 0.0), axis=1))
    soft_log_probs = student_maximum / SOFTEN_FACTOR + jnp.log(soft_partition_sum)
    teacher_log_probs = teacher_maximum / SOFTEN_FACTOR + jnp.log(teacher_partition_sum)
    hard_log_probs = student_maximum + jnp.log(total_hard)
    kullback_divergence = cross_entropy_sum / (SOFTEN_FACTOR * teacher_partition_sum) - teacher_log_probs + soft_log_probs
    per_token_loss = BLEND_WEIGHT * SOFTEN_FACTOR * SOFTEN_FACTOR * kullback_divergence + (1.0 - BLEND_WEIGHT) * (hard_log_probs - selected_logit)
    soft_residual = student_soft_probs / soft_partition_sum[:, None] - teacher_soft_probs / teacher_partition_sum[:, None]
    hard_residual = hard_student / total_hard[:, None] - is_label.astype(jnp.float32)
    logit_gradient = cotangent[:, None] * (BLEND_WEIGHT * SOFTEN_FACTOR * soft_residual + (1.0 - BLEND_WEIGHT) * hard_residual)
    logit_gradient = logit_gradient.astype(jnp.bfloat16)
    feature_grad = jnp.dot(logit_gradient, head_weight.T, preferred_element_type=jnp.float32)
    upstream = norm_gain[None, :] * feature_grad
    inner_mean = lax.optimization_barrier(jnp.sum(upstream * normed, axis=1)) / hidden.shape[1]
    hidden_grad = (reciprocal[:, None] * (upstream - normed * inner_mean[:, None])).astype(jnp.bfloat16)
    return (hidden_grad, per_token_loss)

def reference(hidden, norm_gain, head_weight, teacher, labels, cotangent):
    block_count = hidden.shape[0] // TOK_DEV

    def one_block(block_index):
        row_start = (block_index * TOK_DEV).astype(jnp.int32)
        return token_block(lax.dynamic_slice_in_dim(hidden, row_start, TOK_DEV, 0), norm_gain, head_weight, lax.dynamic_slice_in_dim(teacher, row_start, TOK_DEV, 0), lax.dynamic_slice_in_dim(labels, row_start, TOK_DEV, 0), lax.dynamic_slice_in_dim(cotangent, row_start, TOK_DEV, 0))
    grads, losses = lax.map(one_block, jnp.arange(block_count, dtype=jnp.int32))
    return (grads.reshape(hidden.shape), losses.reshape(-1))
```

```python
import jax
import jax.numpy as jnp
from jax import lax
from jax.experimental import pallas as pl
from jax.experimental.pallas import tpu as pltpu
from jax.sharding import PartitionSpec as P

EPSILON = 1e-05
MESH = pl.DeviceIdType.MESH
F32 = jnp.float32
BF16 = jnp.bfloat16

N = 16
TOK = 256
ROWS = TOK // N
D = 2048
VOCAB = 64128
SHARD = VOCAB // N
LANES = 128
TILES = 32
PAD = TILES * LANES
VTILES = VOCAB // LANES
VALID = SHARD - (TILES - 1) * LANES
PIECES = ((0, 9), (9, 8), (17, 8), (25, 8))
BLOCK = 512
BLOCKS = PAD // BLOCK
BLOCK_TILES = BLOCK // LANES
LOG2E = 1.4426950408889634
LN2 = 0.6931471805599453
RELAYED = (
    (2, 2, 0, 1, 1), (2, 2, 1, 3, 3),
    (0, 2, 0, 0, 1), (0, 2, 1, 0, 3),
    (1, 2, 0, 0, 1), (1, 2, 1, 0, 3),
    (3, 2, 0, 0, 1), (3, 2, 1, 0, 3),
    (2, 0, 0, 1, 0), (2, 0, 1, 3, 0),
)
OWN = D // N
CHIPS = N // 2
FULL_W = (SHARD // 16) * 16


def kernel(
    hidden, gain, wt, teacher, labels, cot,
    out, loss,
    hid, w, t_v, land, relay, feats, logits, fg, g_v,
    lse_src, lse_land, st_src, st_land, fin_src, fin_land,
    cx_src, cx_land, rs_src, rs_land,
    a_b, b_b, c_b, l_b, r_b, mx_b, soft_b, hard_b, pick_b, cross_b, inner_b, rows_v,
    loc_sem, w_sem, ts, tr, fs, ft, ms, mr, cs, cr, rs, rr,
):
    me = lax.axis_index("vocab")
    chip = lax.div(me, 2)
    core = lax.rem(me, 2)
    width = lax.axis_size("dp") // 2
    x = lax.rem(lax.axis_index("dp"), width)
    y = lax.rem(chip, 4)
    z = lax.div(me, 8) * 2 + lax.div(lax.axis_index("dp"), width)

    def group_index(dy, dz, c):
        return (lax.div(lax.rem(z + dz, 4), 2) * 4 + lax.rem(y + dy, 4)) * 2 + c

    def device(dy, dz, c):
        return {
            "dp": lax.rem(z + dz, 2) * width + x,
            "vocab": group_index(dy, dz, c),
        }

    lane = lax.broadcasted_iota(jnp.int32, (ROWS, LANES), 1)
    places = [(lane + i * LANES).astype(F32) for i in range(BLOCK_TILES)]
    my_rows = pl.ds(pl.multiple_of(me * ROWS, ROWS), ROWS)

    hid_copy = pltpu.make_async_copy(hidden, hid, loc_sem.at[0])
    hid_copy.start()
    t_copy = pltpu.make_async_copy(teacher, t_v, loc_sem.at[1])
    t_copy.start()
    w[FULL_W:PAD, :] = jnp.zeros((PAD - FULL_W, D), BF16)
    w_copies = []
    for c in range(BLOCKS):
        lo, hi = c * BLOCK, min((c + 1) * BLOCK, SHARD)
        copy = pltpu.make_async_copy(wt.at[lo:hi], w.at[lo:hi], w_sem.at[c])
        copy.start()
        w_copies.append(copy)

    barrier = pltpu.get_barrier_semaphore()

    def greet(k, _):
        pl.semaphore_signal(
            barrier, inc=1, device_id={"vocab": lax.rem(me + k, N)}, device_id_type=MESH
        )
        return 0

    lax.fori_loop(1, N, greet, 0)
    for dz in (1, 3):
        for dy in (0, 1, 3):
            for c in (0, 1):
                pl.semaphore_signal(
                    barrier, inc=1, device_id=device(dy, dz, c), device_id_type=MESH
                )
    pl.semaphore_wait(barrier, N - 1 + 12)

    def remote_to(src, dst, send_sem, recv_sem, target):
        return pltpu.make_async_remote_copy(
            src_ref=src, dst_ref=dst, send_sem=send_sem, recv_sem=recv_sem,
            device_id=target, device_id_type=MESH,
        )

    def remote(src, dst, send_sem, recv_sem, d):
        return remote_to(src, dst, send_sem, recv_sem, {"vocab": d})

    def columns_of(c):
        first, count = PIECES[c]
        return slice(first * LANES, (first + count) * LANES)

    def piece_copies(d, c, into):
        first, count = PIECES[c]
        base = lax.div(d * SHARD, LANES)
        spans = [(base + first, first, count)]
        if first + count > TILES:
            spans = [
                (base + first, first, count - 1),
                (jnp.minimum(base + TILES, VTILES - 1), TILES, 1),
            ]
        for start, at, tiles in spans:
            yield (
                teacher.at[:, pl.ds(pl.multiple_of(start * LANES, LANES), tiles * LANES)],
                into(slice(at * LANES, (at + tiles) * LANES)),
            )

    for c in range(len(PIECES)):
        for p, (dy, dz, dc, ry, rz) in enumerate(RELAYED):
            d = group_index(dy, dz, dc)
            for src, dst in piece_copies(d, c, lambda cols, p=p: relay.at[p, :, cols]):
                remote_to(src, dst, ts.at[c], ft.at[c], device(ry, rz, core)).start()
        for dy, dc in ((1, 0), (3, 0), (1, 1), (3, 1)):
            d = group_index(dy, 0, dc)
            for src, dst in piece_copies(d, c, lambda cols: land.at[my_rows, cols]):
                remote(src, dst, ts.at[c], tr.at[c], d).start()
        sibling = chip * 2 + (1 - core)
        for src, dst in piece_copies(sibling, c, lambda cols: land.at[my_rows, cols]):
            remote(src, dst, ts.at[c], tr.at[c], sibling).start()
        for src, dst in piece_copies(me, c, lambda cols: land.at[my_rows, cols]):
            pltpu.make_async_copy(src, dst, tr.at[c]).start()

    def forward_pieces(c):
        cols = columns_of(c)
        wait_for(relay.at[:, :, cols], ft.at[c])
        for p, (dy, dz, dc, ry, rz) in enumerate(RELAYED):
            origin = group_index(4 - ry, 4 - rz, core)
            rows = pl.ds(pl.multiple_of(origin * ROWS, ROWS), ROWS)
            remote_to(
                relay.at[p, :, cols], land.at[rows, cols], fs.at[c], tr.at[c],
                device(4 + dy - ry, 4 + dz - rz, dc),
            ).start()

    def wait_for(ref, sem):
        pltpu.make_async_copy(ref, ref, sem).wait()

    t_copy.wait()
    wide = 33
    steps = VTILES // wide
    rest = VTILES - steps * wide

    def t_tiles(i, count):
        start = i * (wide * LANES)
        return [
            t_v[:, pl.ds(pl.multiple_of(start + t * LANES, LANES), LANES)] for t in range(count)
        ]

    def tile_max(i, accs, count=wide):
        accs = list(accs)
        for t, x in enumerate(t_tiles(i, count)):
            accs[t % 4] = jnp.maximum(accs[t % 4], x)
        return tuple(accs)

    accs = tile_max(steps, (t_v[:, :LANES],) * 4, rest)
    accs = lax.fori_loop(0, steps, tile_max, accs)
    top = jnp.maximum(jnp.maximum(accs[0], accs[1]), jnp.maximum(accs[2], accs[3]))
    top = (0.5 * LOG2E) * jnp.max(top.astype(F32), axis=1, keepdims=True)

    def tile_sum(i, accs, count=wide):
        accs = list(accs)
        for t, x in enumerate(t_tiles(i, count)):
            accs[t % 4] = accs[t % 4] + jnp.exp2((0.5 * LOG2E) * x.astype(F32) - top)
        return tuple(accs)

    accs = tile_sum(steps, (jnp.zeros((ROWS, LANES), F32),) * 4, rest)
    accs = lax.fori_loop(0, steps, tile_sum, accs)
    total = jnp.sum((accs[0] + accs[1]) + (accs[2] + accs[3]), axis=1, keepdims=True)
    lse_src[...] = jnp.broadcast_to(top + LOG2E * jnp.log(total), (ROWS, LANES))

    def send_lse(k, _):
        remote(
            lse_src, lse_land.at[my_rows, :], ms.at[0], mr.at[0], lax.rem(me + k, N)
        ).start()
        return 0

    pltpu.make_async_copy(lse_src, lse_land.at[my_rows, :], mr.at[0]).start()
    lax.fori_loop(1, N, send_lse, 0)

    forward_pieces(0)

    local = labels[...] - me * SHARD
    inside = jnp.logical_and(local >= 0, local < SHARD)
    local = jnp.where(inside, local, -1).astype(F32)
    columns = jnp.concatenate(
        [local, cot[...], jnp.zeros((LANES - 2, TOK), F32)], axis=0
    ).T
    l_b[...] = jnp.broadcast_to(columns[:, 0:1], (TOK, LANES))
    c_b[...] = jnp.broadcast_to(columns[:, 1:2], (TOK, LANES))

    hid_copy.wait()

    tall = 64

    def make_features(s, _):
        at = pl.ds(pl.multiple_of(s * tall, tall), tall)
        acc = jnp.zeros((tall, LANES), F32)
        for t in range(D // LANES):
            h = hid[at, t * LANES : (t + 1) * LANES].astype(F32)
            acc = acc + h * h
        r = lax.rsqrt(jnp.sum(acc, axis=1, keepdims=True) * (1.0 / D) + EPSILON)
        r = jnp.broadcast_to(r, (tall, LANES))
        r_b[at, :] = r
        for t in range(D // LANES):
            cols = slice(t * LANES, (t + 1) * LANES)
            feats[at, cols] = ((hid[at, cols].astype(F32) * r) * gain[:, cols]).astype(BF16)
        return 0

    lax.fori_loop(0, TOK // tall, make_features, 0)

    zeros = jnp.zeros((TOK, LANES), F32)
    mx_b[...] = jnp.full((TOK, LANES), -1e30, F32)
    soft_b[...] = zeros
    hard_b[...] = zeros
    pick_b[...] = zeros
    for c in range(BLOCKS):
        w_copies[c].wait()

    forward_pieces(1)

    def forward(c):
        at = pl.ds(pl.multiple_of(c * BLOCK, BLOCK), BLOCK)
        logits[c] = lax.dot_general(
            feats[...], w[at, :], (((1,), (1,)), ((), ())), preferred_element_type=F32
        )

    def student_sums(c, s):
        at = pl.ds(s * ROWS, ROWS)
        tiles = [logits[c, at, i * LANES : (i + 1) * LANES] for i in range(BLOCK_TILES)]
        top = mx_b[at, :]
        label = l_b[at, :] - jnp.float32(c * BLOCK)
        new = jnp.maximum(
            jnp.maximum(top, tiles[0]), jnp.maximum(jnp.maximum(tiles[1], tiles[2]), tiles[3])
        )
        mx_b[at, :] = new
        scale = jnp.exp2((0.5 * LOG2E) * (top - new))
        soft = soft_b[at, :] * scale
        hard = hard_b[at, :] * (scale * scale)
        picked = pick_b[at, :]
        for i, v in enumerate(tiles):
            e = jnp.exp2((0.5 * LOG2E) * (v - new))
            soft = soft + e
            hard = hard + e * e
            picked = picked + jnp.where(places[i] == label, v, 0.0)
        soft_b[at, :] = soft
        hard_b[at, :] = hard
        pick_b[at, :] = picked

    forward(0)

    def forward_step(c, _):
        @pl.when(c == 4)
        def _():
            forward_pieces(2)

        for s in range(TOK // ROWS):
            student_sums(c - 1, s)
        forward(c)
        return 0

    lax.fori_loop(1, BLOCKS, forward_step, 0)
    last = slice((BLOCK_TILES - 1) * LANES, BLOCK)
    wide_lane = lax.broadcasted_iota(jnp.int32, (TOK, LANES), 1)
    logits[BLOCKS - 1, :, last] = jnp.where(
        wide_lane < VALID, logits[BLOCKS - 1, :, last], -1e30
    )
    for s in range(TOK // ROWS):
        student_sums(BLOCKS - 1, s)
    forward_pieces(3)

    top = mx_b[...]
    m = jnp.max(top, axis=1, keepdims=True)
    scale = jnp.exp2((0.5 * LOG2E) * (top - m))
    soft = jnp.sum(soft_b[...] * scale, axis=1, keepdims=True)
    hard = jnp.sum(hard_b[...] * (scale * scale), axis=1, keepdims=True)
    picked = jnp.sum(pick_b[...], axis=1, keepdims=True)
    stat = jnp.where(wide_lane == 0, m, jnp.where(wide_lane == 1, soft, hard))
    st_src[...] = jnp.where(wide_lane == 3, picked, stat).T[0:8, :]

    def send_stats(k, _):
        remote(
            st_src, st_land.at[me], ms.at[1], mr.at[1], lax.rem(me + k, N)
        ).start()
        return 0

    pltpu.make_async_copy(st_src, st_land.at[me], mr.at[1]).start()
    lax.fori_loop(1, N, send_stats, 0)
    wait_for(st_land, mr.at[1])

    top = st_land[0, 0:1, :]
    for s in range(1, N):
        top = jnp.maximum(top, st_land[s, 0:1, :])
    soft = jnp.zeros((1, TOK), F32)
    hard = jnp.zeros((1, TOK), F32)
    picked = jnp.zeros((1, TOK), F32)
    for s in range(N):
        stat = st_land[s]
        scale = jnp.exp2((0.5 * LOG2E) * (stat[0:1] - top))
        soft = soft + stat[1:2] * scale
        hard = hard + stat[2:3] * (scale * scale)
        picked = picked + stat[3:4]
    lse_soft = 0.5 * top + jnp.log(soft)
    rows_v[0:1, :] = lse_soft
    rows_v[1:2, :] = top + jnp.log(hard)
    rows_v[2:3, :] = picked
    columns = jnp.concatenate(
        [
            LOG2E * lse_soft,
            0.5 * cot[...] * (soft * soft) / hard,
            jnp.zeros((LANES - 2, TOK), F32),
        ],
        axis=0,
    ).T
    a_b[...] = jnp.broadcast_to(columns[:, 0:1], (TOK, LANES))
    b_b[...] = jnp.broadcast_to(columns[:, 1:2], (TOK, LANES))
    cross_b[...] = zeros
    inner_b[...] = zeros
    for n in range(CHIPS):
        fg[n] = jnp.zeros((TOK, 2 * OWN), F32)
    wait_for(lse_land, mr.at[0])

    off = lax.rem(me * SHARD, LANES)
    shift = lax.rem(LANES - off, LANES)
    keep = lane < LANES - off
    partner = chip * 2 + (1 - core)

    def wait_piece(c):
        wait_for(land.at[:, columns_of(c)], tr.at[c])

    def gradient(c, s):
        at = pl.ds(s * ROWS, ROWS)
        slot = lax.rem(c, 2)
        lse_s, b, ct = a_b[at, :], b_b[at, :], c_b[at, :]
        label = l_b[at, :] - jnp.float32(c * BLOCK)
        lse_t = lse_land[at, :]
        half = 0.5 * ct
        cross, inner = cross_b[at, :], inner_b[at, :]

        def turned(i):
            start = pl.multiple_of(c * BLOCK + i * LANES, LANES)
            return pltpu.roll(land[at, pl.ds(start, LANES)].astype(F32), shift, 1)

        here = turned(0)
        for i in range(BLOCK_TILES):
            after = turned(i + 1)
            x = jnp.where(keep, here, after)
            here = after
            v = logits[c, at, i * LANES : (i + 1) * LANES]
            p = jnp.exp2((0.5 * LOG2E) * x - lse_t)
            e = jnp.exp2((0.5 * LOG2E) * v - lse_s)
            if i == BLOCK_TILES - 1:
                p = jnp.where(lane < SHARD - i * LANES - c * BLOCK, p, 0.0)
            cross = cross + p * (x - v)
            g = e * (ct + e * b) - ct * p
            g = g - jnp.where(places[i] == label, half, 0.0)
            g = g.astype(BF16)
            g_v[slot, at, i * LANES : (i + 1) * LANES] = g
            inner = inner + g.astype(F32) * v
        cross_b[at, :] = cross
        inner_b[at, :] = inner

    def backward(c, n):
        rows = pl.ds(pl.multiple_of(c * BLOCK, BLOCK), BLOCK)
        at = pl.ds(pl.multiple_of(n * (2 * OWN), 2 * OWN), 2 * OWN)
        part = jnp.dot(g_v[lax.rem(c, 2)], w[rows, at], preferred_element_type=F32)
        return fg[n] + part

    wait_piece(0)
    for s in range(TOK // ROWS):
        gradient(0, s)

    def step(c, _):
        for p in range(1, len(PIECES)):

            @pl.when(c + 1 == 2 * p)
            def _():
                wait_piece(p)

        for s in range(TOK // ROWS):
            gradient(c + 1, s)
        for n in range(CHIPS):
            fg[n] = backward(c, n)
        return 0

    lax.fori_loop(0, BLOCKS - 1, step, 0)

    cross = jnp.sum(cross_b[...], axis=1, keepdims=True)
    inner = jnp.sum(inner_b[...], axis=1, keepdims=True)
    stat = jnp.where(wide_lane == 0, cross, inner)
    fin_src[...] = jnp.where(wide_lane == 2, LN2 * lse_land[...], stat).T[0:8, :]

    def send_final(k, _):
        remote(
            fin_src, fin_land.at[me], ms.at[2], mr.at[2], lax.rem(me + k, N)
        ).start()
        return 0

    pltpu.make_async_copy(fin_src, fin_land.at[me], mr.at[2]).start()
    lax.fori_loop(1, N, send_final, 0)

    for k in range(CHIPS):
        n = lax.rem(chip + 1 + k, CHIPS)
        part = backward(BLOCKS - 1, n)
        fg[n] = part
        theirs = jnp.where(core == 0, part[:, OWN:], part[:, :OWN])
        cx_src[n] = theirs.astype(BF16)
        remote(cx_src.at[n], cx_land.at[n], cs.at[0], cr.at[n], partner).start()

    def own_half(n):
        part = fg[n]
        half = jnp.where(core == 0, part[:, :OWN], part[:, OWN:])
        return half + cx_land[n].astype(F32)

    def share(k, _):
        n = lax.rem(chip + 1 + k, CHIPS)
        wait_for(cx_land.at[n], cr.at[n])
        rs_src[n] = own_half(n).astype(BF16)
        remote(rs_src.at[n], rs_land.at[chip], rs, rr, n * 2 + core).start()
        return 0

    lax.fori_loop(0, CHIPS - 1, share, 0)
    wait_for(cx_land.at[chip], cr.at[chip])
    fg[chip, :, :OWN] = own_half(chip)

    wait_for(fin_land, mr.at[2])
    cross = jnp.zeros((1, TOK), F32)
    inner = jnp.zeros((1, TOK), F32)
    for s in range(N):
        stat = fin_land[s]
        cross = cross + stat[0:1]
        inner = inner + stat[1:2]
    kl = 0.5 * cross - fin_src[2:3, :] + rows_v[0:1, :]
    loss[...] = 2.0 * kl + 0.5 * (rows_v[1:2, :] - rows_v[2:3, :])
    columns = jnp.concatenate(
        [inner * (1.0 / D), jnp.zeros((LANES - 1, TOK), F32)], axis=0
    ).T
    a_b[...] = jnp.broadcast_to(columns[:, 0:1], (TOK, LANES))

    wait_for(rs_land.at[0 : CHIPS - 1], rr)
    mine = pl.ds(pl.multiple_of(me * OWN, OWN), OWN)
    total = fg[chip, :, :OWN]
    for k in range(1, CHIPS):
        total = total + rs_land[lax.rem(chip + k, CHIPS)].astype(F32)
    r = r_b[...]
    normed = hid[:, mine].astype(F32) * r
    out[...] = (r * (gain[:, mine] * total - normed * a_b[...])).astype(BF16)

    for c in range(len(PIECES)):
        wait_for(land.at[0 : TOK - ROWS, columns_of(c)], ts.at[c])
        wait_for(relay.at[:, :, columns_of(c)], fs.at[c])
    wait_for(lse_land.at[0 : TOK - ROWS], ms.at[0])
    wait_for(st_land.at[0 : N - 1], ms.at[1])
    wait_for(fin_land.at[0 : N - 1], ms.at[2])
    wait_for(cx_src, cs.at[0])
    wait_for(rs_src.at[0 : CHIPS - 1], rs)


def on_device(hidden, norm_gain, head_weight, teacher, labels, cotangent):
    vmem = pl.BlockSpec(memory_space=pltpu.VMEM)
    hbm = pl.BlockSpec(memory_space=pl.ANY)
    dma = pltpu.SemaphoreType.DMA
    column = pltpu.VMEM((TOK, LANES), F32)
    grad, loss = pl.pallas_call(
        kernel,
        out_shape=(
            jax.ShapeDtypeStruct((TOK, OWN), BF16),
            jax.ShapeDtypeStruct((1, TOK), F32),
        ),
        in_specs=[hbm, vmem, hbm, hbm, vmem, vmem],
        out_specs=(vmem, vmem),
        scratch_shapes=[
            pltpu.VMEM((TOK, D), BF16),
            pltpu.VMEM((PAD, D), BF16),
            pltpu.VMEM((ROWS, VOCAB), BF16),
            pltpu.VMEM((TOK, PAD + LANES), BF16),
            pltpu.VMEM((len(RELAYED), ROWS, PAD + LANES), BF16),
            pltpu.VMEM((TOK, D), BF16),
            pltpu.VMEM((BLOCKS, TOK, BLOCK), F32),
            pltpu.VMEM((CHIPS, TOK, 2 * OWN), F32),
            pltpu.VMEM((2, TOK, BLOCK), BF16),
            pltpu.VMEM((ROWS, LANES), F32),
            column,
            pltpu.VMEM((8, TOK), F32),
            pltpu.VMEM((N, 8, TOK), F32),
            pltpu.VMEM((8, TOK), F32),
            pltpu.VMEM((N, 8, TOK), F32),
            pltpu.VMEM((CHIPS, TOK, OWN), BF16),
            pltpu.VMEM((CHIPS, TOK, OWN), BF16),
            pltpu.VMEM((CHIPS, TOK, OWN), BF16),
            pltpu.VMEM((CHIPS, TOK, OWN), BF16),
            column, column, column, column, column, column,
            column, column, column, column, column,
            pltpu.VMEM((8, TOK), F32),
            dma((2,)), dma((BLOCKS,)), dma((len(PIECES),)), dma((len(PIECES),)), dma((len(PIECES),)), dma((len(PIECES),)),
            dma((3,)), dma((3,)), dma((1,)), dma((CHIPS,)), dma, dma,
        ],
        compiler_params=pltpu.CompilerParams(
            collective_id=0, has_side_effects=True, vmem_limit_bytes=56 * 1024 * 1024
        ),
        cost_estimate=pl.CostEstimate(
            flops=4 * TOK * D * SHARD, bytes_accessed=20_000_000, transcendentals=3_000_000
        ),
    )(
        hidden,
        norm_gain.reshape(1, D),
        head_weight.T,
        teacher,
        labels.reshape(1, TOK),
        cotangent.reshape(1, TOK),
    )
    return grad, loss.reshape(TOK)


def solution(mesh):
    return jax.shard_map(
        on_device,
        mesh=mesh,
        in_specs=(P("dp", None), P(), P(None, "vocab"), P(("dp", "vocab"), None), P("dp"), P("dp")),
        out_specs=(P("dp", "vocab"), P("dp")),
        check_vma=False,
    )
```

```python
import jax
import jax.numpy as jnp
from jax import lax
from jax.experimental import pallas as pl
from jax.experimental.pallas import tpu as pltpu
from jax.sharding import PartitionSpec as P

EPSILON = 1e-05
MESH = pl.DeviceIdType.MESH
F32 = jnp.float32
BF16 = jnp.bfloat16

N = 16
TOK = 256
ROWS = TOK // N
D = 2048
VOCAB = 64128
SHARD = VOCAB // N
LANES = 128
TILES = 32
PAD = TILES * LANES
VTILES = VOCAB // LANES
VALID = SHARD - (TILES - 1) * LANES
PIECES = ((0, 9), (9, 8), (17, 8), (25, 8))
BLOCK = 512
BLOCKS = PAD // BLOCK
BLOCK_TILES = BLOCK // LANES
FWD = 1024
FWDS = PAD // FWD
LOG2E = 1.4426950408889634
LN2 = 0.6931471805599453
OWN = D // N
CHIPS = N // 2
FULL_W = (SHARD // 16) * 16


def kernel(
    hidden, gain, wt, teacher, labels, cot,
    out, loss,
    hid, w, t_v, land, feats, logits, fg, g_now, g_next,
    lse_src, lse_land, st_src, st_land, fin_src, fin_land,
    cx_src, cx_land, rs_src, rs_land,
    a_b, b_b, c_b, l_b, r_b, mx_b, soft_b, hard_b, pick_b, cross_b, inner_b, rows_v,
    loc_sem, w_sem, ts, tr, ms, mr, cs, cr, rs, rr,
):
    me = lax.axis_index("vocab")
    chip = lax.div(me, 2)
    core = lax.rem(me, 2)
    lane = lax.broadcasted_iota(jnp.int32, (ROWS, LANES), 1)
    places = [(lane + i * LANES).astype(F32) for i in range(BLOCK_TILES)]
    my_rows = pl.ds(pl.multiple_of(me * ROWS, ROWS), ROWS)

    hid_copy = pltpu.make_async_copy(hidden, hid, loc_sem.at[0])
    hid_copy.start()
    t_copy = pltpu.make_async_copy(teacher, t_v, loc_sem.at[1])
    t_copy.start()
    w[FULL_W:PAD, :] = jnp.zeros((PAD - FULL_W, D), BF16)
    w_copies = []
    for c in range(BLOCKS):
        lo, hi = c * BLOCK, min((c + 1) * BLOCK, SHARD)
        copy = pltpu.make_async_copy(wt.at[lo:hi], w.at[lo:hi], w_sem.at[c])
        copy.start()
        w_copies.append(copy)

    barrier = pltpu.get_barrier_semaphore()

    def greet(k, _):
        pl.semaphore_signal(
            barrier, inc=1, device_id={"vocab": lax.rem(me + k, N)}, device_id_type=MESH
        )
        return 0

    lax.fori_loop(1, N, greet, 0)
    pl.semaphore_wait(barrier, N - 1)

    def piece_refs(d, first, count):
        base = lax.div(d * SHARD, LANES) + first
        if first + count > TILES:
            count = count - 1
        src = teacher.at[:, pl.ds(pl.multiple_of(base * LANES, LANES), count * LANES)]
        dst = land.at[my_rows, first * LANES : (first + count) * LANES]
        return src, dst

    def last_refs(d):
        base = jnp.minimum(lax.div(d * SHARD, LANES) + TILES, VTILES - 1)
        src = teacher.at[:, pl.ds(pl.multiple_of(base * LANES, LANES), LANES)]
        dst = land.at[my_rows, TILES * LANES : (TILES + 1) * LANES]
        return src, dst

    def remote(src, dst, send_sem, recv_sem, d):
        return pltpu.make_async_remote_copy(
            src_ref=src, dst_ref=dst, send_sem=send_sem, recv_sem=recv_sem,
            device_id={"vocab": d}, device_id_type=MESH,
        )

    for c, (first, count) in enumerate(PIECES):

        def send(k, _, c=c, first=first, count=count):
            d = lax.rem(me + k, N)
            src, dst = piece_refs(d, first, count)
            remote(src, dst, ts.at[c], tr.at[c], d).start()
            if first + count > TILES:
                src, dst = last_refs(d)
                remote(src, dst, ts.at[c], tr.at[c], d).start()
            return 0

        src, dst = piece_refs(me, first, count)
        pltpu.make_async_copy(src, dst, tr.at[c]).start()
        if first + count > TILES:
            src, dst = last_refs(me)
            pltpu.make_async_copy(src, dst, tr.at[c]).start()
        lax.fori_loop(1, N, send, 0)

    def wait_for(ref, sem):
        pltpu.make_async_copy(ref, ref, sem).wait()

    t_copy.wait()
    wide = 33
    steps = VTILES // wide
    rest = VTILES - steps * wide

    def t_tiles(i, count):
        start = i * (wide * LANES)
        return [
            t_v[:, pl.ds(pl.multiple_of(start + t * LANES, LANES), LANES)] for t in range(count)
        ]

    def tile_max(i, accs, count=wide):
        accs = list(accs)
        for t, x in enumerate(t_tiles(i, count)):
            accs[t % 4] = jnp.maximum(accs[t % 4], x)
        return tuple(accs)

    accs = tile_max(steps, (t_v[:, :LANES],) * 4, rest)
    accs = lax.fori_loop(0, steps, tile_max, accs)
    top = jnp.maximum(jnp.maximum(accs[0], accs[1]), jnp.maximum(accs[2], accs[3]))
    top = (0.5 * LOG2E) * jnp.max(top.astype(F32), axis=1, keepdims=True)

    def tile_sum(i, accs, count=wide):
        accs = list(accs)
        for t, x in enumerate(t_tiles(i, count)):
            accs[t % 4] = accs[t % 4] + jnp.exp2((0.5 * LOG2E) * x.astype(F32) - top)
        return tuple(accs)

    accs = tile_sum(steps, (jnp.zeros((ROWS, LANES), F32),) * 4, rest)
    accs = lax.fori_loop(0, steps, tile_sum, accs)
    total = jnp.sum((accs[0] + accs[1]) + (accs[2] + accs[3]), axis=1, keepdims=True)
    lse_src[...] = jnp.broadcast_to(top + LOG2E * jnp.log(total), (ROWS, LANES))

    def send_lse(k, _):
        remote(
            lse_src, lse_land.at[my_rows, :], ms.at[0], mr.at[0], lax.rem(me + k, N)
        ).start()
        return 0

    pltpu.make_async_copy(lse_src, lse_land.at[my_rows, :], mr.at[0]).start()
    lax.fori_loop(1, N, send_lse, 0)

    local = labels[...] - me * SHARD
    inside = jnp.logical_and(local >= 0, local < SHARD)
    local = jnp.where(inside, local, -1).astype(F32)
    columns = jnp.concatenate(
        [local, cot[...], jnp.zeros((LANES - 2, TOK), F32)], axis=0
    ).T
    l_b[...] = jnp.broadcast_to(columns[:, 0:1], (TOK, LANES))
    c_b[...] = jnp.broadcast_to(columns[:, 1:2], (TOK, LANES))

    hid_copy.wait()

    tall = 64

    def make_features(s, _):
        at = pl.ds(pl.multiple_of(s * tall, tall), tall)
        acc = jnp.zeros((tall, LANES), F32)
        for t in range(D // LANES):
            h = hid[at, t * LANES : (t + 1) * LANES].astype(F32)
            acc = acc + h * h
        r = lax.rsqrt(jnp.sum(acc, axis=1, keepdims=True) * (1.0 / D) + EPSILON)
        r = jnp.broadcast_to(r, (tall, LANES))
        r_b[at, :] = r
        for t in range(D // LANES):
            cols = slice(t * LANES, (t + 1) * LANES)
            feats[at, cols] = ((hid[at, cols].astype(F32) * r) * gain[:, cols]).astype(BF16)
        return 0

    lax.fori_loop(0, TOK // tall, make_features, 0)

    zeros = jnp.zeros((TOK, LANES), F32)
    mx_b[...] = jnp.full((TOK, LANES), -1e30, F32)
    soft_b[...] = zeros
    hard_b[...] = zeros
    pick_b[...] = zeros
    for copy in w_copies:
        copy.wait()

    def forward(c):
        logits[:, c * FWD : (c + 1) * FWD] = lax.dot_general(
            feats[...], w[c * FWD : (c + 1) * FWD, :], (((1,), (1,)), ((), ())),
            preferred_element_type=F32,
        )

    def student_sums(c, s):
        at = slice(s * ROWS, (s + 1) * ROWS)
        tiles = []
        for i in range(FWD // LANES):
            start = c * FWD + i * LANES
            v = logits[at, start : start + LANES]
            if start + LANES > SHARD:
                v = jnp.where(lane < SHARD - start, v, -1e30)
                logits[at, start : start + LANES] = v
            tiles.append(v)
        top = mx_b[at, :]
        label = l_b[at, :]
        new = top
        for v in tiles:
            new = jnp.maximum(new, v)
        mx_b[at, :] = new
        scale = jnp.exp2((0.5 * LOG2E) * (top - new))
        soft = soft_b[at, :] * scale
        hard = hard_b[at, :] * (scale * scale)
        picked = pick_b[at, :]
        for i, v in enumerate(tiles):
            if i % BLOCK_TILES == 0:
                here = label - float(c * FWD + i * LANES)
            e = jnp.exp2((0.5 * LOG2E) * (v - new))
            soft = soft + e
            hard = hard + e * e
            picked = picked + jnp.where(places[i % BLOCK_TILES] == here, v, 0.0)
        soft_b[at, :] = soft
        hard_b[at, :] = hard
        pick_b[at, :] = picked

    for c in range(FWDS + 1):
        if c > 0:
            for s in range(TOK // ROWS):
                student_sums(c - 1, s)
        if c < FWDS:
            forward(c)

    wide_lane = lax.broadcasted_iota(jnp.int32, (TOK, LANES), 1)
    top = mx_b[...]
    m = jnp.max(top, axis=1, keepdims=True)
    scale = jnp.exp2((0.5 * LOG2E) * (top - m))
    soft = jnp.sum(soft_b[...] * scale, axis=1, keepdims=True)
    hard = jnp.sum(hard_b[...] * (scale * scale), axis=1, keepdims=True)
    picked = jnp.sum(pick_b[...], axis=1, keepdims=True)
    stat = jnp.where(wide_lane == 0, m, jnp.where(wide_lane == 1, soft, hard))
    st_src[...] = jnp.where(wide_lane == 3, picked, stat).T[0:8, :]

    def send_stats(k, _):
        remote(
            st_src, st_land.at[me], ms.at[1], mr.at[1], lax.rem(me + k, N)
        ).start()
        return 0

    pltpu.make_async_copy(st_src, st_land.at[me], mr.at[1]).start()
    lax.fori_loop(1, N, send_stats, 0)
    wait_for(st_land, mr.at[1])

    top = st_land[0, 0:1, :]
    for s in range(1, N):
        top = jnp.maximum(top, st_land[s, 0:1, :])
    soft = jnp.zeros((1, TOK), F32)
    hard = jnp.zeros((1, TOK), F32)
    picked = jnp.zeros((1, TOK), F32)
    for s in range(N):
        stat = st_land[s]
        scale = jnp.exp2((0.5 * LOG2E) * (stat[0:1] - top))
        soft = soft + stat[1:2] * scale
        hard = hard + stat[2:3] * (scale * scale)
        picked = picked + stat[3:4]
    lse_soft = 0.5 * top + jnp.log(soft)
    rows_v[0:1, :] = lse_soft
    rows_v[1:2, :] = top + jnp.log(hard)
    rows_v[2:3, :] = picked
    columns = jnp.concatenate(
        [
            LOG2E * lse_soft,
            0.5 * cot[...] * (soft * soft) / hard,
            jnp.zeros((LANES - 2, TOK), F32),
        ],
        axis=0,
    ).T
    a_b[...] = jnp.broadcast_to(columns[:, 0:1], (TOK, LANES))
    b_b[...] = jnp.broadcast_to(columns[:, 1:2], (TOK, LANES))
    cross_b[...] = zeros
    inner_b[...] = zeros
    fg[...] = jnp.zeros((TOK, D), F32)
    wait_for(lse_land, mr.at[0])

    off = lax.rem(me * SHARD, LANES)
    shift = lax.rem(LANES - off, LANES)
    keep = lane < LANES - off
    partner = chip * 2 + (1 - core)

    def wait_piece(c):
        first, count = PIECES[c]
        wait_for(land.at[:, first * LANES : (first + count) * LANES], tr.at[c])

    def gradient(c, s, g_v):
        at = pl.ds(s * ROWS, ROWS)
        lse_s, b, ct = a_b[at, :], b_b[at, :], c_b[at, :]
        label = l_b[at, :] - jnp.float32(c * BLOCK)
        lse_t = lse_land[at, :]
        half = 0.5 * ct
        cross, inner = cross_b[at, :], inner_b[at, :]

        def turned(i):
            start = pl.multiple_of(c * BLOCK + i * LANES, LANES)
            return pltpu.roll(land[at, pl.ds(start, LANES)].astype(F32), shift, 1)

        here = turned(0)
        for i in range(BLOCK_TILES):
            after = turned(i + 1)
            x = jnp.where(keep, here, after)
            here = after
            v = logits[at, pl.ds(pl.multiple_of(c * BLOCK + i * LANES, LANES), LANES)]
            p = jnp.exp2((0.5 * LOG2E) * x - lse_t)
            e = jnp.exp2((0.5 * LOG2E) * v - lse_s)
            if i == BLOCK_TILES - 1:
                p = jnp.where(lane < SHARD - i * LANES - c * BLOCK, p, 0.0)
            cross = cross + p * (x - v)
            g = e * (ct + e * b) - ct * p
            g = g - jnp.where(places[i] == label, half, 0.0)
            g = g.astype(BF16)
            g_v[at, i * LANES : (i + 1) * LANES] = g
            inner = inner + g.astype(F32) * v
        cross_b[at, :] = cross
        inner_b[at, :] = inner

    wait_piece(0)
    for s in range(TOK // ROWS):
        gradient(0, s, g_now)

    def step(c, _):
        for p in range(1, len(PIECES)):

            @pl.when(c + 1 == 2 * p)
            def _():
                wait_piece(p)

        for s in range(TOK // ROWS):
            gradient(c + 1, s, g_next)
        rows = pl.ds(pl.multiple_of(c * BLOCK, BLOCK), BLOCK)
        fg[...] += jnp.dot(g_now[...], w[rows, :], preferred_element_type=F32)
        g_now[...] = g_next[...]
        return 0

    lax.fori_loop(0, BLOCKS - 1, step, 0)

    cross = jnp.sum(cross_b[...], axis=1, keepdims=True)
    inner = jnp.sum(inner_b[...], axis=1, keepdims=True)
    stat = jnp.where(wide_lane == 0, cross, inner)
    fin_src[...] = jnp.where(wide_lane == 2, LN2 * lse_land[...], stat).T[0:8, :]

    def send_final(k, _):
        remote(
            fin_src, fin_land.at[me], ms.at[2], mr.at[2], lax.rem(me + k, N)
        ).start()
        return 0

    pltpu.make_async_copy(fin_src, fin_land.at[me], mr.at[2]).start()
    lax.fori_loop(1, N, send_final, 0)

    fg[...] += jnp.dot(g_now[...], w[PAD - BLOCK :, :], preferred_element_type=F32)

    def half_of(n, c):
        return fg[:, pl.ds(pl.multiple_of((2 * n + c) * OWN, OWN), OWN)]

    def give(k, _):
        n = lax.rem(chip + 1 + k, CHIPS)
        cx_src[n] = half_of(n, 1 - core).astype(BF16)
        remote(cx_src.at[n], cx_land.at[n], cs.at[0], cr.at[n], partner).start()
        return 0

    lax.fori_loop(0, CHIPS, give, 0)

    def own_half(n):
        return half_of(n, core) + cx_land[n].astype(F32)

    def share(k, _):
        n = lax.rem(chip + 1 + k, CHIPS)
        wait_for(cx_land.at[n], cr.at[n])
        rs_src[n] = own_half(n).astype(BF16)
        remote(rs_src.at[n], rs_land.at[chip], rs, rr, n * 2 + core).start()
        return 0

    lax.fori_loop(0, CHIPS - 1, share, 0)
    wait_for(cx_land.at[chip], cr.at[chip])

    wait_for(fin_land, mr.at[2])
    cross = jnp.zeros((1, TOK), F32)
    inner = jnp.zeros((1, TOK), F32)
    for s in range(N):
        stat = fin_land[s]
        cross = cross + stat[0:1]
        inner = inner + stat[1:2]
    kl = 0.5 * cross - fin_src[2:3, :] + rows_v[0:1, :]
    loss[...] = 2.0 * kl + 0.5 * (rows_v[1:2, :] - rows_v[2:3, :])
    columns = jnp.concatenate(
        [inner * (1.0 / D), jnp.zeros((LANES - 1, TOK), F32)], axis=0
    ).T
    a_b[...] = jnp.broadcast_to(columns[:, 0:1], (TOK, LANES))

    wait_for(rs_land.at[0 : CHIPS - 1], rr)
    mine = pl.ds(pl.multiple_of(me * OWN, OWN), OWN)
    total = own_half(chip)
    for k in range(1, CHIPS):
        total = total + rs_land[lax.rem(chip + k, CHIPS)].astype(F32)
    r = r_b[...]
    normed = hid[:, mine].astype(F32) * r
    out[...] = (r * (gain[:, mine] * total - normed * a_b[...])).astype(BF16)

    for c, (first, count) in enumerate(PIECES):
        wait_for(land.at[0 : TOK - ROWS, first * LANES : (first + count) * LANES], ts.at[c])
    wait_for(lse_land.at[0 : TOK - ROWS], ms.at[0])
    wait_for(st_land.at[0 : N - 1], ms.at[1])
    wait_for(fin_land.at[0 : N - 1], ms.at[2])
    wait_for(cx_src, cs.at[0])
    wait_for(rs_src.at[0 : CHIPS - 1], rs)


def on_device(hidden, norm_gain, head_weight, teacher, labels, cotangent):
    vmem = pl.BlockSpec(memory_space=pltpu.VMEM)
    hbm = pl.BlockSpec(memory_space=pl.ANY)
    dma = pltpu.SemaphoreType.DMA
    column = pltpu.VMEM((TOK, LANES), F32)
    grad, loss = pl.pallas_call(
        kernel,
        out_shape=(
            jax.ShapeDtypeStruct((TOK, OWN), BF16),
            jax.ShapeDtypeStruct((1, TOK), F32),
        ),
        in_specs=[hbm, vmem, hbm, hbm, vmem, vmem],
        out_specs=(vmem, vmem),
        scratch_shapes=[
            pltpu.VMEM((TOK, D), BF16),
            pltpu.VMEM((PAD, D), BF16),
            pltpu.VMEM((ROWS, VOCAB), BF16),
            pltpu.VMEM((TOK, PAD + LANES), BF16),
            pltpu.VMEM((TOK, D), BF16),
            pltpu.VMEM((TOK, PAD), F32),
            pltpu.VMEM((TOK, D), F32),
            pltpu.VMEM((TOK, BLOCK), BF16),
            pltpu.VMEM((TOK, BLOCK), BF16),
            pltpu.VMEM((ROWS, LANES), F32),
            column,
            pltpu.VMEM((8, TOK), F32),
            pltpu.VMEM((N, 8, TOK), F32),
            pltpu.VMEM((8, TOK), F32),
            pltpu.VMEM((N, 8, TOK), F32),
            pltpu.VMEM((CHIPS, TOK, OWN), BF16),
            pltpu.VMEM((CHIPS, TOK, OWN), BF16),
            pltpu.VMEM((CHIPS, TOK, OWN), BF16),
            pltpu.VMEM((CHIPS, TOK, OWN), BF16),
            column, column, column, column, column, column,
            column, column, column, column, column,
            pltpu.VMEM((8, TOK), F32),
            dma((2,)), dma((BLOCKS,)), dma((len(PIECES),)), dma((len(PIECES),)),
            dma((3,)), dma((3,)), dma((1,)), dma((CHIPS,)), dma, dma,
        ],
        compiler_params=pltpu.CompilerParams(
            collective_id=0, has_side_effects=True, vmem_limit_bytes=56 * 1024 * 1024
        ),
        cost_estimate=pl.CostEstimate(
            flops=4 * TOK * D * SHARD, bytes_accessed=20_000_000, transcendentals=3_000_000
        ),
    )(
        hidden,
        norm_gain.reshape(1, D),
        head_weight.T,
        teacher,
        labels.reshape(1, TOK),
        cotangent.reshape(1, TOK),
    )
    return grad, loss.reshape(TOK)


def solution(mesh):
    return jax.shard_map(
        on_device,
        mesh=mesh,
        in_specs=(P("dp", None), P(), P(None, "vocab"), P(("dp", "vocab"), None), P("dp"), P("dp")),
        out_specs=(P("dp", "vocab"), P("dp")),
        check_vma=False,
    )
```

```python
import jax
import jax.numpy as jnp
from jax import lax
from jax.experimental import pallas as pl
from jax.experimental.pallas import tpu as pltpu
from jax.sharding import PartitionSpec as P

EPSILON = 1e-05
MESH = pl.DeviceIdType.MESH
F32 = jnp.float32
BF16 = jnp.bfloat16

N = 16
TOK = 256
ROWS = TOK // N
D = 2048
VOCAB = 64128
SHARD = VOCAB // N
LANES = 128
TILES = 32
PAD = TILES * LANES
VTILES = VOCAB // LANES
VALID = SHARD - (TILES - 1) * LANES
PIECES = ((0, 9), (9, 8), (17, 8), (25, 8))
BLOCK = 512
BLOCKS = PAD // BLOCK
BLOCK_TILES = BLOCK // LANES
FWD = 1024
FWDS = PAD // FWD
LOG2E = 1.4426950408889634
LN2 = 0.6931471805599453
RELAYED = (
    (2, 2, 0, 1, 1), (2, 2, 1, 3, 3),
    (0, 2, 0, 0, 1), (0, 2, 1, 0, 3),
    (1, 2, 0, 0, 1), (1, 2, 1, 0, 3),
    (3, 2, 0, 0, 1), (3, 2, 1, 0, 3),
    (2, 0, 0, 1, 0), (2, 0, 1, 3, 0),
)
OWN = D // N
CHIPS = N // 2
FULL_W = (SHARD // 16) * 16


def kernel(
    hidden, gain, wt, teacher, labels, cot,
    out, loss,
    hid, w, t_v, land, relay, feats, logits, fg, g_now, g_next,
    lse_src, lse_land, st_src, st_land, fin_src, fin_land,
    cx_src, cx_land, rs_src, rs_land,
    a_b, b_b, c_b, l_b, r_b, mx_b, soft_b, hard_b, pick_b, cross_b, inner_b, rows_v,
    loc_sem, w_sem, ts, tr, fs, ft, ms, mr, cs, cr, rs, rr,
):
    me = lax.axis_index("vocab")
    chip = lax.div(me, 2)
    core = lax.rem(me, 2)
    width = lax.axis_size("dp") // 2
    x = lax.rem(lax.axis_index("dp"), width)
    y = lax.rem(chip, 4)
    z = lax.div(me, 8) * 2 + lax.div(lax.axis_index("dp"), width)

    def group_index(dy, dz, c):
        return (lax.div(lax.rem(z + dz, 4), 2) * 4 + lax.rem(y + dy, 4)) * 2 + c

    def device(dy, dz, c):
        return {
            "dp": lax.rem(z + dz, 2) * width + x,
            "vocab": group_index(dy, dz, c),
        }

    lane = lax.broadcasted_iota(jnp.int32, (ROWS, LANES), 1)
    places = [(lane + i * LANES).astype(F32) for i in range(BLOCK_TILES)]
    my_rows = pl.ds(pl.multiple_of(me * ROWS, ROWS), ROWS)

    hid_copy = pltpu.make_async_copy(hidden, hid, loc_sem.at[0])
    hid_copy.start()
    t_copy = pltpu.make_async_copy(teacher, t_v, loc_sem.at[1])
    t_copy.start()
    w[FULL_W:PAD, :] = jnp.zeros((PAD - FULL_W, D), BF16)
    w_copies = []
    for c in range(BLOCKS):
        lo, hi = c * BLOCK, min((c + 1) * BLOCK, SHARD)
        copy = pltpu.make_async_copy(wt.at[lo:hi], w.at[lo:hi], w_sem.at[c])
        copy.start()
        w_copies.append(copy)

    barrier = pltpu.get_barrier_semaphore()

    def greet(k, _):
        pl.semaphore_signal(
            barrier, inc=1, device_id={"vocab": lax.rem(me + k, N)}, device_id_type=MESH
        )
        return 0

    lax.fori_loop(1, N, greet, 0)
    for dz in (1, 3):
        for dy in (0, 1, 3):
            for c in (0, 1):
                pl.semaphore_signal(
                    barrier, inc=1, device_id=device(dy, dz, c), device_id_type=MESH
                )
    pl.semaphore_wait(barrier, N - 1 + 12)

    def remote_to(src, dst, send_sem, recv_sem, target):
        return pltpu.make_async_remote_copy(
            src_ref=src, dst_ref=dst, send_sem=send_sem, recv_sem=recv_sem,
            device_id=target, device_id_type=MESH,
        )

    def remote(src, dst, send_sem, recv_sem, d):
        return remote_to(src, dst, send_sem, recv_sem, {"vocab": d})

    def columns_of(c):
        first, count = PIECES[c]
        return slice(first * LANES, (first + count) * LANES)

    def piece_copies(d, c, into):
        first, count = PIECES[c]
        base = lax.div(d * SHARD, LANES)
        spans = [(base + first, first, count)]
        if first + count > TILES:
            spans = [
                (base + first, first, count - 1),
                (jnp.minimum(base + TILES, VTILES - 1), TILES, 1),
            ]
        for start, at, tiles in spans:
            yield (
                teacher.at[:, pl.ds(pl.multiple_of(start * LANES, LANES), tiles * LANES)],
                into(slice(at * LANES, (at + tiles) * LANES)),
            )

    for c in range(len(PIECES)):
        for p, (dy, dz, dc, ry, rz) in enumerate(RELAYED):
            d = group_index(dy, dz, dc)
            for src, dst in piece_copies(d, c, lambda cols, p=p: relay.at[p, :, cols]):
                remote_to(src, dst, ts.at[c], ft.at[c], device(ry, rz, core)).start()
        for dy, dc in ((1, 0), (3, 0), (1, 1), (3, 1)):
            d = group_index(dy, 0, dc)
            for src, dst in piece_copies(d, c, lambda cols: land.at[my_rows, cols]):
                remote(src, dst, ts.at[c], tr.at[c], d).start()
        sibling = chip * 2 + (1 - core)
        for src, dst in piece_copies(sibling, c, lambda cols: land.at[my_rows, cols]):
            remote(src, dst, ts.at[c], tr.at[c], sibling).start()
        for src, dst in piece_copies(me, c, lambda cols: land.at[my_rows, cols]):
            pltpu.make_async_copy(src, dst, tr.at[c]).start()

    def forward_pieces(c):
        cols = columns_of(c)
        wait_for(relay.at[:, :, cols], ft.at[c])
        for p, (dy, dz, dc, ry, rz) in enumerate(RELAYED):
            origin = group_index(4 - ry, 4 - rz, core)
            rows = pl.ds(pl.multiple_of(origin * ROWS, ROWS), ROWS)
            remote_to(
                relay.at[p, :, cols], land.at[rows, cols], fs.at[c], tr.at[c],
                device(4 + dy - ry, 4 + dz - rz, dc),
            ).start()

    def wait_for(ref, sem):
        pltpu.make_async_copy(ref, ref, sem).wait()

    t_copy.wait()
    wide = 33
    steps = VTILES // wide
    rest = VTILES - steps * wide

    def t_tiles(i, count):
        start = i * (wide * LANES)
        return [
            t_v[:, pl.ds(pl.multiple_of(start + t * LANES, LANES), LANES)] for t in range(count)
        ]

    def tile_max(i, accs, count=wide):
        accs = list(accs)
        for t, x in enumerate(t_tiles(i, count)):
            accs[t % 4] = jnp.maximum(accs[t % 4], x)
        return tuple(accs)

    accs = tile_max(steps, (t_v[:, :LANES],) * 4, rest)
    accs = lax.fori_loop(0, steps, tile_max, accs)
    top = jnp.maximum(jnp.maximum(accs[0], accs[1]), jnp.maximum(accs[2], accs[3]))
    top = (0.5 * LOG2E) * jnp.max(top.astype(F32), axis=1, keepdims=True)

    def tile_sum(i, accs, count=wide):
        accs = list(accs)
        for t, x in enumerate(t_tiles(i, count)):
            accs[t % 4] = accs[t % 4] + jnp.exp2((0.5 * LOG2E) * x.astype(F32) - top)
        return tuple(accs)

    accs = tile_sum(steps, (jnp.zeros((ROWS, LANES), F32),) * 4, rest)
    accs = lax.fori_loop(0, steps, tile_sum, accs)
    total = jnp.sum((accs[0] + accs[1]) + (accs[2] + accs[3]), axis=1, keepdims=True)
    lse_src[...] = jnp.broadcast_to(top + LOG2E * jnp.log(total), (ROWS, LANES))

    def send_lse(k, _):
        remote(
            lse_src, lse_land.at[my_rows, :], ms.at[0], mr.at[0], lax.rem(me + k, N)
        ).start()
        return 0

    pltpu.make_async_copy(lse_src, lse_land.at[my_rows, :], mr.at[0]).start()
    lax.fori_loop(1, N, send_lse, 0)

    forward_pieces(0)

    local = labels[...] - me * SHARD
    inside = jnp.logical_and(local >= 0, local < SHARD)
    local = jnp.where(inside, local, -1).astype(F32)
    columns = jnp.concatenate(
        [local, cot[...], jnp.zeros((LANES - 2, TOK), F32)], axis=0
    ).T
    l_b[...] = jnp.broadcast_to(columns[:, 0:1], (TOK, LANES))
    c_b[...] = jnp.broadcast_to(columns[:, 1:2], (TOK, LANES))

    hid_copy.wait()

    tall = 64

    def make_features(s, _):
        at = pl.ds(pl.multiple_of(s * tall, tall), tall)
        acc = jnp.zeros((tall, LANES), F32)
        for t in range(D // LANES):
            h = hid[at, t * LANES : (t + 1) * LANES].astype(F32)
            acc = acc + h * h
        r = lax.rsqrt(jnp.sum(acc, axis=1, keepdims=True) * (1.0 / D) + EPSILON)
        r = jnp.broadcast_to(r, (tall, LANES))
        r_b[at, :] = r
        for t in range(D // LANES):
            cols = slice(t * LANES, (t + 1) * LANES)
            feats[at, cols] = ((hid[at, cols].astype(F32) * r) * gain[:, cols]).astype(BF16)
        return 0

    lax.fori_loop(0, TOK // tall, make_features, 0)

    zeros = jnp.zeros((TOK, LANES), F32)
    mx_b[...] = jnp.full((TOK, LANES), -1e30, F32)
    soft_b[...] = zeros
    hard_b[...] = zeros
    pick_b[...] = zeros
    for copy in w_copies:
        copy.wait()

    forward_pieces(1)

    def forward(c):
        logits[:, c * FWD : (c + 1) * FWD] = lax.dot_general(
            feats[...], w[c * FWD : (c + 1) * FWD, :], (((1,), (1,)), ((), ())),
            preferred_element_type=F32,
        )

    def student_sums(c, s):
        at = slice(s * ROWS, (s + 1) * ROWS)
        tiles = []
        for i in range(FWD // LANES):
            start = c * FWD + i * LANES
            v = logits[at, start : start + LANES]
            if start + LANES > SHARD:
                v = jnp.where(lane < SHARD - start, v, -1e30)
                logits[at, start : start + LANES] = v
            tiles.append(v)
        top = mx_b[at, :]
        label = l_b[at, :]
        new = top
        for v in tiles:
            new = jnp.maximum(new, v)
        mx_b[at, :] = new
        scale = jnp.exp2((0.5 * LOG2E) * (top - new))
        soft = soft_b[at, :] * scale
        hard = hard_b[at, :] * (scale * scale)
        picked = pick_b[at, :]
        for i, v in enumerate(tiles):
            if i % BLOCK_TILES == 0:
                here = label - float(c * FWD + i * LANES)
            e = jnp.exp2((0.5 * LOG2E) * (v - new))
            soft = soft + e
            hard = hard + e * e
            picked = picked + jnp.where(places[i % BLOCK_TILES] == here, v, 0.0)
        soft_b[at, :] = soft
        hard_b[at, :] = hard
        pick_b[at, :] = picked

    for c in range(FWDS + 1):
        if c == 2:
            forward_pieces(2)
        if c > 0:
            for s in range(TOK // ROWS):
                student_sums(c - 1, s)
        if c < FWDS:
            forward(c)

    forward_pieces(3)
    wide_lane = lax.broadcasted_iota(jnp.int32, (TOK, LANES), 1)
    top = mx_b[...]
    m = jnp.max(top, axis=1, keepdims=True)
    scale = jnp.exp2((0.5 * LOG2E) * (top - m))
    soft = jnp.sum(soft_b[...] * scale, axis=1, keepdims=True)
    hard = jnp.sum(hard_b[...] * (scale * scale), axis=1, keepdims=True)
    picked = jnp.sum(pick_b[...], axis=1, keepdims=True)
    stat = jnp.where(wide_lane == 0, m, jnp.where(wide_lane == 1, soft, hard))
    st_src[...] = jnp.where(wide_lane == 3, picked, stat).T[0:8, :]

    def send_stats(k, _):
        remote(
            st_src, st_land.at[me], ms.at[1], mr.at[1], lax.rem(me + k, N)
        ).start()
        return 0

    pltpu.make_async_copy(st_src, st_land.at[me], mr.at[1]).start()
    lax.fori_loop(1, N, send_stats, 0)
    wait_for(st_land, mr.at[1])

    top = st_land[0, 0:1, :]
    for s in range(1, N):
        top = jnp.maximum(top, st_land[s, 0:1, :])
    soft = jnp.zeros((1, TOK), F32)
    hard = jnp.zeros((1, TOK), F32)
    picked = jnp.zeros((1, TOK), F32)
    for s in range(N):
        stat = st_land[s]
        scale = jnp.exp2((0.5 * LOG2E) * (stat[0:1] - top))
        soft = soft + stat[1:2] * scale
        hard = hard + stat[2:3] * (scale * scale)
        picked = picked + stat[3:4]
    lse_soft = 0.5 * top + jnp.log(soft)
    rows_v[0:1, :] = lse_soft
    rows_v[1:2, :] = top + jnp.log(hard)
    rows_v[2:3, :] = picked
    columns = jnp.concatenate(
        [
            LOG2E * lse_soft,
            0.5 * cot[...] * (soft * soft) / hard,
            jnp.zeros((LANES - 2, TOK), F32),
        ],
        axis=0,
    ).T
    a_b[...] = jnp.broadcast_to(columns[:, 0:1], (TOK, LANES))
    b_b[...] = jnp.broadcast_to(columns[:, 1:2], (TOK, LANES))
    cross_b[...] = zeros
    inner_b[...] = zeros
    fg[...] = jnp.zeros((TOK, D), F32)
    wait_for(lse_land, mr.at[0])

    off = lax.rem(me * SHARD, LANES)
    shift = lax.rem(LANES - off, LANES)
    keep = lane < LANES - off
    partner = chip * 2 + (1 - core)

    def wait_piece(c):
        wait_for(land.at[:, columns_of(c)], tr.at[c])

    def gradient(c, s, g_v):
        at = pl.ds(s * ROWS, ROWS)
        lse_s, b, ct = a_b[at, :], b_b[at, :], c_b[at, :]
        label = l_b[at, :] - jnp.float32(c * BLOCK)
        lse_t = lse_land[at, :]
        half = 0.5 * ct
        cross, inner = cross_b[at, :], inner_b[at, :]

        def turned(i):
            start = pl.multiple_of(c * BLOCK + i * LANES, LANES)
            return pltpu.roll(land[at, pl.ds(start, LANES)].astype(F32), shift, 1)

        here = turned(0)
        for i in range(BLOCK_TILES):
            after = turned(i + 1)
            x = jnp.where(keep, here, after)
            here = after
            v = logits[at, pl.ds(pl.multiple_of(c * BLOCK + i * LANES, LANES), LANES)]
            p = jnp.exp2((0.5 * LOG2E) * x - lse_t)
            e = jnp.exp2((0.5 * LOG2E) * v - lse_s)
            if i == BLOCK_TILES - 1:
                p = jnp.where(lane < SHARD - i * LANES - c * BLOCK, p, 0.0)
            cross = cross + p * (x - v)
            g = e * (ct + e * b) - ct * p
            g = g - jnp.where(places[i] == label, half, 0.0)
            g = g.astype(BF16)
            g_v[at, i * LANES : (i + 1) * LANES] = g
            inner = inner + g.astype(F32) * v
        cross_b[at, :] = cross
        inner_b[at, :] = inner

    wait_piece(0)
    for s in range(TOK // ROWS):
        gradient(0, s, g_now)

    def step(c, _):
        for p in range(1, len(PIECES)):

            @pl.when(c + 1 == 2 * p)
            def _():
                wait_piece(p)

        for s in range(TOK // ROWS):
            gradient(c + 1, s, g_next)
        rows = pl.ds(pl.multiple_of(c * BLOCK, BLOCK), BLOCK)
        fg[...] += jnp.dot(g_now[...], w[rows, :], preferred_element_type=F32)
        g_now[...] = g_next[...]
        return 0

    lax.fori_loop(0, BLOCKS - 1, step, 0)

    cross = jnp.sum(cross_b[...], axis=1, keepdims=True)
    inner = jnp.sum(inner_b[...], axis=1, keepdims=True)
    stat = jnp.where(wide_lane == 0, cross, inner)
    fin_src[...] = jnp.where(wide_lane == 2, LN2 * lse_land[...], stat).T[0:8, :]

    def send_final(k, _):
        remote(
            fin_src, fin_land.at[me], ms.at[2], mr.at[2], lax.rem(me + k, N)
        ).start()
        return 0

    pltpu.make_async_copy(fin_src, fin_land.at[me], mr.at[2]).start()
    lax.fori_loop(1, N, send_final, 0)

    fg[...] += jnp.dot(g_now[...], w[PAD - BLOCK :, :], preferred_element_type=F32)

    def half_of(n, c):
        return fg[:, pl.ds(pl.multiple_of((2 * n + c) * OWN, OWN), OWN)]

    def give(k, _):
        n = lax.rem(chip + 1 + k, CHIPS)
        cx_src[n] = half_of(n, 1 - core).astype(BF16)
        remote(cx_src.at[n], cx_land.at[n], cs.at[0], cr.at[n], partner).start()
        return 0

    lax.fori_loop(0, CHIPS, give, 0)

    def own_half(n):
        return half_of(n, core) + cx_land[n].astype(F32)

    def share(k, _):
        n = lax.rem(chip + 1 + k, CHIPS)
        wait_for(cx_land.at[n], cr.at[n])
        rs_src[n] = own_half(n).astype(BF16)
        remote(rs_src.at[n], rs_land.at[chip], rs, rr, n * 2 + core).start()
        return 0

    lax.fori_loop(0, CHIPS - 1, share, 0)
    wait_for(cx_land.at[chip], cr.at[chip])

    wait_for(fin_land, mr.at[2])
    cross = jnp.zeros((1, TOK), F32)
    inner = jnp.zeros((1, TOK), F32)
    for s in range(N):
        stat = fin_land[s]
        cross = cross + stat[0:1]
        inner = inner + stat[1:2]
    kl = 0.5 * cross - fin_src[2:3, :] + rows_v[0:1, :]
    loss[...] = 2.0 * kl + 0.5 * (rows_v[1:2, :] - rows_v[2:3, :])
    columns = jnp.concatenate(
        [inner * (1.0 / D), jnp.zeros((LANES - 1, TOK), F32)], axis=0
    ).T
    a_b[...] = jnp.broadcast_to(columns[:, 0:1], (TOK, LANES))

    wait_for(rs_land.at[0 : CHIPS - 1], rr)
    mine = pl.ds(pl.multiple_of(me * OWN, OWN), OWN)
    total = own_half(chip)
    for k in range(1, CHIPS):
        total = total + rs_land[lax.rem(chip + k, CHIPS)].astype(F32)
    r = r_b[...]
    normed = hid[:, mine].astype(F32) * r
    out[...] = (r * (gain[:, mine] * total - normed * a_b[...])).astype(BF16)

    for c in range(len(PIECES)):
        wait_for(land.at[0 : TOK - ROWS, columns_of(c)], ts.at[c])
        wait_for(relay.at[:, :, columns_of(c)], fs.at[c])
    wait_for(lse_land.at[0 : TOK - ROWS], ms.at[0])
    wait_for(st_land.at[0 : N - 1], ms.at[1])
    wait_for(fin_land.at[0 : N - 1], ms.at[2])
    wait_for(cx_src, cs.at[0])
    wait_for(rs_src.at[0 : CHIPS - 1], rs)


def on_device(hidden, norm_gain, head_weight, teacher, labels, cotangent):
    vmem = pl.BlockSpec(memory_space=pltpu.VMEM)
    hbm = pl.BlockSpec(memory_space=pl.ANY)
    dma = pltpu.SemaphoreType.DMA
    column = pltpu.VMEM((TOK, LANES), F32)
    grad, loss = pl.pallas_call(
        kernel,
        out_shape=(
            jax.ShapeDtypeStruct((TOK, OWN), BF16),
            jax.ShapeDtypeStruct((1, TOK), F32),
        ),
        in_specs=[hbm, vmem, hbm, hbm, vmem, vmem],
        out_specs=(vmem, vmem),
        scratch_shapes=[
            pltpu.VMEM((TOK, D), BF16),
            pltpu.VMEM((PAD, D), BF16),
            pltpu.VMEM((ROWS, VOCAB), BF16),
            pltpu.VMEM((TOK, PAD + LANES), BF16),
            pltpu.VMEM((len(RELAYED), ROWS, PAD + LANES), BF16),
            pltpu.VMEM((TOK, D), BF16),
            pltpu.VMEM((TOK, PAD), F32),
            pltpu.VMEM((TOK, D), F32),
            pltpu.VMEM((TOK, BLOCK), BF16),
            pltpu.VMEM((TOK, BLOCK), BF16),
            pltpu.VMEM((ROWS, LANES), F32),
            column,
            pltpu.VMEM((8, TOK), F32),
            pltpu.VMEM((N, 8, TOK), F32),
            pltpu.VMEM((8, TOK), F32),
            pltpu.VMEM((N, 8, TOK), F32),
            pltpu.VMEM((CHIPS, TOK, OWN), BF16),
            pltpu.VMEM((CHIPS, TOK, OWN), BF16),
            pltpu.VMEM((CHIPS, TOK, OWN), BF16),
            pltpu.VMEM((CHIPS, TOK, OWN), BF16),
            column, column, column, column, column, column,
            column, column, column, column, column,
            pltpu.VMEM((8, TOK), F32),
            dma((2,)), dma((BLOCKS,)), dma((len(PIECES),)), dma((len(PIECES),)), dma((len(PIECES),)), dma((len(PIECES),)),
            dma((3,)), dma((3,)), dma((1,)), dma((CHIPS,)), dma, dma,
        ],
        compiler_params=pltpu.CompilerParams(
            collective_id=0, has_side_effects=True, vmem_limit_bytes=56 * 1024 * 1024
        ),
        cost_estimate=pl.CostEstimate(
            flops=4 * TOK * D * SHARD, bytes_accessed=20_000_000, transcendentals=3_000_000
        ),
    )(
        hidden,
        norm_gain.reshape(1, D),
        head_weight.T,
        teacher,
        labels.reshape(1, TOK),
        cotangent.reshape(1, TOK),
    )
    return grad, loss.reshape(TOK)


def solution(mesh):
    return jax.shard_map(
        on_device,
        mesh=mesh,
        in_specs=(P("dp", None), P(), P(None, "vocab"), P(("dp", "vocab"), None), P("dp"), P("dp")),
        out_specs=(P("dp", "vocab"), P("dp")),
        check_vma=False,
    )
```

```python
import jax
import jax.numpy as jnp
from jax import lax
from jax.experimental import pallas as pl
from jax.experimental.pallas import tpu as pltpu
from jax.sharding import PartitionSpec as P

EPSILON = 1e-05
MESH = pl.DeviceIdType.MESH
F32 = jnp.float32
BF16 = jnp.bfloat16

N = 16
TOK = 256
ROWS = TOK // N
D = 2048
VOCAB = 64128
SHARD = VOCAB // N
LANES = 128
TILES = 32
PAD = TILES * LANES
VTILES = VOCAB // LANES
VALID = SHARD - (TILES - 1) * LANES
PIECES = ((0, 9), (9, 8), (17, 8), (25, 8))
BLOCK = 512
BLOCKS = PAD // BLOCK
BLOCK_TILES = BLOCK // LANES
FWD = 1024
FWDS = PAD // FWD
LOG2E = 1.4426950408889634
LN2 = 0.6931471805599453
OWN = D // N
CHIPS = N // 2
FULL_W = (SHARD // 16) * 16


def kernel(
    hidden, gain, wt, teacher, labels, cot,
    out, loss,
    hid, w, t_v, land, feats, logits, fg, g_now, g_next,
    lse_src, lse_land, st_src, st_land, fin_src, fin_land,
    cx_src, cx_land, rs_src, rs_land,
    a_b, b_b, c_b, l_b, r_b, mx_b, soft_b, hard_b, pick_b, cross_b, inner_b, rows_v,
    loc_sem, w_sem, ts, tr, ms, mr, cs, cr, rs, rr,
):
    me = lax.axis_index("vocab")
    chip = lax.div(me, 2)
    core = lax.rem(me, 2)
    y = lax.rem(chip, 4)
    z_hi = lax.div(me, 8)
    lane = lax.broadcasted_iota(jnp.int32, (ROWS, LANES), 1)
    places = [(lane + i * LANES).astype(F32) for i in range(BLOCK_TILES)]
    my_rows = pl.ds(pl.multiple_of(me * ROWS, ROWS), ROWS)

    hid_copy = pltpu.make_async_copy(hidden, hid, loc_sem.at[0])
    hid_copy.start()
    t_copy = pltpu.make_async_copy(teacher, t_v, loc_sem.at[1])
    t_copy.start()
    w[FULL_W:PAD, :] = jnp.zeros((PAD - FULL_W, D), BF16)
    w_copies = []
    for c in range(BLOCKS):
        lo, hi = c * BLOCK, min((c + 1) * BLOCK, SHARD)
        w_copies.append(pltpu.make_async_copy(wt.at[lo:hi], w.at[lo:hi], w_sem.at[c]))
    for copy in w_copies[:2]:
        copy.start()

    barrier = pltpu.get_barrier_semaphore()

    def greet(k, _):
        pl.semaphore_signal(
            barrier, inc=1, device_id={"vocab": lax.rem(me + k, N)}, device_id_type=MESH
        )
        return 0

    lax.fori_loop(1, N, greet, 0)
    pl.semaphore_wait(barrier, N - 1)

    def remote(src, dst, send_sem, recv_sem, d):
        return pltpu.make_async_remote_copy(
            src_ref=src, dst_ref=dst, send_sem=send_sem, recv_sem=recv_sem,
            device_id={"vocab": d}, device_id_type=MESH,
        )

    def piece_copies(d, c):
        first, count = PIECES[c]
        base = lax.div(d * SHARD, LANES)
        spans = [(base + first, first, count)]
        if first + count > TILES:
            spans = [
                (base + first, first, count - 1),
                (jnp.minimum(base + TILES, VTILES - 1), TILES, 1),
            ]
        for start, at, tiles in spans:
            yield (
                teacher.at[:, pl.ds(pl.multiple_of(start * LANES, LANES), tiles * LANES)],
                land.at[my_rows, at * LANES : (at + tiles) * LANES],
            )

    for c in range(len(PIECES)):
        for dc in (0, 1):
            for dy, dz in ((0, 1), (1, 0), (3, 0), (2, 1), (1, 1), (2, 0), (3, 1)):
                d = (lax.rem(z_hi + dz, 2) * 4 + lax.rem(y + dy, 4)) * 2 + lax.rem(core + dc, 2)
                for src, dst in piece_copies(d, c):
                    remote(src, dst, ts.at[c], tr.at[c], d).start()
        sibling = chip * 2 + (1 - core)
        for src, dst in piece_copies(sibling, c):
            remote(src, dst, ts.at[c], tr.at[c], sibling).start()
        for src, dst in piece_copies(me, c):
            pltpu.make_async_copy(src, dst, tr.at[c]).start()
        for copy in w_copies[2 + 2 * c : 4 + 2 * c]:
            copy.start()

    def wait_for(ref, sem):
        pltpu.make_async_copy(ref, ref, sem).wait()

    t_copy.wait()
    wide = 33
    steps = VTILES // wide
    rest = VTILES - steps * wide

    def t_tiles(i, count):
        start = i * (wide * LANES)
        return [
            t_v[:, pl.ds(pl.multiple_of(start + t * LANES, LANES), LANES)] for t in range(count)
        ]

    def tile_max(i, accs, count=wide):
        accs = list(accs)
        for t, x in enumerate(t_tiles(i, count)):
            accs[t % 4] = jnp.maximum(accs[t % 4], x)
        return tuple(accs)

    accs = tile_max(steps, (t_v[:, :LANES],) * 4, rest)
    accs = lax.fori_loop(0, steps, tile_max, accs)
    top = jnp.maximum(jnp.maximum(accs[0], accs[1]), jnp.maximum(accs[2], accs[3]))
    top = (0.5 * LOG2E) * jnp.max(top.astype(F32), axis=1, keepdims=True)

    def tile_sum(i, accs, count=wide):
        accs = list(accs)
        for t, x in enumerate(t_tiles(i, count)):
            accs[t % 4] = accs[t % 4] + jnp.exp2((0.5 * LOG2E) * x.astype(F32) - top)
        return tuple(accs)

    accs = tile_sum(steps, (jnp.zeros((ROWS, LANES), F32),) * 4, rest)
    accs = lax.fori_loop(0, steps, tile_sum, accs)
    total = jnp.sum((accs[0] + accs[1]) + (accs[2] + accs[3]), axis=1, keepdims=True)
    lse_src[...] = jnp.broadcast_to(top + LOG2E * jnp.log(total), (ROWS, LANES))

    def send_lse(k, _):
        remote(
            lse_src, lse_land.at[my_rows, :], ms.at[0], mr.at[0], lax.rem(me + k, N)
        ).start()
        return 0

    pltpu.make_async_copy(lse_src, lse_land.at[my_rows, :], mr.at[0]).start()
    lax.fori_loop(1, N, send_lse, 0)

    local = labels[...] - me * SHARD
    inside = jnp.logical_and(local >= 0, local < SHARD)
    local = jnp.where(inside, local, -1).astype(F32)
    columns = jnp.concatenate(
        [local, cot[...], jnp.zeros((LANES - 2, TOK), F32)], axis=0
    ).T
    l_b[...] = jnp.broadcast_to(columns[:, 0:1], (TOK, LANES))
    c_b[...] = jnp.broadcast_to(columns[:, 1:2], (TOK, LANES))

    hid_copy.wait()

    tall = 64

    def make_features(s, _):
        at = pl.ds(pl.multiple_of(s * tall, tall), tall)
        acc = jnp.zeros((tall, LANES), F32)
        for t in range(D // LANES):
            h = hid[at, t * LANES : (t + 1) * LANES].astype(F32)
            acc = acc + h * h
        r = lax.rsqrt(jnp.sum(acc, axis=1, keepdims=True) * (1.0 / D) + EPSILON)
        r = jnp.broadcast_to(r, (tall, LANES))
        r_b[at, :] = r
        for t in range(D // LANES):
            cols = slice(t * LANES, (t + 1) * LANES)
            feats[at, cols] = ((hid[at, cols].astype(F32) * r) * gain[:, cols]).astype(BF16)
        return 0

    lax.fori_loop(0, TOK // tall, make_features, 0)

    zeros = jnp.zeros((TOK, LANES), F32)
    mx_b[...] = jnp.full((TOK, LANES), -1e30, F32)
    soft_b[...] = zeros
    hard_b[...] = zeros
    pick_b[...] = zeros

    def forward(c):
        for copy in w_copies[c * FWD // BLOCK : (c + 1) * FWD // BLOCK]:
            copy.wait()
        logits[:, c * FWD : (c + 1) * FWD] = lax.dot_general(
            feats[...], w[c * FWD : (c + 1) * FWD, :], (((1,), (1,)), ((), ())),
            preferred_element_type=F32,
        )

    def student_sums(c, s):
        at = slice(s * ROWS, (s + 1) * ROWS)
        tiles = []
        for i in range(FWD // LANES):
            start = c * FWD + i * LANES
            v = logits[at, start : start + LANES]
            if start + LANES > SHARD:
                v = jnp.where(lane < SHARD - start, v, -1e30)
                logits[at, start : start + LANES] = v
            tiles.append(v)
        top = mx_b[at, :]
        label = l_b[at, :]
        new = top
        for v in tiles:
            new = jnp.maximum(new, v)
        mx_b[at, :] = new
        scale = jnp.exp2((0.5 * LOG2E) * (top - new))
        soft = soft_b[at, :] * scale
        hard = hard_b[at, :] * (scale * scale)
        picked = pick_b[at, :]
        for i, v in enumerate(tiles):
            if i % BLOCK_TILES == 0:
                here = label - float(c * FWD + i * LANES)
            e = jnp.exp2((0.5 * LOG2E) * (v - new))
            soft = soft + e
            hard = hard + e * e
            picked = picked + jnp.where(places[i % BLOCK_TILES] == here, v, 0.0)
        soft_b[at, :] = soft
        hard_b[at, :] = hard
        pick_b[at, :] = picked

    for c in range(FWDS + 1):
        if c > 0:
            for s in range(TOK // ROWS):
                student_sums(c - 1, s)
        if c < FWDS:
            forward(c)

    wide_lane = lax.broadcasted_iota(jnp.int32, (TOK, LANES), 1)
    top = mx_b[...]
    m = jnp.max(top, axis=1, keepdims=True)
    scale = jnp.exp2((0.5 * LOG2E) * (top - m))
    soft = jnp.sum(soft_b[...] * scale, axis=1, keepdims=True)
    hard = jnp.sum(hard_b[...] * (scale * scale), axis=1, keepdims=True)
    picked = jnp.sum(pick_b[...], axis=1, keepdims=True)
    stat = jnp.where(wide_lane == 0, m, jnp.where(wide_lane == 1, soft, hard))
    st_src[...] = jnp.where(wide_lane == 3, picked, stat).T[0:8, :]

    def send_stats(k, _):
        remote(
            st_src, st_land.at[me], ms.at[1], mr.at[1], lax.rem(me + k, N)
        ).start()
        return 0

    pltpu.make_async_copy(st_src, st_land.at[me], mr.at[1]).start()
    lax.fori_loop(1, N, send_stats, 0)
    wait_for(st_land, mr.at[1])

    top = st_land[0, 0:1, :]
    for s in range(1, N):
        top = jnp.maximum(top, st_land[s, 0:1, :])
    soft = jnp.zeros((1, TOK), F32)
    hard = jnp.zeros((1, TOK), F32)
    picked = jnp.zeros((1, TOK), F32)
    for s in range(N):
        stat = st_land[s]
        scale = jnp.exp2((0.5 * LOG2E) * (stat[0:1] - top))
        soft = soft + stat[1:2] * scale
        hard = hard + stat[2:3] * (scale * scale)
        picked = picked + stat[3:4]
    lse_soft = 0.5 * top + jnp.log(soft)
    rows_v[0:1, :] = lse_soft
    rows_v[1:2, :] = top + jnp.log(hard)
    rows_v[2:3, :] = picked
    columns = jnp.concatenate(
        [
            LOG2E * lse_soft,
            0.5 * cot[...] * (soft * soft) / hard,
            jnp.zeros((LANES - 2, TOK), F32),
        ],
        axis=0,
    ).T
    a_b[...] = jnp.broadcast_to(columns[:, 0:1], (TOK, LANES))
    b_b[...] = jnp.broadcast_to(columns[:, 1:2], (TOK, LANES))
    cross_b[...] = zeros
    inner_b[...] = zeros
    fg[...] = jnp.zeros((TOK, D), F32)
    wait_for(lse_land, mr.at[0])

    off = lax.rem(me * SHARD, LANES)
    shift = lax.rem(LANES - off, LANES)
    keep = lane < LANES - off
    partner = chip * 2 + (1 - core)

    def wait_piece(c):
        first, count = PIECES[c]
        wait_for(land.at[:, first * LANES : (first + count) * LANES], tr.at[c])

    def gradient(c, s, g_v):
        at = pl.ds(s * ROWS, ROWS)
        lse_s, b, ct = a_b[at, :], b_b[at, :], c_b[at, :]
        label = l_b[at, :] - jnp.float32(c * BLOCK)
        lse_t = lse_land[at, :]
        half = 0.5 * ct
        cross, inner = cross_b[at, :], inner_b[at, :]

        def turned(i):
            start = pl.multiple_of(c * BLOCK + i * LANES, LANES)
            return pltpu.roll(land[at, pl.ds(start, LANES)].astype(F32), shift, 1)

        here = turned(0)
        for i in range(BLOCK_TILES):
            after = turned(i + 1)
            x = jnp.where(keep, here, after)
            here = after
            v = logits[at, pl.ds(pl.multiple_of(c * BLOCK + i * LANES, LANES), LANES)]
            p = jnp.exp2((0.5 * LOG2E) * x - lse_t)
            e = jnp.exp2((0.5 * LOG2E) * v - lse_s)
            if i == BLOCK_TILES - 1:
                p = jnp.where(lane < SHARD - i * LANES - c * BLOCK, p, 0.0)
            cross = cross + p * (x - v)
            g = e * (ct + e * b) - ct * p
            g = g - jnp.where(places[i] == label, half, 0.0)
            g = g.astype(BF16)
            g_v[at, i * LANES : (i + 1) * LANES] = g
            inner = inner + g.astype(F32) * v
        cross_b[at, :] = cross
        inner_b[at, :] = inner

    wait_piece(0)
    for s in range(TOK // ROWS):
        gradient(0, s, g_now)

    def step(c, _):
        for p in range(1, len(PIECES)):

            @pl.when(c + 1 == 2 * p)
            def _():
                wait_piece(p)

        for s in range(TOK // ROWS):
            gradient(c + 1, s, g_next)
        rows = pl.ds(pl.multiple_of(c * BLOCK, BLOCK), BLOCK)
        fg[...] += jnp.dot(g_now[...], w[rows, :], preferred_element_type=F32)
        g_now[...] = g_next[...]
        return 0

    lax.fori_loop(0, BLOCKS - 1, step, 0)

    cross = jnp.sum(cross_b[...], axis=1, keepdims=True)
    inner = jnp.sum(inner_b[...], axis=1, keepdims=True)
    stat = jnp.where(wide_lane == 0, cross, inner)
    fin_src[...] = jnp.where(wide_lane == 2, LN2 * lse_land[...], stat).T[0:8, :]

    def send_final(k, _):
        remote(
            fin_src, fin_land.at[me], ms.at[2], mr.at[2], lax.rem(me + k, N)
        ).start()
        return 0

    pltpu.make_async_copy(fin_src, fin_land.at[me], mr.at[2]).start()
    lax.fori_loop(1, N, send_final, 0)

    fg[...] += jnp.dot(g_now[...], w[PAD - BLOCK :, :], preferred_element_type=F32)

    def half_of(n, c):
        return fg[:, pl.ds(pl.multiple_of((2 * n + c) * OWN, OWN), OWN)]

    def give(k, _):
        n = lax.rem(chip + 1 + k, CHIPS)
        cx_src[n] = half_of(n, 1 - core).astype(BF16)
        remote(cx_src.at[n], cx_land.at[n], cs.at[0], cr.at[n], partner).start()
        return 0

    lax.fori_loop(0, CHIPS, give, 0)

    def own_half(n):
        return half_of(n, core) + cx_land[n].astype(F32)

    def share(k, _):
        n = lax.rem(chip + 1 + k, CHIPS)
        wait_for(cx_land.at[n], cr.at[n])
        rs_src[n] = own_half(n).astype(BF16)
        remote(rs_src.at[n], rs_land.at[chip], rs, rr, n * 2 + core).start()
        return 0

    lax.fori_loop(0, CHIPS - 1, share, 0)
    wait_for(cx_land.at[chip], cr.at[chip])

    wait_for(fin_land, mr.at[2])
    cross = jnp.zeros((1, TOK), F32)
    inner = jnp.zeros((1, TOK), F32)
    for s in range(N):
        stat = fin_land[s]
        cross = cross + stat[0:1]
        inner = inner + stat[1:2]
    kl = 0.5 * cross - fin_src[2:3, :] + rows_v[0:1, :]
    loss[...] = 2.0 * kl + 0.5 * (rows_v[1:2, :] - rows_v[2:3, :])
    columns = jnp.concatenate(
        [inner * (1.0 / D), jnp.zeros((LANES - 1, TOK), F32)], axis=0
    ).T
    a_b[...] = jnp.broadcast_to(columns[:, 0:1], (TOK, LANES))

    wait_for(rs_land.at[0 : CHIPS - 1], rr)
    mine = pl.ds(pl.multiple_of(me * OWN, OWN), OWN)
    total = own_half(chip)
    for k in range(1, CHIPS):
        total = total + rs_land[lax.rem(chip + k, CHIPS)].astype(F32)
    r = r_b[...]
    normed = hid[:, mine].astype(F32) * r
    out[...] = (r * (gain[:, mine] * total - normed * a_b[...])).astype(BF16)

    for c, (first, count) in enumerate(PIECES):
        wait_for(land.at[0 : TOK - ROWS, first * LANES : (first + count) * LANES], ts.at[c])
    wait_for(lse_land.at[0 : TOK - ROWS], ms.at[0])
    wait_for(st_land.at[0 : N - 1], ms.at[1])
    wait_for(fin_land.at[0 : N - 1], ms.at[2])
    wait_for(cx_src, cs.at[0])
    wait_for(rs_src.at[0 : CHIPS - 1], rs)


def finish(grad, loss, grad_out, loss_out):
    grad_out[...] = grad[...]
    loss_out[...] = loss[...]


def on_device(hidden, norm_gain, head_weight, teacher, labels, cotangent):
    vmem = pl.BlockSpec(memory_space=pltpu.VMEM)
    hbm = pl.BlockSpec(memory_space=pl.ANY)
    dma = pltpu.SemaphoreType.DMA
    column = pltpu.VMEM((TOK, LANES), F32)
    grad, loss = pl.pallas_call(
        kernel,
        out_shape=(
            jax.ShapeDtypeStruct((TOK, OWN), BF16),
            jax.ShapeDtypeStruct((1, TOK), F32),
        ),
        in_specs=[hbm, vmem, hbm, hbm, vmem, vmem],
        out_specs=(vmem, vmem),
        scratch_shapes=[
            pltpu.VMEM((TOK, D), BF16),
            pltpu.VMEM((PAD, D), BF16),
            pltpu.VMEM((ROWS, VOCAB), BF16),
            pltpu.VMEM((TOK, PAD + LANES), BF16),
            pltpu.VMEM((TOK, D), BF16),
            pltpu.VMEM((TOK, PAD), F32),
            pltpu.VMEM((TOK, D), F32),
            pltpu.VMEM((TOK, BLOCK), BF16),
            pltpu.VMEM((TOK, BLOCK), BF16),
            pltpu.VMEM((ROWS, LANES), F32),
            column,
            pltpu.VMEM((8, TOK), F32),
            pltpu.VMEM((N, 8, TOK), F32),
            pltpu.VMEM((8, TOK), F32),
            pltpu.VMEM((N, 8, TOK), F32),
            pltpu.VMEM((CHIPS, TOK, OWN), BF16),
            pltpu.VMEM((CHIPS, TOK, OWN), BF16),
            pltpu.VMEM((CHIPS, TOK, OWN), BF16),
            pltpu.VMEM((CHIPS, TOK, OWN), BF16),
            column, column, column, column, column, column,
            column, column, column, column, column,
            pltpu.VMEM((8, TOK), F32),
            dma((2,)), dma((BLOCKS,)), dma((len(PIECES),)), dma((len(PIECES),)),
            dma((3,)), dma((3,)), dma((1,)), dma((CHIPS,)), dma, dma,
        ],
        compiler_params=pltpu.CompilerParams(
            collective_id=0, has_side_effects=True, vmem_limit_bytes=56 * 1024 * 1024
        ),
        cost_estimate=pl.CostEstimate(
            flops=4 * TOK * D * SHARD, bytes_accessed=20_000_000, transcendentals=3_000_000
        ),
    )(
        hidden,
        norm_gain.reshape(1, D),
        head_weight.T,
        teacher,
        labels.reshape(1, TOK),
        cotangent.reshape(1, TOK),
    )
    grad, loss = pl.pallas_call(
        finish,
        out_shape=(
            jax.ShapeDtypeStruct((TOK, OWN), BF16),
            jax.ShapeDtypeStruct((1, TOK), F32),
        ),
        in_specs=[vmem, vmem],
        out_specs=(vmem, vmem),
    )(grad, loss)
    return grad, loss.reshape(TOK)


def solution(mesh):
    return jax.shard_map(
        on_device,
        mesh=mesh,
        in_specs=(P("dp", None), P(), P(None, "vocab"), P(("dp", "vocab"), None), P("dp"), P("dp")),
        out_specs=(P("dp", "vocab"), P("dp")),
        check_vma=False,
    )
```

```python
import jax
import jax.numpy as jnp
from jax import lax
from jax.experimental import pallas as pl
from jax.experimental.pallas import tpu as pltpu
from jax.sharding import PartitionSpec as P

EPSILON = 1e-05
MESH = pl.DeviceIdType.MESH
F32 = jnp.float32
BF16 = jnp.bfloat16

N = 16
TOK = 256
ROWS = TOK // N
D = 2048
VOCAB = 64128
SHARD = VOCAB // N
LANES = 128
TILES = 32
PAD = TILES * LANES
VTILES = VOCAB // LANES
VALID = SHARD - (TILES - 1) * LANES
PIECES = ((0, 9), (9, 8), (17, 8), (25, 8))
BLOCK = 512
BLOCKS = PAD // BLOCK
BLOCK_TILES = BLOCK // LANES
FWD = 1024
FWDS = PAD // FWD
LOG2E = 1.4426950408889634
LN2 = 0.6931471805599453
OWN = D // N
CHIPS = N // 2
FULL_W = (SHARD // 16) * 16


def kernel(
    hidden, gain, wt, teacher, labels, cot,
    out, loss,
    hid, w, t_v, land, feats, logits, fg, g_now, g_next,
    lse_src, lse_land, st_src, st_land, fin_src, fin_land,
    cx_src, cx_land, rs_src, rs_land,
    a_b, b_b, c_b, l_b, r_b, mx_b, soft_b, hard_b, pick_b, cross_b, inner_b, rows_v,
    loc_sem, w_sem, ts, tr, ms, mr, cs, cr, rs, rr,
):
    me = lax.axis_index("vocab")
    chip = lax.div(me, 2)
    core = lax.rem(me, 2)
    y = lax.rem(chip, 4)
    z_hi = lax.div(me, 8)
    lane = lax.broadcasted_iota(jnp.int32, (ROWS, LANES), 1)
    places = [(lane + i * LANES).astype(F32) for i in range(BLOCK_TILES)]
    my_rows = pl.ds(pl.multiple_of(me * ROWS, ROWS), ROWS)

    hid_copy = pltpu.make_async_copy(hidden, hid, loc_sem.at[0])
    hid_copy.start()
    t_copy = pltpu.make_async_copy(teacher, t_v, loc_sem.at[1])
    t_copy.start()
    w[FULL_W:PAD, :] = jnp.zeros((PAD - FULL_W, D), BF16)
    w_copies = []
    for c in range(BLOCKS):
        lo, hi = c * BLOCK, min((c + 1) * BLOCK, SHARD)
        w_copies.append(pltpu.make_async_copy(wt.at[lo:hi], w.at[lo:hi], w_sem.at[c]))
    for copy in w_copies[:2]:
        copy.start()

    barrier = pltpu.get_barrier_semaphore()

    def greet(k, _):
        pl.semaphore_signal(
            barrier, inc=1, device_id={"vocab": lax.rem(me + k, N)}, device_id_type=MESH
        )
        return 0

    lax.fori_loop(1, N, greet, 0)
    pl.semaphore_wait(barrier, N - 1)

    def remote(src, dst, send_sem, recv_sem, d):
        return pltpu.make_async_remote_copy(
            src_ref=src, dst_ref=dst, send_sem=send_sem, recv_sem=recv_sem,
            device_id={"vocab": d}, device_id_type=MESH,
        )

    def piece_copies(d, c):
        first, count = PIECES[c]
        base = lax.div(d * SHARD, LANES)
        spans = [(base + first, first, count)]
        if first + count > TILES:
            spans = [
                (base + first, first, count - 1),
                (jnp.minimum(base + TILES, VTILES - 1), TILES, 1),
            ]
        for start, at, tiles in spans:
            yield (
                teacher.at[:, pl.ds(pl.multiple_of(start * LANES, LANES), tiles * LANES)],
                land.at[my_rows, at * LANES : (at + tiles) * LANES],
            )

    def send_piece(c):
        for dc in (0, 1):
            for dy, dz in ((0, 1), (1, 0), (3, 0), (2, 1), (1, 1), (2, 0), (3, 1)):
                d = (lax.rem(z_hi + dz, 2) * 4 + lax.rem(y + dy, 4)) * 2 + lax.rem(core + dc, 2)
                for src, dst in piece_copies(d, c):
                    remote(src, dst, ts.at[c], tr.at[c], d).start()
        sibling = chip * 2 + (1 - core)
        for src, dst in piece_copies(sibling, c):
            remote(src, dst, ts.at[c], tr.at[c], sibling).start()
        for src, dst in piece_copies(me, c):
            pltpu.make_async_copy(src, dst, tr.at[c]).start()

    send_piece(0)
    for copy in w_copies[2:]:
        copy.start()

    def wait_for(ref, sem):
        pltpu.make_async_copy(ref, ref, sem).wait()

    t_copy.wait()
    wide = 33
    steps = VTILES // wide
    rest = VTILES - steps * wide

    def t_tiles(i, count):
        start = i * (wide * LANES)
        return [
            t_v[:, pl.ds(pl.multiple_of(start + t * LANES, LANES), LANES)] for t in range(count)
        ]

    def tile_max(i, accs, count=wide):
        accs = list(accs)
        for t, x in enumerate(t_tiles(i, count)):
            accs[t % 4] = jnp.maximum(accs[t % 4], x)
        return tuple(accs)

    accs = tile_max(steps, (t_v[:, :LANES],) * 4, rest)
    accs = lax.fori_loop(0, steps, tile_max, accs)
    top = jnp.maximum(jnp.maximum(accs[0], accs[1]), jnp.maximum(accs[2], accs[3]))
    top = (0.5 * LOG2E) * jnp.max(top.astype(F32), axis=1, keepdims=True)

    def tile_sum(i, accs, count=wide):
        accs = list(accs)
        for t, x in enumerate(t_tiles(i, count)):
            accs[t % 4] = accs[t % 4] + jnp.exp2((0.5 * LOG2E) * x.astype(F32) - top)
        return tuple(accs)

    accs = tile_sum(steps, (jnp.zeros((ROWS, LANES), F32),) * 4, rest)
    accs = lax.fori_loop(0, steps, tile_sum, accs)
    total = jnp.sum((accs[0] + accs[1]) + (accs[2] + accs[3]), axis=1, keepdims=True)
    lse_src[...] = jnp.broadcast_to(top + LOG2E * jnp.log(total), (ROWS, LANES))

    def send_lse(k, _):
        remote(
            lse_src, lse_land.at[my_rows, :], ms.at[0], mr.at[0], lax.rem(me + k, N)
        ).start()
        return 0

    pltpu.make_async_copy(lse_src, lse_land.at[my_rows, :], mr.at[0]).start()
    lax.fori_loop(1, N, send_lse, 0)

    send_piece(1)

    local = labels[...] - me * SHARD
    inside = jnp.logical_and(local >= 0, local < SHARD)
    local = jnp.where(inside, local, -1).astype(F32)
    columns = jnp.concatenate(
        [local, cot[...], jnp.zeros((LANES - 2, TOK), F32)], axis=0
    ).T
    l_b[...] = jnp.broadcast_to(columns[:, 0:1], (TOK, LANES))
    c_b[...] = jnp.broadcast_to(columns[:, 1:2], (TOK, LANES))

    hid_copy.wait()

    tall = 64

    def make_features(s, _):
        at = pl.ds(pl.multiple_of(s * tall, tall), tall)
        acc = jnp.zeros((tall, LANES), F32)
        for t in range(D // LANES):
            h = hid[at, t * LANES : (t + 1) * LANES].astype(F32)
            acc = acc + h * h
        r = lax.rsqrt(jnp.sum(acc, axis=1, keepdims=True) * (1.0 / D) + EPSILON)
        r = jnp.broadcast_to(r, (tall, LANES))
        r_b[at, :] = r
        for t in range(D // LANES):
            cols = slice(t * LANES, (t + 1) * LANES)
            feats[at, cols] = ((hid[at, cols].astype(F32) * r) * gain[:, cols]).astype(BF16)
        return 0

    lax.fori_loop(0, TOK // tall, make_features, 0)

    zeros = jnp.zeros((TOK, LANES), F32)
    mx_b[...] = jnp.full((TOK, LANES), -1e30, F32)
    soft_b[...] = zeros
    hard_b[...] = zeros
    pick_b[...] = zeros

    def forward(c):
        for copy in w_copies[c * FWD // BLOCK : (c + 1) * FWD // BLOCK]:
            copy.wait()
        logits[:, c * FWD : (c + 1) * FWD] = lax.dot_general(
            feats[...], w[c * FWD : (c + 1) * FWD, :], (((1,), (1,)), ((), ())),
            preferred_element_type=F32,
        )

    def student_sums(c, s):
        at = slice(s * ROWS, (s + 1) * ROWS)
        tiles = []
        for i in range(FWD // LANES):
            start = c * FWD + i * LANES
            v = logits[at, start : start + LANES]
            if start + LANES > SHARD:
                v = jnp.where(lane < SHARD - start, v, -1e30)
                logits[at, start : start + LANES] = v
            tiles.append(v)
        top = mx_b[at, :]
        label = l_b[at, :]
        new = top
        for v in tiles:
            new = jnp.maximum(new, v)
        mx_b[at, :] = new
        scale = jnp.exp2((0.5 * LOG2E) * (top - new))
        soft = soft_b[at, :] * scale
        hard = hard_b[at, :] * (scale * scale)
        picked = pick_b[at, :]
        for i, v in enumerate(tiles):
            if i % BLOCK_TILES == 0:
                here = label - float(c * FWD + i * LANES)
            e = jnp.exp2((0.5 * LOG2E) * (v - new))
            soft = soft + e
            hard = hard + e * e
            picked = picked + jnp.where(places[i % BLOCK_TILES] == here, v, 0.0)
        soft_b[at, :] = soft
        hard_b[at, :] = hard
        pick_b[at, :] = picked

    for c in range(FWDS + 1):
        if c > 0:
            for s in range(TOK // ROWS):
                student_sums(c - 1, s)
        if c < FWDS:
            forward(c)

    wide_lane = lax.broadcasted_iota(jnp.int32, (TOK, LANES), 1)
    top = mx_b[...]
    m = jnp.max(top, axis=1, keepdims=True)
    scale = jnp.exp2((0.5 * LOG2E) * (top - m))
    soft = jnp.sum(soft_b[...] * scale, axis=1, keepdims=True)
    hard = jnp.sum(hard_b[...] * (scale * scale), axis=1, keepdims=True)
    picked = jnp.sum(pick_b[...], axis=1, keepdims=True)
    stat = jnp.where(wide_lane == 0, m, jnp.where(wide_lane == 1, soft, hard))
    st_src[...] = jnp.where(wide_lane == 3, picked, stat).T[0:8, :]

    def send_stats(k, _):
        remote(
            st_src, st_land.at[me], ms.at[1], mr.at[1], lax.rem(me + k, N)
        ).start()
        return 0

    pltpu.make_async_copy(st_src, st_land.at[me], mr.at[1]).start()
    lax.fori_loop(1, N, send_stats, 0)
    send_piece(2)
    send_piece(3)
    wait_for(st_land, mr.at[1])

    top = st_land[0, 0:1, :]
    for s in range(1, N):
        top = jnp.maximum(top, st_land[s, 0:1, :])
    soft = jnp.zeros((1, TOK), F32)
    hard = jnp.zeros((1, TOK), F32)
    picked = jnp.zeros((1, TOK), F32)
    for s in range(N):
        stat = st_land[s]
        scale = jnp.exp2((0.5 * LOG2E) * (stat[0:1] - top))
        soft = soft + stat[1:2] * scale
        hard = hard + stat[2:3] * (scale * scale)
        picked = picked + stat[3:4]
    lse_soft = 0.5 * top + jnp.log(soft)
    rows_v[0:1, :] = lse_soft
    rows_v[1:2, :] = top + jnp.log(hard)
    rows_v[2:3, :] = picked
    columns = jnp.concatenate(
        [
            LOG2E * lse_soft,
            0.5 * cot[...] * (soft * soft) / hard,
            jnp.zeros((LANES - 2, TOK), F32),
        ],
        axis=0,
    ).T
    a_b[...] = jnp.broadcast_to(columns[:, 0:1], (TOK, LANES))
    b_b[...] = jnp.broadcast_to(columns[:, 1:2], (TOK, LANES))
    cross_b[...] = zeros
    inner_b[...] = zeros
    fg[...] = jnp.zeros((TOK, D), F32)
    wait_for(lse_land, mr.at[0])

    off = lax.rem(me * SHARD, LANES)
    shift = lax.rem(LANES - off, LANES)
    keep = lane < LANES - off
    partner = chip * 2 + (1 - core)

    def wait_piece(c):
        first, count = PIECES[c]
        wait_for(land.at[:, first * LANES : (first + count) * LANES], tr.at[c])

    def gradient(c, s, g_v):
        at = pl.ds(s * ROWS, ROWS)
        lse_s, b, ct = a_b[at, :], b_b[at, :], c_b[at, :]
        label = l_b[at, :] - jnp.float32(c * BLOCK)
        lse_t = lse_land[at, :]
        half = 0.5 * ct
        cross, inner = cross_b[at, :], inner_b[at, :]

        def turned(i):
            start = pl.multiple_of(c * BLOCK + i * LANES, LANES)
            return pltpu.roll(land[at, pl.ds(start, LANES)].astype(F32), shift, 1)

        here = turned(0)
        for i in range(BLOCK_TILES):
            after = turned(i + 1)
            x = jnp.where(keep, here, after)
            here = after
            v = logits[at, pl.ds(pl.multiple_of(c * BLOCK + i * LANES, LANES), LANES)]
            p = jnp.exp2((0.5 * LOG2E) * x - lse_t)
            e = jnp.exp2((0.5 * LOG2E) * v - lse_s)
            if i == BLOCK_TILES - 1:
                p = jnp.where(lane < SHARD - i * LANES - c * BLOCK, p, 0.0)
            cross = cross + p * (x - v)
            g = e * (ct + e * b) - ct * p
            g = g - jnp.where(places[i] == label, half, 0.0)
            g = g.astype(BF16)
            g_v[at, i * LANES : (i + 1) * LANES] = g
            inner = inner + g.astype(F32) * v
        cross_b[at, :] = cross
        inner_b[at, :] = inner

    wait_piece(0)
    for s in range(TOK // ROWS):
        gradient(0, s, g_now)

    def step(c, _):
        for p in range(1, len(PIECES)):

            @pl.when(c + 1 == 2 * p)
            def _():
                wait_piece(p)

        for s in range(TOK // ROWS):
            gradient(c + 1, s, g_next)
        rows = pl.ds(pl.multiple_of(c * BLOCK, BLOCK), BLOCK)
        fg[...] += jnp.dot(g_now[...], w[rows, :], preferred_element_type=F32)
        g_now[...] = g_next[...]
        return 0

    lax.fori_loop(0, BLOCKS - 1, step, 0)

    cross = jnp.sum(cross_b[...], axis=1, keepdims=True)
    inner = jnp.sum(inner_b[...], axis=1, keepdims=True)
    stat = jnp.where(wide_lane == 0, cross, inner)
    fin_src[...] = jnp.where(wide_lane == 2, LN2 * lse_land[...], stat).T[0:8, :]

    def send_final(k, _):
        remote(
            fin_src, fin_land.at[me], ms.at[2], mr.at[2], lax.rem(me + k, N)
        ).start()
        return 0

    pltpu.make_async_copy(fin_src, fin_land.at[me], mr.at[2]).start()
    lax.fori_loop(1, N, send_final, 0)

    fg[...] += jnp.dot(g_now[...], w[PAD - BLOCK :, :], preferred_element_type=F32)

    def half_of(n, c):
        return fg[:, pl.ds(pl.multiple_of((2 * n + c) * OWN, OWN), OWN)]

    def give(k, _):
        n = lax.rem(chip + 1 + k, CHIPS)
        cx_src[n] = half_of(n, 1 - core).astype(BF16)
        remote(cx_src.at[n], cx_land.at[n], cs.at[0], cr.at[n], partner).start()
        return 0

    lax.fori_loop(0, CHIPS, give, 0)

    def own_half(n):
        return half_of(n, core) + cx_land[n].astype(F32)

    def share(k, _):
        n = lax.rem(chip + 1 + k, CHIPS)
        wait_for(cx_land.at[n], cr.at[n])
        rs_src[n] = own_half(n).astype(BF16)
        remote(rs_src.at[n], rs_land.at[chip], rs, rr, n * 2 + core).start()
        return 0

    lax.fori_loop(0, CHIPS - 1, share, 0)
    wait_for(cx_land.at[chip], cr.at[chip])

    wait_for(fin_land, mr.at[2])
    cross = jnp.zeros((1, TOK), F32)
    inner = jnp.zeros((1, TOK), F32)
    for s in range(N):
        stat = fin_land[s]
        cross = cross + stat[0:1]
        inner = inner + stat[1:2]
    kl = 0.5 * cross - fin_src[2:3, :] + rows_v[0:1, :]
    loss[...] = 2.0 * kl + 0.5 * (rows_v[1:2, :] - rows_v[2:3, :])
    columns = jnp.concatenate(
        [inner * (1.0 / D), jnp.zeros((LANES - 1, TOK), F32)], axis=0
    ).T
    a_b[...] = jnp.broadcast_to(columns[:, 0:1], (TOK, LANES))

    wait_for(rs_land.at[0 : CHIPS - 1], rr)
    mine = pl.ds(pl.multiple_of(me * OWN, OWN), OWN)
    total = own_half(chip)
    for k in range(1, CHIPS):
        total = total + rs_land[lax.rem(chip + k, CHIPS)].astype(F32)
    r = r_b[...]
    normed = hid[:, mine].astype(F32) * r
    out[...] = (r * (gain[:, mine] * total - normed * a_b[...])).astype(BF16)

    for c, (first, count) in enumerate(PIECES):
        wait_for(land.at[0 : TOK - ROWS, first * LANES : (first + count) * LANES], ts.at[c])
    wait_for(lse_land.at[0 : TOK - ROWS], ms.at[0])
    wait_for(st_land.at[0 : N - 1], ms.at[1])
    wait_for(fin_land.at[0 : N - 1], ms.at[2])
    wait_for(cx_src, cs.at[0])
    wait_for(rs_src.at[0 : CHIPS - 1], rs)


def finish(grad, loss, grad_out, loss_out):
    grad_out[...] = grad[...]
    loss_out[...] = loss[...]


def on_device(hidden, norm_gain, head_weight, teacher, labels, cotangent):
    vmem = pl.BlockSpec(memory_space=pltpu.VMEM)
    hbm = pl.BlockSpec(memory_space=pl.ANY)
    dma = pltpu.SemaphoreType.DMA
    column = pltpu.VMEM((TOK, LANES), F32)
    grad, loss = pl.pallas_call(
        kernel,
        out_shape=(
            jax.ShapeDtypeStruct((TOK, OWN), BF16),
            jax.ShapeDtypeStruct((1, TOK), F32),
        ),
        in_specs=[hbm, vmem, hbm, hbm, vmem, vmem],
        out_specs=(vmem, vmem),
        scratch_shapes=[
            pltpu.VMEM((TOK, D), BF16),
            pltpu.VMEM((PAD, D), BF16),
            pltpu.VMEM((ROWS, VOCAB), BF16),
            pltpu.VMEM((TOK, PAD + LANES), BF16),
            pltpu.VMEM((TOK, D), BF16),
            pltpu.VMEM((TOK, PAD), F32),
            pltpu.VMEM((TOK, D), F32),
            pltpu.VMEM((TOK, BLOCK), BF16),
            pltpu.VMEM((TOK, BLOCK), BF16),
            pltpu.VMEM((ROWS, LANES), F32),
            column,
            pltpu.VMEM((8, TOK), F32),
            pltpu.VMEM((N, 8, TOK), F32),
            pltpu.VMEM((8, TOK), F32),
            pltpu.VMEM((N, 8, TOK), F32),
            pltpu.VMEM((CHIPS, TOK, OWN), BF16),
            pltpu.VMEM((CHIPS, TOK, OWN), BF16),
            pltpu.VMEM((CHIPS, TOK, OWN), BF16),
            pltpu.VMEM((CHIPS, TOK, OWN), BF16),
            column, column, column, column, column, column,
            column, column, column, column, column,
            pltpu.VMEM((8, TOK), F32),
            dma((2,)), dma((BLOCKS,)), dma((len(PIECES),)), dma((len(PIECES),)),
            dma((3,)), dma((3,)), dma((1,)), dma((CHIPS,)), dma, dma,
        ],
        compiler_params=pltpu.CompilerParams(
            collective_id=0, has_side_effects=True, vmem_limit_bytes=56 * 1024 * 1024
        ),
        cost_estimate=pl.CostEstimate(
            flops=4 * TOK * D * SHARD, bytes_accessed=20_000_000, transcendentals=3_000_000
        ),
    )(
        hidden,
        norm_gain.reshape(1, D),
        head_weight.T,
        teacher,
        labels.reshape(1, TOK),
        cotangent.reshape(1, TOK),
    )
    grad, loss = pl.pallas_call(
        finish,
        out_shape=(
            jax.ShapeDtypeStruct((TOK, OWN), BF16),
            jax.ShapeDtypeStruct((1, TOK), F32),
        ),
        in_specs=[vmem, vmem],
        out_specs=(vmem, vmem),
    )(grad, loss)
    return grad, loss.reshape(TOK)


def solution(mesh):
    return jax.shard_map(
        on_device,
        mesh=mesh,
        in_specs=(P("dp", None), P(), P(None, "vocab"), P(("dp", "vocab"), None), P("dp"), P("dp")),
        out_specs=(P("dp", "vocab"), P("dp")),
        check_vma=False,
    )
```

```python
import jax
import jax.numpy as jnp
from jax import lax
from jax.experimental import pallas as pl
from jax.experimental.pallas import tpu as pltpu
from jax.sharding import PartitionSpec as P

EPSILON = 1e-05
MESH = pl.DeviceIdType.MESH
F32 = jnp.float32
BF16 = jnp.bfloat16

N = 16
TOK = 256
ROWS = TOK // N
D = 2048
VOCAB = 64128
SHARD = VOCAB // N
LANES = 128
TILES = 32
PAD = TILES * LANES
VTILES = VOCAB // LANES
VALID = SHARD - (TILES - 1) * LANES
PIECES = ((0, 9), (9, 8), (17, 8), (25, 4), (29, 4))
FIRST_BLOCK = (0, 2, 4, 6, 7)
BLOCK = 512
BLOCKS = PAD // BLOCK
BLOCK_TILES = BLOCK // LANES
FWD = 1024
FWDS = PAD // FWD
LOG2E = 1.4426950408889634
LN2 = 0.6931471805599453
OWN = D // N
CHIPS = N // 2
FULL_W = (SHARD // 16) * 16


def kernel(
    hidden, gain, wt, teacher, labels, cot,
    out, loss,
    hid, w, t_v, land, feats, logits, fg, g_now, g_next,
    lse_src, lse_land, st_src, st_land, fin_src, fin_land,
    cx_src, cx_land, rs_src, rs_land,
    a_b, b_b, c_b, l_b, r_b, mx_b, soft_b, hard_b, pick_b, cross_b, inner_b, rows_v,
    loc_sem, w_sem, ts, tr, ms, mr, cs, cr, rs, rr,
):
    me = lax.axis_index("vocab")
    chip = lax.div(me, 2)
    core = lax.rem(me, 2)
    y = lax.rem(chip, 4)
    z_hi = lax.div(me, 8)
    lane = lax.broadcasted_iota(jnp.int32, (ROWS, LANES), 1)
    places = [(lane + i * LANES).astype(F32) for i in range(BLOCK_TILES)]
    my_rows = pl.ds(pl.multiple_of(me * ROWS, ROWS), ROWS)

    hid_copy = pltpu.make_async_copy(hidden, hid, loc_sem.at[0])
    hid_copy.start()
    t_copy = pltpu.make_async_copy(teacher, t_v, loc_sem.at[1])
    t_copy.start()
    w[FULL_W:PAD, :] = jnp.zeros((PAD - FULL_W, D), BF16)
    w_copies = []
    for c in range(BLOCKS):
        lo, hi = c * BLOCK, min((c + 1) * BLOCK, SHARD)
        w_copies.append(pltpu.make_async_copy(wt.at[lo:hi], w.at[lo:hi], w_sem.at[c]))
    for copy in w_copies[:2]:
        copy.start()

    barrier = pltpu.get_barrier_semaphore()

    def greet(k, _):
        pl.semaphore_signal(
            barrier, inc=1, device_id={"vocab": lax.rem(me + k, N)}, device_id_type=MESH
        )
        return 0

    lax.fori_loop(1, N, greet, 0)
    pl.semaphore_wait(barrier, N - 1)

    def remote(src, dst, send_sem, recv_sem, d):
        return pltpu.make_async_remote_copy(
            src_ref=src, dst_ref=dst, send_sem=send_sem, recv_sem=recv_sem,
            device_id={"vocab": d}, device_id_type=MESH,
        )

    def piece_copies(d, c):
        first, count = PIECES[c]
        base = lax.div(d * SHARD, LANES)
        spans = [(base + first, first, count)]
        if first + count > TILES:
            spans = [
                (base + first, first, count - 1),
                (jnp.minimum(base + TILES, VTILES - 1), TILES, 1),
            ]
        for start, at, tiles in spans:
            yield (
                teacher.at[:, pl.ds(pl.multiple_of(start * LANES, LANES), tiles * LANES)],
                land.at[my_rows, at * LANES : (at + tiles) * LANES],
            )

    def send_piece(c):
        for dc in (0, 1):
            for dy, dz in ((0, 1), (1, 0), (3, 0), (2, 1), (1, 1), (2, 0), (3, 1)):
                d = (lax.rem(z_hi + dz, 2) * 4 + lax.rem(y + dy, 4)) * 2 + lax.rem(core + dc, 2)
                for src, dst in piece_copies(d, c):
                    remote(src, dst, ts.at[c], tr.at[c], d).start()
        sibling = chip * 2 + (1 - core)
        for src, dst in piece_copies(sibling, c):
            remote(src, dst, ts.at[c], tr.at[c], sibling).start()
        for src, dst in piece_copies(me, c):
            pltpu.make_async_copy(src, dst, tr.at[c]).start()

    send_piece(0)
    for copy in w_copies[2:]:
        copy.start()

    def wait_for(ref, sem):
        pltpu.make_async_copy(ref, ref, sem).wait()

    t_copy.wait()
    wide = 33
    steps = VTILES // wide
    rest = VTILES - steps * wide

    def t_tiles(i, count):
        start = i * (wide * LANES)
        return [
            t_v[:, pl.ds(pl.multiple_of(start + t * LANES, LANES), LANES)] for t in range(count)
        ]

    def tile_max(i, accs, count=wide):
        accs = list(accs)
        for t, x in enumerate(t_tiles(i, count)):
            accs[t % 4] = jnp.maximum(accs[t % 4], x)
        return tuple(accs)

    accs = tile_max(steps, (t_v[:, :LANES],) * 4, rest)
    accs = lax.fori_loop(0, steps, tile_max, accs)
    top = jnp.maximum(jnp.maximum(accs[0], accs[1]), jnp.maximum(accs[2], accs[3]))
    top = (0.5 * LOG2E) * jnp.max(top.astype(F32), axis=1, keepdims=True)

    def tile_sum(i, accs, count=wide):
        accs = list(accs)
        for t, x in enumerate(t_tiles(i, count)):
            accs[t % 4] = accs[t % 4] + jnp.exp2((0.5 * LOG2E) * x.astype(F32) - top)
        return tuple(accs)

    accs = tile_sum(steps, (jnp.zeros((ROWS, LANES), F32),) * 4, rest)
    accs = lax.fori_loop(0, steps, tile_sum, accs)
    total = jnp.sum((accs[0] + accs[1]) + (accs[2] + accs[3]), axis=1, keepdims=True)
    lse_src[...] = jnp.broadcast_to(top + LOG2E * jnp.log(total), (ROWS, LANES))

    def send_lse(k, _):
        remote(
            lse_src, lse_land.at[my_rows, :], ms.at[0], mr.at[0], lax.rem(me + k, N)
        ).start()
        return 0

    pltpu.make_async_copy(lse_src, lse_land.at[my_rows, :], mr.at[0]).start()
    lax.fori_loop(1, N, send_lse, 0)

    send_piece(1)

    local = labels[...] - me * SHARD
    inside = jnp.logical_and(local >= 0, local < SHARD)
    local = jnp.where(inside, local, -1).astype(F32)
    columns = jnp.concatenate(
        [local, cot[...], jnp.zeros((LANES - 2, TOK), F32)], axis=0
    ).T
    l_b[...] = jnp.broadcast_to(columns[:, 0:1], (TOK, LANES))
    c_b[...] = jnp.broadcast_to(columns[:, 1:2], (TOK, LANES))

    hid_copy.wait()

    tall = 64

    def make_features(s, _):
        at = pl.ds(pl.multiple_of(s * tall, tall), tall)
        acc = jnp.zeros((tall, LANES), F32)
        for t in range(D // LANES):
            h = hid[at, t * LANES : (t + 1) * LANES].astype(F32)
            acc = acc + h * h
        r = lax.rsqrt(jnp.sum(acc, axis=1, keepdims=True) * (1.0 / D) + EPSILON)
        r = jnp.broadcast_to(r, (tall, LANES))
        r_b[at, :] = r
        for t in range(D // LANES):
            cols = slice(t * LANES, (t + 1) * LANES)
            feats[at, cols] = ((hid[at, cols].astype(F32) * r) * gain[:, cols]).astype(BF16)
        return 0

    lax.fori_loop(0, TOK // tall, make_features, 0)

    zeros = jnp.zeros((TOK, LANES), F32)
    mx_b[...] = jnp.full((TOK, LANES), -1e30, F32)
    soft_b[...] = zeros
    hard_b[...] = zeros
    pick_b[...] = zeros

    def forward(c):
        for copy in w_copies[c * FWD // BLOCK : (c + 1) * FWD // BLOCK]:
            copy.wait()
        logits[:, c * FWD : (c + 1) * FWD] = lax.dot_general(
            feats[...], w[c * FWD : (c + 1) * FWD, :], (((1,), (1,)), ((), ())),
            preferred_element_type=F32,
        )

    def student_sums(c, s):
        at = slice(s * ROWS, (s + 1) * ROWS)
        tiles = []
        for i in range(FWD // LANES):
            start = c * FWD + i * LANES
            v = logits[at, start : start + LANES]
            if start + LANES > SHARD:
                v = jnp.where(lane < SHARD - start, v, -1e30)
                logits[at, start : start + LANES] = v
            tiles.append(v)
        top = mx_b[at, :]
        label = l_b[at, :]
        new = top
        for v in tiles:
            new = jnp.maximum(new, v)
        mx_b[at, :] = new
        scale = jnp.exp2((0.5 * LOG2E) * (top - new))
        soft = soft_b[at, :] * scale
        hard = hard_b[at, :] * (scale * scale)
        picked = pick_b[at, :]
        for i, v in enumerate(tiles):
            if i % BLOCK_TILES == 0:
                here = label - float(c * FWD + i * LANES)
            e = jnp.exp2((0.5 * LOG2E) * (v - new))
            soft = soft + e
            hard = hard + e * e
            picked = picked + jnp.where(places[i % BLOCK_TILES] == here, v, 0.0)
        soft_b[at, :] = soft
        hard_b[at, :] = hard
        pick_b[at, :] = picked

    for c in range(FWDS + 1):
        if c == 2:
            send_piece(2)
        if c > 0:
            for s in range(TOK // ROWS):
                student_sums(c - 1, s)
        if c < FWDS:
            forward(c)

    wide_lane = lax.broadcasted_iota(jnp.int32, (TOK, LANES), 1)
    top = mx_b[...]
    m = jnp.max(top, axis=1, keepdims=True)
    scale = jnp.exp2((0.5 * LOG2E) * (top - m))
    soft = jnp.sum(soft_b[...] * scale, axis=1, keepdims=True)
    hard = jnp.sum(hard_b[...] * (scale * scale), axis=1, keepdims=True)
    picked = jnp.sum(pick_b[...], axis=1, keepdims=True)
    stat = jnp.where(wide_lane == 0, m, jnp.where(wide_lane == 1, soft, hard))
    st_src[...] = jnp.where(wide_lane == 3, picked, stat).T[0:8, :]

    def send_stats(k, _):
        remote(
            st_src, st_land.at[me], ms.at[1], mr.at[1], lax.rem(me + k, N)
        ).start()
        return 0

    pltpu.make_async_copy(st_src, st_land.at[me], mr.at[1]).start()
    lax.fori_loop(1, N, send_stats, 0)
    send_piece(3)
    send_piece(4)
    wait_for(st_land, mr.at[1])

    top = st_land[0, 0:1, :]
    for s in range(1, N):
        top = jnp.maximum(top, st_land[s, 0:1, :])
    soft = jnp.zeros((1, TOK), F32)
    hard = jnp.zeros((1, TOK), F32)
    picked = jnp.zeros((1, TOK), F32)
    for s in range(N):
        stat = st_land[s]
        scale = jnp.exp2((0.5 * LOG2E) * (stat[0:1] - top))
        soft = soft + stat[1:2] * scale
        hard = hard + stat[2:3] * (scale * scale)
        picked = picked + stat[3:4]
    lse_soft = 0.5 * top + jnp.log(soft)
    rows_v[0:1, :] = lse_soft
    rows_v[1:2, :] = top + jnp.log(hard)
    rows_v[2:3, :] = picked
    columns = jnp.concatenate(
        [
            LOG2E * lse_soft,
            0.5 * cot[...] * (soft * soft) / hard,
            jnp.zeros((LANES - 2, TOK), F32),
        ],
        axis=0,
    ).T
    a_b[...] = jnp.broadcast_to(columns[:, 0:1], (TOK, LANES))
    b_b[...] = jnp.broadcast_to(columns[:, 1:2], (TOK, LANES))
    cross_b[...] = zeros
    inner_b[...] = zeros
    fg[...] = jnp.zeros((TOK, D), F32)
    wait_for(lse_land, mr.at[0])

    off = lax.rem(me * SHARD, LANES)
    shift = lax.rem(LANES - off, LANES)
    keep = lane < LANES - off
    partner = chip * 2 + (1 - core)

    def wait_piece(c):
        first, count = PIECES[c]
        wait_for(land.at[:, first * LANES : (first + count) * LANES], tr.at[c])

    def gradient(c, s, g_v):
        at = pl.ds(s * ROWS, ROWS)
        lse_s, b, ct = a_b[at, :], b_b[at, :], c_b[at, :]
        label = l_b[at, :] - jnp.float32(c * BLOCK)
        lse_t = lse_land[at, :]
        half = 0.5 * ct
        cross, inner = cross_b[at, :], inner_b[at, :]

        def turned(i):
            start = pl.multiple_of(c * BLOCK + i * LANES, LANES)
            return pltpu.roll(land[at, pl.ds(start, LANES)].astype(F32), shift, 1)

        here = turned(0)
        for i in range(BLOCK_TILES):
            after = turned(i + 1)
            x = jnp.where(keep, here, after)
            here = after
            v = logits[at, pl.ds(pl.multiple_of(c * BLOCK + i * LANES, LANES), LANES)]
            p = jnp.exp2((0.5 * LOG2E) * x - lse_t)
            e = jnp.exp2((0.5 * LOG2E) * v - lse_s)
            if i == BLOCK_TILES - 1:
                p = jnp.where(lane < SHARD - i * LANES - c * BLOCK, p, 0.0)
            cross = cross + p * (x - v)
            g = e * (ct + e * b) - ct * p
            g = g - jnp.where(places[i] == label, half, 0.0)
            g = g.astype(BF16)
            g_v[at, i * LANES : (i + 1) * LANES] = g
            inner = inner + g.astype(F32) * v
        cross_b[at, :] = cross
        inner_b[at, :] = inner

    wait_piece(0)
    for s in range(TOK // ROWS):
        gradient(0, s, g_now)

    def step(c, _):
        for p in range(1, len(PIECES)):

            @pl.when(c + 1 == FIRST_BLOCK[p])
            def _():
                wait_piece(p)

        for s in range(TOK // ROWS):
            gradient(c + 1, s, g_next)
        rows = pl.ds(pl.multiple_of(c * BLOCK, BLOCK), BLOCK)
        fg[...] += jnp.dot(g_now[...], w[rows, :], preferred_element_type=F32)
        g_now[...] = g_next[...]
        return 0

    lax.fori_loop(0, BLOCKS - 1, step, 0)

    def half_of(n, c):
        return fg[:, pl.ds(pl.multiple_of((2 * n + c) * OWN, OWN), OWN)]

    for h in range(2):
        cols = slice(h * (D // 2), (h + 1) * (D // 2))
        fg[:, cols] += jnp.dot(
            g_now[...], w[PAD - BLOCK :, cols], preferred_element_type=F32
        )
        for n in range(h * CHIPS // 2, (h + 1) * CHIPS // 2):
            cx_src[n] = half_of(n, 1 - core).astype(BF16)
            remote(cx_src.at[n], cx_land.at[n], cs.at[0], cr.at[n], partner).start()

    cross = jnp.sum(cross_b[...], axis=1, keepdims=True)
    inner = jnp.sum(inner_b[...], axis=1, keepdims=True)
    stat = jnp.where(wide_lane == 0, cross, inner)
    fin_src[...] = jnp.where(wide_lane == 2, LN2 * lse_land[...], stat).T[0:8, :]

    def send_final(k, _):
        remote(
            fin_src, fin_land.at[me], ms.at[2], mr.at[2], lax.rem(me + k, N)
        ).start()
        return 0

    pltpu.make_async_copy(fin_src, fin_land.at[me], mr.at[2]).start()
    lax.fori_loop(1, N, send_final, 0)

    def own_half(n):
        return half_of(n, core) + cx_land[n].astype(F32)

    def share(k, _):
        n = lax.rem(chip + 1 + k, CHIPS)
        wait_for(cx_land.at[n], cr.at[n])
        rs_src[n] = own_half(n).astype(BF16)
        remote(rs_src.at[n], rs_land.at[chip], rs, rr, n * 2 + core).start()
        return 0

    lax.fori_loop(0, CHIPS - 1, share, 0)
    wait_for(cx_land.at[chip], cr.at[chip])

    wait_for(fin_land, mr.at[2])
    cross = jnp.zeros((1, TOK), F32)
    inner = jnp.zeros((1, TOK), F32)
    for s in range(N):
        stat = fin_land[s]
        cross = cross + stat[0:1]
        inner = inner + stat[1:2]
    kl = 0.5 * cross - fin_src[2:3, :] + rows_v[0:1, :]
    loss[...] = 2.0 * kl + 0.5 * (rows_v[1:2, :] - rows_v[2:3, :])
    columns = jnp.concatenate(
        [inner * (1.0 / D), jnp.zeros((LANES - 1, TOK), F32)], axis=0
    ).T
    a_b[...] = jnp.broadcast_to(columns[:, 0:1], (TOK, LANES))

    wait_for(rs_land.at[0 : CHIPS - 1], rr)
    mine = pl.ds(pl.multiple_of(me * OWN, OWN), OWN)
    total = own_half(chip)
    for k in range(1, CHIPS):
        total = total + rs_land[lax.rem(chip + k, CHIPS)].astype(F32)
    r = r_b[...]
    normed = hid[:, mine].astype(F32) * r
    out[...] = (r * (gain[:, mine] * total - normed * a_b[...])).astype(BF16)

    for c, (first, count) in enumerate(PIECES):
        wait_for(land.at[0 : TOK - ROWS, first * LANES : (first + count) * LANES], ts.at[c])
    wait_for(lse_land.at[0 : TOK - ROWS], ms.at[0])
    wait_for(st_land.at[0 : N - 1], ms.at[1])
    wait_for(fin_land.at[0 : N - 1], ms.at[2])
    wait_for(cx_src, cs.at[0])
    wait_for(rs_src.at[0 : CHIPS - 1], rs)


def finish(grad, loss, grad_out, loss_out):
    grad_out[...] = grad[...]
    loss_out[...] = loss[...]


def on_device(hidden, norm_gain, head_weight, teacher, labels, cotangent):
    vmem = pl.BlockSpec(memory_space=pltpu.VMEM)
    hbm = pl.BlockSpec(memory_space=pl.ANY)
    dma = pltpu.SemaphoreType.DMA
    column = pltpu.VMEM((TOK, LANES), F32)
    grad, loss = pl.pallas_call(
        kernel,
        out_shape=(
            jax.ShapeDtypeStruct((TOK, OWN), BF16),
            jax.ShapeDtypeStruct((1, TOK), F32),
        ),
        in_specs=[hbm, vmem, hbm, hbm, vmem, vmem],
        out_specs=(vmem, vmem),
        scratch_shapes=[
            pltpu.VMEM((TOK, D), BF16),
            pltpu.VMEM((PAD, D), BF16),
            pltpu.VMEM((ROWS, VOCAB), BF16),
            pltpu.VMEM((TOK, PAD + LANES), BF16),
            pltpu.VMEM((TOK, D), BF16),
            pltpu.VMEM((TOK, PAD), F32),
            pltpu.VMEM((TOK, D), F32),
            pltpu.VMEM((TOK, BLOCK), BF16),
            pltpu.VMEM((TOK, BLOCK), BF16),
            pltpu.VMEM((ROWS, LANES), F32),
            column,
            pltpu.VMEM((8, TOK), F32),
            pltpu.VMEM((N, 8, TOK), F32),
            pltpu.VMEM((8, TOK), F32),
            pltpu.VMEM((N, 8, TOK), F32),
            pltpu.VMEM((CHIPS, TOK, OWN), BF16),
            pltpu.VMEM((CHIPS, TOK, OWN), BF16),
            pltpu.VMEM((CHIPS, TOK, OWN), BF16),
            pltpu.VMEM((CHIPS, TOK, OWN), BF16),
            column, column, column, column, column, column,
            column, column, column, column, column,
            pltpu.VMEM((8, TOK), F32),
            dma((2,)), dma((BLOCKS,)), dma((len(PIECES),)), dma((len(PIECES),)),
            dma((3,)), dma((3,)), dma((1,)), dma((CHIPS,)), dma, dma,
        ],
        compiler_params=pltpu.CompilerParams(
            collective_id=0, has_side_effects=True, vmem_limit_bytes=56 * 1024 * 1024
        ),
        cost_estimate=pl.CostEstimate(
            flops=4 * TOK * D * SHARD, bytes_accessed=20_000_000, transcendentals=3_000_000
        ),
    )(
        hidden,
        norm_gain.reshape(1, D),
        head_weight.T,
        teacher,
        labels.reshape(1, TOK),
        cotangent.reshape(1, TOK),
    )
    grad, loss = pl.pallas_call(
        finish,
        out_shape=(
            jax.ShapeDtypeStruct((TOK, OWN), BF16),
            jax.ShapeDtypeStruct((1, TOK), F32),
        ),
        in_specs=[vmem, vmem],
        out_specs=(vmem, vmem),
    )(grad, loss)
    return grad, loss.reshape(TOK)


def solution(mesh):
    return jax.shard_map(
        on_device,
        mesh=mesh,
        in_specs=(P("dp", None), P(), P(None, "vocab"), P(("dp", "vocab"), None), P("dp"), P("dp")),
        out_specs=(P("dp", "vocab"), P("dp")),
        check_vma=False,
    )
```

```python
import jax
import jax.numpy as jnp
from jax import lax
from jax.experimental import pallas as pl
from jax.experimental.pallas import tpu as pltpu
from jax.sharding import PartitionSpec as P

EPSILON = 1e-05
MESH = pl.DeviceIdType.MESH
F32 = jnp.float32
BF16 = jnp.bfloat16

N = 16
TOK = 256
ROWS = TOK // N
D = 2048
VOCAB = 64128
SHARD = VOCAB // N
LANES = 128
TILES = 32
PAD = TILES * LANES
VTILES = VOCAB // LANES
VALID = SHARD - (TILES - 1) * LANES
PIECES = ((0, 9), (9, 8), (17, 8), (25, 4), (29, 4))
FIRST_BLOCK = (0, 2, 4, 6, 7)
BLOCK = 512
BLOCKS = PAD // BLOCK
BLOCK_TILES = BLOCK // LANES
FWD = 1024
FWDS = PAD // FWD
LOG2E = 1.4426950408889634
LN2 = 0.6931471805599453
OWN = D // N
CHIPS = N // 2
FULL_W = (SHARD // 16) * 16


def kernel(
    hidden, gain, wt, teacher, labels, cot,
    out, loss,
    hid, w, t_v, land, feats, turned_feats, logits, fg, g_now, g_next,
    lse_src, lse_land, st_src, st_land, fin_src, fin_land,
    cx_src, cx_land, rs_src, rs_land,
    a_b, b_b, c_b, l_b, r_b, mx_b, soft_b, hard_b, pick_b, cross_b, inner_b, rows_v,
    loc_sem, w_sem, ts, tr, ms, mr, cs, cr, rs, rr,
):
    me = lax.axis_index("vocab")
    chip = lax.div(me, 2)
    core = lax.rem(me, 2)
    y = lax.rem(chip, 4)
    z_hi = lax.div(me, 8)
    lane = lax.broadcasted_iota(jnp.int32, (ROWS, LANES), 1)
    places = [(lane + i * LANES).astype(F32) for i in range(BLOCK_TILES)]
    my_rows = pl.ds(pl.multiple_of(me * ROWS, ROWS), ROWS)

    hid_copy = pltpu.make_async_copy(hidden, hid, loc_sem.at[0])
    hid_copy.start()
    t_copy = pltpu.make_async_copy(teacher, t_v, loc_sem.at[1])
    t_copy.start()
    w[FULL_W:PAD, :] = jnp.zeros((PAD - FULL_W, D), BF16)
    w_copies = []
    for c in range(BLOCKS):
        lo, hi = c * BLOCK, min((c + 1) * BLOCK, SHARD)
        w_copies.append(pltpu.make_async_copy(wt.at[lo:hi], w.at[lo:hi], w_sem.at[c]))
    for copy in w_copies[:2]:
        copy.start()

    barrier = pltpu.get_barrier_semaphore()

    def greet(k, _):
        pl.semaphore_signal(
            barrier, inc=1, device_id={"vocab": lax.rem(me + k, N)}, device_id_type=MESH
        )
        return 0

    lax.fori_loop(1, N, greet, 0)
    pl.semaphore_wait(barrier, N - 1)

    def remote(src, dst, send_sem, recv_sem, d):
        return pltpu.make_async_remote_copy(
            src_ref=src, dst_ref=dst, send_sem=send_sem, recv_sem=recv_sem,
            device_id={"vocab": d}, device_id_type=MESH,
        )

    def piece_copies(d, c):
        first, count = PIECES[c]
        base = lax.div(d * SHARD, LANES)
        spans = [(base + first, first, count)]
        if first + count > TILES:
            spans = [
                (base + first, first, count - 1),
                (jnp.minimum(base + TILES, VTILES - 1), TILES, 1),
            ]
        for start, at, tiles in spans:
            yield (
                teacher.at[:, pl.ds(pl.multiple_of(start * LANES, LANES), tiles * LANES)],
                land.at[my_rows, at * LANES : (at + tiles) * LANES],
            )

    def send_piece(c):
        for dc in (0, 1):
            for dy, dz in ((0, 1), (1, 0), (3, 0), (2, 1), (1, 1), (2, 0), (3, 1)):
                d = (lax.rem(z_hi + dz, 2) * 4 + lax.rem(y + dy, 4)) * 2 + lax.rem(core + dc, 2)
                for src, dst in piece_copies(d, c):
                    remote(src, dst, ts.at[c], tr.at[c], d).start()
        sibling = chip * 2 + (1 - core)
        for src, dst in piece_copies(sibling, c):
            remote(src, dst, ts.at[c], tr.at[c], sibling).start()
        for src, dst in piece_copies(me, c):
            pltpu.make_async_copy(src, dst, tr.at[c]).start()

    send_piece(0)
    for copy in w_copies[2:]:
        copy.start()

    def wait_for(ref, sem):
        pltpu.make_async_copy(ref, ref, sem).wait()

    t_copy.wait()
    wide = 33
    steps = VTILES // wide
    rest = VTILES - steps * wide

    def t_tiles(i, count):
        start = i * (wide * LANES)
        return [
            t_v[:, pl.ds(pl.multiple_of(start + t * LANES, LANES), LANES)] for t in range(count)
        ]

    def tile_max(i, accs, count=wide):
        accs = list(accs)
        for t, x in enumerate(t_tiles(i, count)):
            accs[t % 4] = jnp.maximum(accs[t % 4], x)
        return tuple(accs)

    accs = tile_max(steps, (t_v[:, :LANES],) * 4, rest)
    accs = lax.fori_loop(0, steps, tile_max, accs)
    top = jnp.maximum(jnp.maximum(accs[0], accs[1]), jnp.maximum(accs[2], accs[3]))
    top = (0.5 * LOG2E) * jnp.max(top.astype(F32), axis=1, keepdims=True)

    def tile_sum(i, accs, count=wide):
        accs = list(accs)
        for t, x in enumerate(t_tiles(i, count)):
            accs[t % 4] = accs[t % 4] + jnp.exp2((0.5 * LOG2E) * x.astype(F32) - top)
        return tuple(accs)

    accs = tile_sum(steps, (jnp.zeros((ROWS, LANES), F32),) * 4, rest)
    accs = lax.fori_loop(0, steps, tile_sum, accs)
    total = jnp.sum((accs[0] + accs[1]) + (accs[2] + accs[3]), axis=1, keepdims=True)
    lse_src[...] = jnp.broadcast_to(top + LOG2E * jnp.log(total), (ROWS, LANES))

    def send_lse(k, _):
        remote(
            lse_src, lse_land.at[my_rows, :], ms.at[0], mr.at[0], lax.rem(me + k, N)
        ).start()
        return 0

    pltpu.make_async_copy(lse_src, lse_land.at[my_rows, :], mr.at[0]).start()
    lax.fori_loop(1, N, send_lse, 0)

    send_piece(1)

    local = labels[...] - me * SHARD
    inside = jnp.logical_and(local >= 0, local < SHARD)
    local = jnp.where(inside, local, -1).astype(F32)
    columns = jnp.concatenate(
        [local, cot[...], jnp.zeros((LANES - 2, TOK), F32)], axis=0
    ).T
    l_b[...] = jnp.broadcast_to(columns[:, 0:1], (TOK, LANES))
    c_b[...] = jnp.broadcast_to(columns[:, 1:2], (TOK, LANES))

    hid_copy.wait()

    tall = 64

    def make_features(s, _):
        at = pl.ds(pl.multiple_of(s * tall, tall), tall)
        acc = jnp.zeros((tall, LANES), F32)
        for t in range(D // LANES):
            h = hid[at, t * LANES : (t + 1) * LANES].astype(F32)
            acc = acc + h * h
        r = lax.rsqrt(jnp.sum(acc, axis=1, keepdims=True) * (1.0 / D) + EPSILON)
        r = jnp.broadcast_to(r, (tall, LANES))
        r_b[at, :] = r
        for t in range(D // LANES):
            cols = slice(t * LANES, (t + 1) * LANES)
            feats[at, cols] = ((hid[at, cols].astype(F32) * r) * gain[:, cols]).astype(BF16)
        return 0

    lax.fori_loop(0, TOK // tall, make_features, 0)

    zeros = jnp.zeros((TOK, LANES), F32)
    mx_b[...] = jnp.full((TOK, LANES), -1e30, F32)
    soft_b[...] = zeros
    hard_b[...] = zeros
    pick_b[...] = zeros

    turned_feats[...] = feats[...].T

    def forward(c):
        for copy in w_copies[c * FWD // BLOCK : (c + 1) * FWD // BLOCK]:
            copy.wait()
        logits[:, c * FWD : (c + 1) * FWD] = jnp.dot(
            w[c * FWD : (c + 1) * FWD, :], turned_feats[...], preferred_element_type=F32
        ).T

    def student_sums(c, s):
        at = slice(s * ROWS, (s + 1) * ROWS)
        tiles = []
        for i in range(FWD // LANES):
            start = c * FWD + i * LANES
            v = logits[at, start : start + LANES]
            if start + LANES > SHARD:
                v = jnp.where(lane < SHARD - start, v, -1e30)
                logits[at, start : start + LANES] = v
            tiles.append(v)
        top = mx_b[at, :]
        label = l_b[at, :]
        new = top
        for v in tiles:
            new = jnp.maximum(new, v)
        mx_b[at, :] = new
        scale = jnp.exp2((0.5 * LOG2E) * (top - new))
        soft = soft_b[at, :] * scale
        hard = hard_b[at, :] * (scale * scale)
        picked = pick_b[at, :]
        for i, v in enumerate(tiles):
            if i % BLOCK_TILES == 0:
                here = label - float(c * FWD + i * LANES)
            e = jnp.exp2((0.5 * LOG2E) * (v - new))
            soft = soft + e
            hard = hard + e * e
            picked = picked + jnp.where(places[i % BLOCK_TILES] == here, v, 0.0)
        soft_b[at, :] = soft
        hard_b[at, :] = hard
        pick_b[at, :] = picked

    for c in range(FWDS + 1):
        if c > 0:
            for s in range(TOK // ROWS):
                student_sums(c - 1, s)
        if c < FWDS:
            forward(c)

    wide_lane = lax.broadcasted_iota(jnp.int32, (TOK, LANES), 1)
    top = mx_b[...]
    m = jnp.max(top, axis=1, keepdims=True)
    scale = jnp.exp2((0.5 * LOG2E) * (top - m))
    soft = jnp.sum(soft_b[...] * scale, axis=1, keepdims=True)
    hard = jnp.sum(hard_b[...] * (scale * scale), axis=1, keepdims=True)
    picked = jnp.sum(pick_b[...], axis=1, keepdims=True)
    stat = jnp.where(wide_lane == 0, m, jnp.where(wide_lane == 1, soft, hard))
    st_src[...] = jnp.where(wide_lane == 3, picked, stat).T[0:8, :]

    def send_stats(k, _):
        remote(
            st_src, st_land.at[me], ms.at[1], mr.at[1], lax.rem(me + k, N)
        ).start()
        return 0

    pltpu.make_async_copy(st_src, st_land.at[me], mr.at[1]).start()
    lax.fori_loop(1, N, send_stats, 0)
    send_piece(2)
    send_piece(3)
    send_piece(4)
    wait_for(st_land, mr.at[1])

    top = st_land[0, 0:1, :]
    for s in range(1, N):
        top = jnp.maximum(top, st_land[s, 0:1, :])
    soft = jnp.zeros((1, TOK), F32)
    hard = jnp.zeros((1, TOK), F32)
    picked = jnp.zeros((1, TOK), F32)
    for s in range(N):
        stat = st_land[s]
        scale = jnp.exp2((0.5 * LOG2E) * (stat[0:1] - top))
        soft = soft + stat[1:2] * scale
        hard = hard + stat[2:3] * (scale * scale)
        picked = picked + stat[3:4]
    lse_soft = 0.5 * top + jnp.log(soft)
    rows_v[0:1, :] = lse_soft
    rows_v[1:2, :] = top + jnp.log(hard)
    rows_v[2:3, :] = picked
    columns = jnp.concatenate(
        [
            LOG2E * lse_soft,
            0.5 * cot[...] * (soft * soft) / hard,
            jnp.zeros((LANES - 2, TOK), F32),
        ],
        axis=0,
    ).T
    a_b[...] = jnp.broadcast_to(columns[:, 0:1], (TOK, LANES))
    b_b[...] = jnp.broadcast_to(columns[:, 1:2], (TOK, LANES))
    cross_b[...] = zeros
    inner_b[...] = zeros
    fg[...] = jnp.zeros((TOK, D), F32)
    wait_for(lse_land, mr.at[0])

    off = lax.rem(me * SHARD, LANES)
    shift = lax.rem(LANES - off, LANES)
    keep = lane < LANES - off
    partner = chip * 2 + (1 - core)

    def wait_piece(c):
        first, count = PIECES[c]
        wait_for(land.at[:, first * LANES : (first + count) * LANES], tr.at[c])

    def gradient(c, s, g_v):
        at = pl.ds(s * ROWS, ROWS)
        lse_s, b, ct = a_b[at, :], b_b[at, :], c_b[at, :]
        label = l_b[at, :] - jnp.float32(c * BLOCK)
        lse_t = lse_land[at, :]
        half = 0.5 * ct
        cross, inner = cross_b[at, :], inner_b[at, :]

        def turned(i):
            start = pl.multiple_of(c * BLOCK + i * LANES, LANES)
            return pltpu.roll(land[at, pl.ds(start, LANES)].astype(F32), shift, 1)

        here = turned(0)
        for i in range(BLOCK_TILES):
            after = turned(i + 1)
            x = jnp.where(keep, here, after)
            here = after
            v = logits[at, pl.ds(pl.multiple_of(c * BLOCK + i * LANES, LANES), LANES)]
            p = jnp.exp2((0.5 * LOG2E) * x - lse_t)
            e = jnp.exp2((0.5 * LOG2E) * v - lse_s)
            if i == BLOCK_TILES - 1:
                p = jnp.where(lane < SHARD - i * LANES - c * BLOCK, p, 0.0)
            cross = cross + p * (x - v)
            g = e * (ct + e * b) - ct * p
            g = g - jnp.where(places[i] == label, half, 0.0)
            g = g.astype(BF16)
            g_v[at, i * LANES : (i + 1) * LANES] = g
            inner = inner + g.astype(F32) * v
        cross_b[at, :] = cross
        inner_b[at, :] = inner

    wait_piece(0)
    for s in range(TOK // ROWS):
        gradient(0, s, g_now)

    def step(c, _):
        for p in range(1, len(PIECES)):

            @pl.when(c + 1 == FIRST_BLOCK[p])
            def _():
                wait_piece(p)

        for s in range(TOK // ROWS):
            gradient(c + 1, s, g_next)
        rows = pl.ds(pl.multiple_of(c * BLOCK, BLOCK), BLOCK)
        fg[...] += jnp.dot(g_now[...], w[rows, :], preferred_element_type=F32)
        g_now[...] = g_next[...]
        return 0

    lax.fori_loop(0, BLOCKS - 1, step, 0)

    def half_of(n, c):
        return fg[:, pl.ds(pl.multiple_of((2 * n + c) * OWN, OWN), OWN)]

    for h in range(2):
        cols = slice(h * (D // 2), (h + 1) * (D // 2))
        fg[:, cols] += jnp.dot(
            g_now[...], w[PAD - BLOCK :, cols], preferred_element_type=F32
        )
        for n in range(h * CHIPS // 2, (h + 1) * CHIPS // 2):
            cx_src[n] = half_of(n, 1 - core).astype(BF16)
            remote(cx_src.at[n], cx_land.at[n], cs.at[0], cr.at[n], partner).start()

    cross = jnp.sum(cross_b[...], axis=1, keepdims=True)
    inner = jnp.sum(inner_b[...], axis=1, keepdims=True)
    stat = jnp.where(wide_lane == 0, cross, inner)
    fin_src[...] = jnp.where(wide_lane == 2, LN2 * lse_land[...], stat).T[0:8, :]

    def send_final(k, _):
        remote(
            fin_src, fin_land.at[me], ms.at[2], mr.at[2], lax.rem(me + k, N)
        ).start()
        return 0

    pltpu.make_async_copy(fin_src, fin_land.at[me], mr.at[2]).start()
    lax.fori_loop(1, N, send_final, 0)

    def own_half(n):
        return half_of(n, core) + cx_land[n].astype(F32)

    def share(k, _):
        n = lax.rem(chip + 1 + k, CHIPS)
        wait_for(cx_land.at[n], cr.at[n])
        rs_src[n] = own_half(n).astype(BF16)
        remote(rs_src.at[n], rs_land.at[chip], rs, rr, n * 2 + core).start()
        return 0

    lax.fori_loop(0, CHIPS - 1, share, 0)
    wait_for(cx_land.at[chip], cr.at[chip])

    wait_for(fin_land, mr.at[2])
    cross = jnp.zeros((1, TOK), F32)
    inner = jnp.zeros((1, TOK), F32)
    for s in range(N):
        stat = fin_land[s]
        cross = cross + stat[0:1]
        inner = inner + stat[1:2]
    kl = 0.5 * cross - fin_src[2:3, :] + rows_v[0:1, :]
    loss[...] = 2.0 * kl + 0.5 * (rows_v[1:2, :] - rows_v[2:3, :])
    columns = jnp.concatenate(
        [inner * (1.0 / D), jnp.zeros((LANES - 1, TOK), F32)], axis=0
    ).T
    a_b[...] = jnp.broadcast_to(columns[:, 0:1], (TOK, LANES))

    wait_for(rs_land.at[0 : CHIPS - 1], rr)
    mine = pl.ds(pl.multiple_of(me * OWN, OWN), OWN)
    total = own_half(chip)
    for k in range(1, CHIPS):
        total = total + rs_land[lax.rem(chip + k, CHIPS)].astype(F32)
    r = r_b[...]
    normed = hid[:, mine].astype(F32) * r
    out[...] = (r * (gain[:, mine] * total - normed * a_b[...])).astype(BF16)

    for c, (first, count) in enumerate(PIECES):
        wait_for(land.at[0 : TOK - ROWS, first * LANES : (first + count) * LANES], ts.at[c])
    wait_for(lse_land.at[0 : TOK - ROWS], ms.at[0])
    wait_for(st_land.at[0 : N - 1], ms.at[1])
    wait_for(fin_land.at[0 : N - 1], ms.at[2])
    wait_for(cx_src, cs.at[0])
    wait_for(rs_src.at[0 : CHIPS - 1], rs)


def finish(grad, loss, grad_out, loss_out):
    grad_out[...] = grad[...]
    loss_out[...] = loss[...]


def on_device(hidden, norm_gain, head_weight, teacher, labels, cotangent):
    vmem = pl.BlockSpec(memory_space=pltpu.VMEM)
    hbm = pl.BlockSpec(memory_space=pl.ANY)
    dma = pltpu.SemaphoreType.DMA
    column = pltpu.VMEM((TOK, LANES), F32)
    grad, loss = pl.pallas_call(
        kernel,
        out_shape=(
            jax.ShapeDtypeStruct((TOK, OWN), BF16),
            jax.ShapeDtypeStruct((1, TOK), F32),
        ),
        in_specs=[hbm, vmem, hbm, hbm, vmem, vmem],
        out_specs=(vmem, vmem),
        scratch_shapes=[
            pltpu.VMEM((TOK, D), BF16),
            pltpu.VMEM((PAD, D), BF16),
            pltpu.VMEM((ROWS, VOCAB), BF16),
            pltpu.VMEM((TOK, PAD + LANES), BF16),
            pltpu.VMEM((TOK, D), BF16),
            pltpu.VMEM((D, TOK), BF16),
            pltpu.VMEM((TOK, PAD), F32),
            pltpu.VMEM((TOK, D), F32),
            pltpu.VMEM((TOK, BLOCK), BF16),
            pltpu.VMEM((TOK, BLOCK), BF16),
            pltpu.VMEM((ROWS, LANES), F32),
            column,
            pltpu.VMEM((8, TOK), F32),
            pltpu.VMEM((N, 8, TOK), F32),
            pltpu.VMEM((8, TOK), F32),
            pltpu.VMEM((N, 8, TOK), F32),
            pltpu.VMEM((CHIPS, TOK, OWN), BF16),
            pltpu.VMEM((CHIPS, TOK, OWN), BF16),
            pltpu.VMEM((CHIPS, TOK, OWN), BF16),
            pltpu.VMEM((CHIPS, TOK, OWN), BF16),
            column, column, column, column, column, column,
            column, column, column, column, column,
            pltpu.VMEM((8, TOK), F32),
            dma((2,)), dma((BLOCKS,)), dma((len(PIECES),)), dma((len(PIECES),)),
            dma((3,)), dma((3,)), dma((1,)), dma((CHIPS,)), dma, dma,
        ],
        compiler_params=pltpu.CompilerParams(
            collective_id=0, has_side_effects=True, vmem_limit_bytes=56 * 1024 * 1024
        ),
        cost_estimate=pl.CostEstimate(
            flops=4 * TOK * D * SHARD, bytes_accessed=20_000_000, transcendentals=3_000_000
        ),
    )(
        hidden,
        norm_gain.reshape(1, D),
        head_weight.T,
        teacher,
        labels.reshape(1, TOK),
        cotangent.reshape(1, TOK),
    )
    grad, loss = pl.pallas_call(
        finish,
        out_shape=(
            jax.ShapeDtypeStruct((TOK, OWN), BF16),
            jax.ShapeDtypeStruct((1, TOK), F32),
        ),
        in_specs=[vmem, vmem],
        out_specs=(vmem, vmem),
    )(grad, loss)
    return grad, loss.reshape(TOK)


def solution(mesh):
    return jax.shard_map(
        on_device,
        mesh=mesh,
        in_specs=(P("dp", None), P(), P(None, "vocab"), P(("dp", "vocab"), None), P("dp"), P("dp")),
        out_specs=(P("dp", "vocab"), P("dp")),
        check_vma=False,
    )
```

```python
import jax
import jax.numpy as jnp
from jax import lax
from jax.experimental import pallas as pl
from jax.experimental.pallas import tpu as pltpu
from jax.sharding import PartitionSpec as P

EPSILON = 1e-05
MESH = pl.DeviceIdType.MESH
F32 = jnp.float32
BF16 = jnp.bfloat16

N = 16
TOK = 256
ROWS = TOK // N
D = 2048
VOCAB = 64128
SHARD = VOCAB // N
LANES = 128
TILES = 32
PAD = TILES * LANES
VTILES = VOCAB // LANES
MOST = TILES + 1
VALID = SHARD - (TILES - 1) * LANES
PIECES = ((0, 10), (10, 8), (18, 8), (26, 7))
FIRST_BLOCK = (0, 2, 4, 6)
BLOCK = 512
BLOCKS = PAD // BLOCK
BLOCK_TILES = BLOCK // LANES
FWD = 1024
FWDS = PAD // FWD
LOG2E = 1.4426950408889634
LN2 = 0.6931471805599453
OWN = D // N
CHIPS = N // 2
FULL_W = (SHARD // 16) * 16


def kernel(
    hidden, gain, wt, teacher, labels, cot,
    out, loss,
    hid, w, t_v, land, feats, logits, fg, g_now, g_next,
    lse_src, lse_land, st_src, st_land, fin_src, fin_land,
    cx_src, cx_land, rs_src, rs_land,
    a_b, b_b, c_b, l_b, r_b, mx_b, soft_b, hard_b, pick_b, cross_b, inner_b, rows_v,
    loc_sem, w_sem, ts, tr, ms, mr, cs, cr, rs, rr,
):
    me = lax.axis_index("vocab")
    chip = lax.div(me, 2)
    core = lax.rem(me, 2)
    y = lax.rem(chip, 4)
    z_hi = lax.div(me, 8)
    lane = lax.broadcasted_iota(jnp.int32, (ROWS, LANES), 1)
    places = [(lane + i * LANES).astype(F32) for i in range(BLOCK_TILES)]
    my_rows = pl.ds(pl.multiple_of(me * ROWS, ROWS), ROWS)

    hid_copy = pltpu.make_async_copy(hidden, hid, loc_sem.at[0])
    hid_copy.start()
    t_copy = pltpu.make_async_copy(teacher, t_v, loc_sem.at[1])
    t_copy.start()
    w[FULL_W:PAD, :] = jnp.zeros((PAD - FULL_W, D), BF16)
    w_copies = []
    for c in range(BLOCKS):
        lo, hi = c * BLOCK, min((c + 1) * BLOCK, SHARD)
        w_copies.append(pltpu.make_async_copy(wt.at[lo:hi], w.at[lo:hi], w_sem.at[c]))
    for copy in w_copies[:2]:
        copy.start()

    barrier = pltpu.get_barrier_semaphore()

    def greet(k, _):
        pl.semaphore_signal(
            barrier, inc=1, device_id={"vocab": lax.rem(me + k, N)}, device_id_type=MESH
        )
        return 0

    lax.fori_loop(1, N, greet, 0)
    pl.semaphore_wait(barrier, N - 1)

    def remote(src, dst, send_sem, recv_sem, d):
        return pltpu.make_async_remote_copy(
            src_ref=src, dst_ref=dst, send_sem=send_sem, recv_sem=recv_sem,
            device_id={"vocab": d}, device_id_type=MESH,
        )

    def first_tile(d):
        return jnp.minimum(lax.div(d * SHARD, LANES), VTILES - MOST)

    def piece_refs(d, c):
        first, count = PIECES[c]
        start = pl.multiple_of((first_tile(d) + first) * LANES, LANES)
        return (
            teacher.at[:, pl.ds(start, count * LANES)],
            land.at[my_rows, first * LANES : (first + count) * LANES],
        )

    def send_piece(c):
        for dc in (0, 1):
            for dy, dz in ((0, 1), (1, 0), (3, 0), (2, 1), (1, 1), (2, 0), (3, 1)):
                d = (lax.rem(z_hi + dz, 2) * 4 + lax.rem(y + dy, 4)) * 2 + lax.rem(core + dc, 2)
                src, dst = piece_refs(d, c)
                remote(src, dst, ts.at[c], tr.at[c], d).start()
        sibling = chip * 2 + (1 - core)
        src, dst = piece_refs(sibling, c)
        remote(src, dst, ts.at[c], tr.at[c], sibling).start()
        src, dst = piece_refs(me, c)
        pltpu.make_async_copy(src, dst, tr.at[c]).start()

    send_piece(0)
    for copy in w_copies[2:]:
        copy.start()

    def wait_for(ref, sem):
        pltpu.make_async_copy(ref, ref, sem).wait()

    t_copy.wait()
    wide = 33
    steps = VTILES // wide
    rest = VTILES - steps * wide

    def t_tiles(i, count):
        start = i * (wide * LANES)
        return [
            t_v[:, pl.ds(pl.multiple_of(start + t * LANES, LANES), LANES)] for t in range(count)
        ]

    def tile_max(i, accs, count=wide):
        accs = list(accs)
        for t, x in enumerate(t_tiles(i, count)):
            accs[t % 4] = jnp.maximum(accs[t % 4], x)
        return tuple(accs)

    accs = tile_max(steps, (t_v[:, :LANES],) * 4, rest)
    accs = lax.fori_loop(0, steps, tile_max, accs)
    top = jnp.maximum(jnp.maximum(accs[0], accs[1]), jnp.maximum(accs[2], accs[3]))
    top = (0.5 * LOG2E) * jnp.max(top.astype(F32), axis=1, keepdims=True)

    def tile_sum(i, accs, count=wide):
        accs = list(accs)
        for t, x in enumerate(t_tiles(i, count)):
            accs[t % 4] = accs[t % 4] + jnp.exp2((0.5 * LOG2E) * x.astype(F32) - top)
        return tuple(accs)

    accs = tile_sum(steps, (jnp.zeros((ROWS, LANES), F32),) * 4, rest)
    accs = lax.fori_loop(0, steps, tile_sum, accs)
    total = jnp.sum((accs[0] + accs[1]) + (accs[2] + accs[3]), axis=1, keepdims=True)
    lse_src[...] = jnp.broadcast_to(top + LOG2E * jnp.log(total), (ROWS, LANES))

    def send_lse(k, _):
        remote(
            lse_src, lse_land.at[my_rows, :], ms.at[0], mr.at[0], lax.rem(me + k, N)
        ).start()
        return 0

    pltpu.make_async_copy(lse_src, lse_land.at[my_rows, :], mr.at[0]).start()
    lax.fori_loop(1, N, send_lse, 0)

    send_piece(1)

    local = labels[...] - me * SHARD
    inside = jnp.logical_and(local >= 0, local < SHARD)
    local = jnp.where(inside, local, -1).astype(F32)
    columns = jnp.concatenate(
        [local, cot[...], jnp.zeros((LANES - 2, TOK), F32)], axis=0
    ).T
    l_b[...] = jnp.broadcast_to(columns[:, 0:1], (TOK, LANES))
    c_b[...] = jnp.broadcast_to(columns[:, 1:2], (TOK, LANES))

    hid_copy.wait()

    tall = 64

    def make_features(s, _):
        at = pl.ds(pl.multiple_of(s * tall, tall), tall)
        acc = jnp.zeros((tall, LANES), F32)
        for t in range(D // LANES):
            h = hid[at, t * LANES : (t + 1) * LANES].astype(F32)
            acc = acc + h * h
        r = lax.rsqrt(jnp.sum(acc, axis=1, keepdims=True) * (1.0 / D) + EPSILON)
        r = jnp.broadcast_to(r, (tall, LANES))
        r_b[at, :] = r
        for t in range(D // LANES):
            cols = slice(t * LANES, (t + 1) * LANES)
            feats[at, cols] = ((hid[at, cols].astype(F32) * r) * gain[:, cols]).astype(BF16)
        return 0

    lax.fori_loop(0, TOK // tall, make_features, 0)

    zeros = jnp.zeros((TOK, LANES), F32)
    mx_b[...] = jnp.full((TOK, LANES), -1e30, F32)
    soft_b[...] = zeros
    hard_b[...] = zeros
    pick_b[...] = zeros

    def forward(c):
        for copy in w_copies[c * FWD // BLOCK : (c + 1) * FWD // BLOCK]:
            copy.wait()
        logits[:, c * FWD : (c + 1) * FWD] = lax.dot_general(
            feats[...], w[c * FWD : (c + 1) * FWD, :], (((1,), (1,)), ((), ())),
            preferred_element_type=F32,
        )

    def student_sums(c, s):
        at = slice(s * ROWS, (s + 1) * ROWS)
        tiles = []
        for i in range(FWD // LANES):
            start = c * FWD + i * LANES
            v = logits[at, start : start + LANES]
            if start + LANES > SHARD:
                v = jnp.where(lane < SHARD - start, v, -1e30)
                logits[at, start : start + LANES] = v
            tiles.append(v)
        top = mx_b[at, :]
        label = l_b[at, :]
        new = top
        for v in tiles:
            new = jnp.maximum(new, v)
        mx_b[at, :] = new
        scale = jnp.exp2((0.5 * LOG2E) * (top - new))
        soft = soft_b[at, :] * scale
        hard = hard_b[at, :] * (scale * scale)
        picked = pick_b[at, :]
        for i, v in enumerate(tiles):
            if i % BLOCK_TILES == 0:
                here = label - float(c * FWD + i * LANES)
            e = jnp.exp2((0.5 * LOG2E) * (v - new))
            soft = soft + e
            hard = hard + e * e
            picked = picked + jnp.where(places[i % BLOCK_TILES] == here, v, 0.0)
        soft_b[at, :] = soft
        hard_b[at, :] = hard
        pick_b[at, :] = picked

    for c in range(FWDS + 1):
        if c > 0:
            for s in range(TOK // ROWS):
                student_sums(c - 1, s)
        if c < FWDS:
            forward(c)

    wide_lane = lax.broadcasted_iota(jnp.int32, (TOK, LANES), 1)
    top = mx_b[...]
    m = jnp.max(top, axis=1, keepdims=True)
    scale = jnp.exp2((0.5 * LOG2E) * (top - m))
    soft = jnp.sum(soft_b[...] * scale, axis=1, keepdims=True)
    hard = jnp.sum(hard_b[...] * (scale * scale), axis=1, keepdims=True)
    picked = jnp.sum(pick_b[...], axis=1, keepdims=True)
    stat = jnp.where(wide_lane == 0, m, jnp.where(wide_lane == 1, soft, hard))
    st_src[...] = jnp.where(wide_lane == 3, picked, stat).T[0:8, :]

    def send_stats(k, _):
        remote(
            st_src, st_land.at[me], ms.at[1], mr.at[1], lax.rem(me + k, N)
        ).start()
        return 0

    pltpu.make_async_copy(st_src, st_land.at[me], mr.at[1]).start()
    lax.fori_loop(1, N, send_stats, 0)
    send_piece(2)
    wait_for(st_land, mr.at[1])
    send_piece(3)

    top = st_land[0, 0:1, :]
    for s in range(1, N):
        top = jnp.maximum(top, st_land[s, 0:1, :])
    soft = jnp.zeros((1, TOK), F32)
    hard = jnp.zeros((1, TOK), F32)
    picked = jnp.zeros((1, TOK), F32)
    for s in range(N):
        stat = st_land[s]
        scale = jnp.exp2((0.5 * LOG2E) * (stat[0:1] - top))
        soft = soft + stat[1:2] * scale
        hard = hard + stat[2:3] * (scale * scale)
        picked = picked + stat[3:4]
    lse_soft = 0.5 * top + jnp.log(soft)
    rows_v[0:1, :] = lse_soft
    rows_v[1:2, :] = top + jnp.log(hard)
    rows_v[2:3, :] = picked
    columns = jnp.concatenate(
        [
            LOG2E * lse_soft,
            0.5 * cot[...] * (soft * soft) / hard,
            jnp.zeros((LANES - 2, TOK), F32),
        ],
        axis=0,
    ).T
    a_b[...] = jnp.broadcast_to(columns[:, 0:1], (TOK, LANES))
    b_b[...] = jnp.broadcast_to(columns[:, 1:2], (TOK, LANES))
    cross_b[...] = zeros
    inner_b[...] = zeros
    fg[...] = jnp.zeros((TOK, D), F32)
    wait_for(lse_land, mr.at[0])

    off = lax.rem(me * SHARD, LANES)
    shift = lax.rem(LANES - off, LANES)
    keep = lane < LANES - off
    skip = lax.div(me * SHARD, LANES) - first_tile(me)
    partner = chip * 2 + (1 - core)

    def wait_piece(c):
        first, count = PIECES[c]
        wait_for(land.at[:, first * LANES : (first + count) * LANES], tr.at[c])

    def gradient(c, s, g_v):
        at = pl.ds(s * ROWS, ROWS)
        lse_s, b, ct = a_b[at, :], b_b[at, :], c_b[at, :]
        label = l_b[at, :] - jnp.float32(c * BLOCK)
        lse_t = lse_land[at, :]
        half = 0.5 * ct
        cross, inner = cross_b[at, :], inner_b[at, :]

        def turned(i):
            tile = jnp.minimum(c * BLOCK_TILES + i + skip, MOST - 1)
            start = pl.multiple_of(tile * LANES, LANES)
            return pltpu.roll(land[at, pl.ds(start, LANES)].astype(F32), shift, 1)

        here = turned(0)
        for i in range(BLOCK_TILES):
            after = turned(i + 1)
            x = jnp.where(keep, here, after)
            here = after
            v = logits[at, pl.ds(pl.multiple_of(c * BLOCK + i * LANES, LANES), LANES)]
            p = jnp.exp2((0.5 * LOG2E) * x - lse_t)
            e = jnp.exp2((0.5 * LOG2E) * v - lse_s)
            if i == BLOCK_TILES - 1:
                p = jnp.where(lane < SHARD - i * LANES - c * BLOCK, p, 0.0)
            cross = cross + p * (x - v)
            g = e * (ct + e * b) - ct * p
            g = g - jnp.where(places[i] == label, half, 0.0)
            g = g.astype(BF16)
            g_v[at, i * LANES : (i + 1) * LANES] = g
            inner = inner + g.astype(F32) * v
        cross_b[at, :] = cross
        inner_b[at, :] = inner

    wait_piece(0)
    for s in range(TOK // ROWS):
        gradient(0, s, g_now)

    def step(c, _):
        for p in range(1, len(PIECES)):

            @pl.when(c + 1 == FIRST_BLOCK[p])
            def _():
                wait_piece(p)

        for s in range(TOK // ROWS):
            gradient(c + 1, s, g_next)
        rows = pl.ds(pl.multiple_of(c * BLOCK, BLOCK), BLOCK)
        fg[...] += jnp.dot(g_now[...], w[rows, :], preferred_element_type=F32)
        g_now[...] = g_next[...]
        return 0

    lax.fori_loop(0, BLOCKS - 1, step, 0)

    def half_of(n, c):
        return fg[:, pl.ds(pl.multiple_of((2 * n + c) * OWN, OWN), OWN)]

    for h in range(2):
        cols = slice(h * (D // 2), (h + 1) * (D // 2))
        fg[:, cols] += jnp.dot(
            g_now[...], w[PAD - BLOCK :, cols], preferred_element_type=F32
        )
        for n in range(h * CHIPS // 2, (h + 1) * CHIPS // 2):
            cx_src[n] = half_of(n, 1 - core).astype(BF16)
            remote(cx_src.at[n], cx_land.at[n], cs.at[0], cr.at[n], partner).start()

    cross = jnp.sum(cross_b[...], axis=1, keepdims=True)
    inner = jnp.sum(inner_b[...], axis=1, keepdims=True)
    stat = jnp.where(wide_lane == 0, cross, inner)
    fin_src[...] = jnp.where(wide_lane == 2, LN2 * lse_land[...], stat).T[0:8, :]

    def send_final(k, _):
        remote(
            fin_src, fin_land.at[me], ms.at[2], mr.at[2], lax.rem(me + k, N)
        ).start()
        return 0

    pltpu.make_async_copy(fin_src, fin_land.at[me], mr.at[2]).start()
    lax.fori_loop(1, N, send_final, 0)

    def own_half(n):
        return half_of(n, core) + cx_land[n].astype(F32)

    def share(k, _):
        n = lax.rem(chip + 1 + k, CHIPS)
        wait_for(cx_land.at[n], cr.at[n])
        rs_src[n] = own_half(n).astype(BF16)
        remote(rs_src.at[n], rs_land.at[chip], rs, rr, n * 2 + core).start()
        return 0

    lax.fori_loop(0, CHIPS - 1, share, 0)
    wait_for(cx_land.at[chip], cr.at[chip])

    wait_for(fin_land, mr.at[2])
    cross = jnp.zeros((1, TOK), F32)
    inner = jnp.zeros((1, TOK), F32)
    for s in range(N):
        stat = fin_land[s]
        cross = cross + stat[0:1]
        inner = inner + stat[1:2]
    kl = 0.5 * cross - fin_src[2:3, :] + rows_v[0:1, :]
    loss[...] = 2.0 * kl + 0.5 * (rows_v[1:2, :] - rows_v[2:3, :])
    columns = jnp.concatenate(
        [inner * (1.0 / D), jnp.zeros((LANES - 1, TOK), F32)], axis=0
    ).T
    a_b[...] = jnp.broadcast_to(columns[:, 0:1], (TOK, LANES))

    wait_for(rs_land.at[0 : CHIPS - 1], rr)
    mine = pl.ds(pl.multiple_of(me * OWN, OWN), OWN)
    total = own_half(chip)
    for k in range(1, CHIPS):
        total = total + rs_land[lax.rem(chip + k, CHIPS)].astype(F32)
    r = r_b[...]
    normed = hid[:, mine].astype(F32) * r
    out[...] = (r * (gain[:, mine] * total - normed * a_b[...])).astype(BF16)

    for c, (first, count) in enumerate(PIECES):
        wait_for(land.at[0 : TOK - ROWS, first * LANES : (first + count) * LANES], ts.at[c])
    wait_for(lse_land.at[0 : TOK - ROWS], ms.at[0])
    wait_for(st_land.at[0 : N - 1], ms.at[1])
    wait_for(fin_land.at[0 : N - 1], ms.at[2])
    wait_for(cx_src, cs.at[0])
    wait_for(rs_src.at[0 : CHIPS - 1], rs)


def finish(grad, loss, grad_out, loss_out):
    grad_out[...] = grad[...]
    loss_out[...] = loss[...]


def on_device(hidden, norm_gain, head_weight, teacher, labels, cotangent):
    vmem = pl.BlockSpec(memory_space=pltpu.VMEM)
    hbm = pl.BlockSpec(memory_space=pl.ANY)
    dma = pltpu.SemaphoreType.DMA
    column = pltpu.VMEM((TOK, LANES), F32)
    grad, loss = pl.pallas_call(
        kernel,
        out_shape=(
            jax.ShapeDtypeStruct((TOK, OWN), BF16),
            jax.ShapeDtypeStruct((1, TOK), F32),
        ),
        in_specs=[hbm, vmem, hbm, hbm, vmem, vmem],
        out_specs=(vmem, vmem),
        scratch_shapes=[
            pltpu.VMEM((TOK, D), BF16),
            pltpu.VMEM((PAD, D), BF16),
            pltpu.VMEM((ROWS, VOCAB), BF16),
            pltpu.VMEM((TOK, PAD + LANES), BF16),
            pltpu.VMEM((TOK, D), BF16),
            pltpu.VMEM((TOK, PAD), F32),
            pltpu.VMEM((TOK, D), F32),
            pltpu.VMEM((TOK, BLOCK), BF16),
            pltpu.VMEM((TOK, BLOCK), BF16),
            pltpu.VMEM((ROWS, LANES), F32),
            column,
            pltpu.VMEM((8, TOK), F32),
            pltpu.VMEM((N, 8, TOK), F32),
            pltpu.VMEM((8, TOK), F32),
            pltpu.VMEM((N, 8, TOK), F32),
            pltpu.VMEM((CHIPS, TOK, OWN), BF16),
            pltpu.VMEM((CHIPS, TOK, OWN), BF16),
            pltpu.VMEM((CHIPS, TOK, OWN), BF16),
            pltpu.VMEM((CHIPS, TOK, OWN), BF16),
            column, column, column, column, column, column,
            column, column, column, column, column,
            pltpu.VMEM((8, TOK), F32),
            dma((2,)), dma((BLOCKS,)), dma((len(PIECES),)), dma((len(PIECES),)),
            dma((3,)), dma((3,)), dma((1,)), dma((CHIPS,)), dma, dma,
        ],
        compiler_params=pltpu.CompilerParams(
            collective_id=0, has_side_effects=True, vmem_limit_bytes=56 * 1024 * 1024
        ),
        cost_estimate=pl.CostEstimate(
            flops=4 * TOK * D * SHARD, bytes_accessed=20_000_000, transcendentals=3_000_000
        ),
    )(
        hidden,
        norm_gain.reshape(1, D),
        head_weight.T,
        teacher,
        labels.reshape(1, TOK),
        cotangent.reshape(1, TOK),
    )
    grad, loss = pl.pallas_call(
        finish,
        out_shape=(
            jax.ShapeDtypeStruct((TOK, OWN), BF16),
            jax.ShapeDtypeStruct((1, TOK), F32),
        ),
        in_specs=[vmem, vmem],
        out_specs=(vmem, vmem),
    )(grad, loss)
    return grad, loss.reshape(TOK)


def solution(mesh):
    return jax.shard_map(
        on_device,
        mesh=mesh,
        in_specs=(P("dp", None), P(), P(None, "vocab"), P(("dp", "vocab"), None), P("dp"), P("dp")),
        out_specs=(P("dp", "vocab"), P("dp")),
        check_vma=False,
    )
```

```python
import jax
import jax.numpy as jnp
from jax import lax
from jax.experimental import pallas as pl
from jax.experimental.pallas import tpu as pltpu
from jax.sharding import PartitionSpec as P

EPSILON = 1e-05
MESH = pl.DeviceIdType.MESH
F32 = jnp.float32
BF16 = jnp.bfloat16

N = 16
TOK = 256
ROWS = TOK // N
D = 2048
VOCAB = 64128
SHARD = VOCAB // N
LANES = 128
TILES = 32
PAD = TILES * LANES
VTILES = VOCAB // LANES
MOST = TILES + 1
VALID = SHARD - (TILES - 1) * LANES
PIECES = ((0, 10), (10, 8), (18, 8), (26, 4), (30, 3))
FIRST_BLOCK = (0, 2, 4, 6, 7)
BLOCK = 512
BLOCKS = PAD // BLOCK
BLOCK_TILES = BLOCK // LANES
FWD = 1024
FWDS = PAD // FWD
LOG2E = 1.4426950408889634
LN2 = 0.6931471805599453
OWN = D // N
CHIPS = N // 2
FULL_W = (SHARD // 16) * 16


def kernel(
    hidden, gain, wt, teacher, labels, cot,
    out, loss,
    hid, w, t_v, land, feats, logits, fg, g_now, g_next,
    lse_src, lse_land, st_src, st_land, fin_src, fin_land,
    cx_src, cx_land, rs_src, rs_land,
    a_b, b_b, c_b, l_b, r_b, mx_b, soft_b, hard_b, pick_b, cross_b, inner_b, rows_v,
    loc_sem, w_sem, ts, tr, ms, mr, cs, cr, rs, rr,
):
    me = lax.axis_index("vocab")
    chip = lax.div(me, 2)
    core = lax.rem(me, 2)
    y = lax.rem(chip, 4)
    z_hi = lax.div(me, 8)
    lane = lax.broadcasted_iota(jnp.int32, (ROWS, LANES), 1)
    places = [(lane + i * LANES).astype(F32) for i in range(BLOCK_TILES)]
    my_rows = pl.ds(pl.multiple_of(me * ROWS, ROWS), ROWS)

    hid_copy = pltpu.make_async_copy(hidden, hid, loc_sem.at[0])
    hid_copy.start()
    t_copy = pltpu.make_async_copy(teacher, t_v, loc_sem.at[1])
    t_copy.start()
    w[FULL_W:PAD, :] = jnp.zeros((PAD - FULL_W, D), BF16)
    w_copies = []
    for c in range(BLOCKS):
        lo, hi = c * BLOCK, min((c + 1) * BLOCK, SHARD)
        w_copies.append(pltpu.make_async_copy(wt.at[lo:hi], w.at[lo:hi], w_sem.at[c]))
    for copy in w_copies[:2]:
        copy.start()

    barrier = pltpu.get_barrier_semaphore()

    def greet(k, _):
        pl.semaphore_signal(
            barrier, inc=1, device_id={"vocab": lax.rem(me + k, N)}, device_id_type=MESH
        )
        return 0

    lax.fori_loop(1, N, greet, 0)
    pl.semaphore_wait(barrier, N - 1)

    def remote(src, dst, send_sem, recv_sem, d):
        return pltpu.make_async_remote_copy(
            src_ref=src, dst_ref=dst, send_sem=send_sem, recv_sem=recv_sem,
            device_id={"vocab": d}, device_id_type=MESH,
        )

    def first_tile(d):
        return jnp.minimum(lax.div(d * SHARD, LANES), VTILES - MOST)

    def piece_refs(d, c):
        first, count = PIECES[c]
        start = pl.multiple_of((first_tile(d) + first) * LANES, LANES)
        return (
            teacher.at[:, pl.ds(start, count * LANES)],
            land.at[my_rows, first * LANES : (first + count) * LANES],
        )

    def send_piece(c):
        for dc in (0, 1):
            for dy, dz in ((0, 1), (1, 0), (3, 0), (2, 1), (1, 1), (2, 0), (3, 1)):
                d = (lax.rem(z_hi + dz, 2) * 4 + lax.rem(y + dy, 4)) * 2 + lax.rem(core + dc, 2)
                src, dst = piece_refs(d, c)
                remote(src, dst, ts.at[c], tr.at[c], d).start()
        sibling = chip * 2 + (1 - core)
        src, dst = piece_refs(sibling, c)
        remote(src, dst, ts.at[c], tr.at[c], sibling).start()
        src, dst = piece_refs(me, c)
        pltpu.make_async_copy(src, dst, tr.at[c]).start()

    send_piece(0)
    for copy in w_copies[2:]:
        copy.start()

    def wait_for(ref, sem):
        pltpu.make_async_copy(ref, ref, sem).wait()

    t_copy.wait()
    wide = 33
    steps = VTILES // wide
    rest = VTILES - steps * wide

    def t_tiles(i, count):
        start = i * (wide * LANES)
        return [
            t_v[:, pl.ds(pl.multiple_of(start + t * LANES, LANES), LANES)] for t in range(count)
        ]

    def tile_max(i, accs, count=wide):
        accs = list(accs)
        for t, x in enumerate(t_tiles(i, count)):
            accs[t % 4] = jnp.maximum(accs[t % 4], x)
        return tuple(accs)

    accs = tile_max(steps, (t_v[:, :LANES],) * 4, rest)
    accs = lax.fori_loop(0, steps, tile_max, accs)
    top = jnp.maximum(jnp.maximum(accs[0], accs[1]), jnp.maximum(accs[2], accs[3]))
    top = (0.5 * LOG2E) * jnp.max(top.astype(F32), axis=1, keepdims=True)

    def tile_sum(i, accs, count=wide):
        accs = list(accs)
        for t, x in enumerate(t_tiles(i, count)):
            accs[t % 4] = accs[t % 4] + jnp.exp2((0.5 * LOG2E) * x.astype(F32) - top)
        return tuple(accs)

    accs = tile_sum(steps, (jnp.zeros((ROWS, LANES), F32),) * 4, rest)
    accs = lax.fori_loop(0, steps, tile_sum, accs)
    total = jnp.sum((accs[0] + accs[1]) + (accs[2] + accs[3]), axis=1, keepdims=True)
    lse_src[...] = jnp.broadcast_to(top + LOG2E * jnp.log(total), (ROWS, LANES))

    def send_lse(k, _):
        remote(
            lse_src, lse_land.at[my_rows, :], ms.at[0], mr.at[0], lax.rem(me + k, N)
        ).start()
        return 0

    pltpu.make_async_copy(lse_src, lse_land.at[my_rows, :], mr.at[0]).start()
    lax.fori_loop(1, N, send_lse, 0)

    send_piece(1)

    local = labels[...] - me * SHARD
    inside = jnp.logical_and(local >= 0, local < SHARD)
    local = jnp.where(inside, local, -1).astype(F32)
    columns = jnp.concatenate(
        [local, cot[...], jnp.zeros((LANES - 2, TOK), F32)], axis=0
    ).T
    l_b[...] = jnp.broadcast_to(columns[:, 0:1], (TOK, LANES))
    c_b[...] = jnp.broadcast_to(columns[:, 1:2], (TOK, LANES))

    hid_copy.wait()

    tall = 64

    def make_features(s, _):
        at = pl.ds(pl.multiple_of(s * tall, tall), tall)
        acc = jnp.zeros((tall, LANES), F32)
        for t in range(D // LANES):
            h = hid[at, t * LANES : (t + 1) * LANES].astype(F32)
            acc = acc + h * h
        r = lax.rsqrt(jnp.sum(acc, axis=1, keepdims=True) * (1.0 / D) + EPSILON)
        r = jnp.broadcast_to(r, (tall, LANES))
        r_b[at, :] = r
        for t in range(D // LANES):
            cols = slice(t * LANES, (t + 1) * LANES)
            feats[at, cols] = ((hid[at, cols].astype(F32) * r) * gain[:, cols]).astype(BF16)
        return 0

    lax.fori_loop(0, TOK // tall, make_features, 0)

    zeros = jnp.zeros((TOK, LANES), F32)
    mx_b[...] = jnp.full((TOK, LANES), -1e30, F32)
    soft_b[...] = zeros
    hard_b[...] = zeros
    pick_b[...] = zeros

    def forward(c):
        for copy in w_copies[c * FWD // BLOCK : (c + 1) * FWD // BLOCK]:
            copy.wait()
        logits[:, c * FWD : (c + 1) * FWD] = lax.dot_general(
            feats[...], w[c * FWD : (c + 1) * FWD, :], (((1,), (1,)), ((), ())),
            preferred_element_type=F32,
        )

    def student_sums(c, s):
        at = slice(s * ROWS, (s + 1) * ROWS)
        tiles = []
        for i in range(FWD // LANES):
            start = c * FWD + i * LANES
            v = logits[at, start : start + LANES]
            if start + LANES > SHARD:
                v = jnp.where(lane < SHARD - start, v, -1e30)
                logits[at, start : start + LANES] = v
            tiles.append(v)
        top = mx_b[at, :]
        label = l_b[at, :]
        new = top
        for v in tiles:
            new = jnp.maximum(new, v)
        mx_b[at, :] = new
        scale = jnp.exp2((0.5 * LOG2E) * (top - new))
        soft = soft_b[at, :] * scale
        hard = hard_b[at, :] * (scale * scale)
        picked = pick_b[at, :]
        for i, v in enumerate(tiles):
            if i % BLOCK_TILES == 0:
                here = label - float(c * FWD + i * LANES)
            e = jnp.exp2((0.5 * LOG2E) * (v - new))
            soft = soft + e
            hard = hard + e * e
            picked = picked + jnp.where(places[i % BLOCK_TILES] == here, v, 0.0)
        soft_b[at, :] = soft
        hard_b[at, :] = hard
        pick_b[at, :] = picked

    for c in range(FWDS + 1):
        if c > 0:
            for s in range(TOK // ROWS):
                student_sums(c - 1, s)
        if c < FWDS:
            forward(c)

    wide_lane = lax.broadcasted_iota(jnp.int32, (TOK, LANES), 1)
    top = mx_b[...]
    m = jnp.max(top, axis=1, keepdims=True)
    scale = jnp.exp2((0.5 * LOG2E) * (top - m))
    soft = jnp.sum(soft_b[...] * scale, axis=1, keepdims=True)
    hard = jnp.sum(hard_b[...] * (scale * scale), axis=1, keepdims=True)
    picked = jnp.sum(pick_b[...], axis=1, keepdims=True)
    stat = jnp.where(wide_lane == 0, m, jnp.where(wide_lane == 1, soft, hard))
    st_src[...] = jnp.where(wide_lane == 3, picked, stat).T[0:8, :]

    def send_stats(k, _):
        remote(
            st_src, st_land.at[me], ms.at[1], mr.at[1], lax.rem(me + k, N)
        ).start()
        return 0

    pltpu.make_async_copy(st_src, st_land.at[me], mr.at[1]).start()
    lax.fori_loop(1, N, send_stats, 0)
    send_piece(2)
    send_piece(3)
    send_piece(4)
    wait_for(st_land, mr.at[1])

    top = st_land[0, 0:1, :]
    for s in range(1, N):
        top = jnp.maximum(top, st_land[s, 0:1, :])
    soft = jnp.zeros((1, TOK), F32)
    hard = jnp.zeros((1, TOK), F32)
    picked = jnp.zeros((1, TOK), F32)
    for s in range(N):
        stat = st_land[s]
        scale = jnp.exp2((0.5 * LOG2E) * (stat[0:1] - top))
        soft = soft + stat[1:2] * scale
        hard = hard + stat[2:3] * (scale * scale)
        picked = picked + stat[3:4]
    lse_soft = 0.5 * top + jnp.log(soft)
    rows_v[0:1, :] = lse_soft
    rows_v[1:2, :] = top + jnp.log(hard)
    rows_v[2:3, :] = picked
    columns = jnp.concatenate(
        [
            LOG2E * lse_soft,
            0.5 * cot[...] * (soft * soft) / hard,
            jnp.zeros((LANES - 2, TOK), F32),
        ],
        axis=0,
    ).T
    a_b[...] = jnp.broadcast_to(columns[:, 0:1], (TOK, LANES))
    b_b[...] = jnp.broadcast_to(columns[:, 1:2], (TOK, LANES))
    cross_b[...] = zeros
    inner_b[...] = zeros
    fg[...] = jnp.zeros((TOK, D), F32)
    wait_for(lse_land, mr.at[0])

    off = lax.rem(me * SHARD, LANES)
    shift = lax.rem(LANES - off, LANES)
    keep = lane < LANES - off
    skip = lax.div(me * SHARD, LANES) - first_tile(me)
    partner = chip * 2 + (1 - core)

    def wait_piece(c):
        first, count = PIECES[c]
        wait_for(land.at[:, first * LANES : (first + count) * LANES], tr.at[c])

    def gradient(c, s, g_v):
        at = pl.ds(s * ROWS, ROWS)
        lse_s, b, ct = a_b[at, :], b_b[at, :], c_b[at, :]
        label = l_b[at, :] - jnp.float32(c * BLOCK)
        lse_t = lse_land[at, :]
        half = 0.5 * ct
        cross, inner = cross_b[at, :], inner_b[at, :]

        def turned(i):
            tile = jnp.minimum(c * BLOCK_TILES + i + skip, MOST - 1)
            start = pl.multiple_of(tile * LANES, LANES)
            return pltpu.roll(land[at, pl.ds(start, LANES)].astype(F32), shift, 1)

        here = turned(0)
        for i in range(BLOCK_TILES):
            after = turned(i + 1)
            x = jnp.where(keep, here, after)
            here = after
            v = logits[at, pl.ds(pl.multiple_of(c * BLOCK + i * LANES, LANES), LANES)]
            p = jnp.exp2((0.5 * LOG2E) * x - lse_t)
            e = jnp.exp2((0.5 * LOG2E) * v - lse_s)
            if i == BLOCK_TILES - 1:
                p = jnp.where(lane < SHARD - i * LANES - c * BLOCK, p, 0.0)
            cross = cross + p * (x - v)
            g = e * (ct + e * b) - ct * p
            g = g - jnp.where(places[i] == label, half, 0.0)
            g = g.astype(BF16)
            g_v[at, i * LANES : (i + 1) * LANES] = g
            inner = inner + g.astype(F32) * v
        cross_b[at, :] = cross
        inner_b[at, :] = inner

    wait_piece(0)
    for s in range(TOK // ROWS):
        gradient(0, s, g_now)

    def step(c, _):
        for p in range(1, len(PIECES)):

            @pl.when(c + 1 == FIRST_BLOCK[p])
            def _():
                wait_piece(p)

        for s in range(TOK // ROWS):
            gradient(c + 1, s, g_next)
        rows = pl.ds(pl.multiple_of(c * BLOCK, BLOCK), BLOCK)
        fg[...] += jnp.dot(g_now[...], w[rows, :], preferred_element_type=F32)
        g_now[...] = g_next[...]
        return 0

    lax.fori_loop(0, BLOCKS - 1, step, 0)

    def half_of(n, c):
        return fg[:, pl.ds(pl.multiple_of((2 * n + c) * OWN, OWN), OWN)]

    for h in range(2):
        cols = slice(h * (D // 2), (h + 1) * (D // 2))
        fg[:, cols] += jnp.dot(
            g_now[...], w[PAD - BLOCK :, cols], preferred_element_type=F32
        )
        for n in range(h * CHIPS // 2, (h + 1) * CHIPS // 2):
            cx_src[n] = half_of(n, 1 - core).astype(BF16)
            remote(cx_src.at[n], cx_land.at[n], cs.at[0], cr.at[n], partner).start()

    cross = jnp.sum(cross_b[...], axis=1, keepdims=True)
    inner = jnp.sum(inner_b[...], axis=1, keepdims=True)
    stat = jnp.where(wide_lane == 0, cross, inner)
    fin_src[...] = jnp.where(wide_lane == 2, LN2 * lse_land[...], stat).T[0:8, :]

    def send_final(k, _):
        remote(
            fin_src, fin_land.at[me], ms.at[2], mr.at[2], lax.rem(me + k, N)
        ).start()
        return 0

    pltpu.make_async_copy(fin_src, fin_land.at[me], mr.at[2]).start()
    lax.fori_loop(1, N, send_final, 0)

    def own_half(n):
        return half_of(n, core) + cx_land[n].astype(F32)

    def share(k, _):
        n = lax.rem(chip + 1 + k, CHIPS)
        wait_for(cx_land.at[n], cr.at[n])
        rs_src[n] = own_half(n).astype(BF16)
        remote(rs_src.at[n], rs_land.at[chip], rs, rr, n * 2 + core).start()
        return 0

    lax.fori_loop(0, CHIPS - 1, share, 0)
    wait_for(cx_land.at[chip], cr.at[chip])

    wait_for(fin_land, mr.at[2])
    cross = jnp.zeros((1, TOK), F32)
    inner = jnp.zeros((1, TOK), F32)
    for s in range(N):
        stat = fin_land[s]
        cross = cross + stat[0:1]
        inner = inner + stat[1:2]
    kl = 0.5 * cross - fin_src[2:3, :] + rows_v[0:1, :]
    loss[...] = 2.0 * kl + 0.5 * (rows_v[1:2, :] - rows_v[2:3, :])
    columns = jnp.concatenate(
        [inner * (1.0 / D), jnp.zeros((LANES - 1, TOK), F32)], axis=0
    ).T
    a_b[...] = jnp.broadcast_to(columns[:, 0:1], (TOK, LANES))

    wait_for(rs_land.at[0 : CHIPS - 1], rr)
    mine = pl.ds(pl.multiple_of(me * OWN, OWN), OWN)
    total = own_half(chip)
    for k in range(1, CHIPS):
        total = total + rs_land[lax.rem(chip + k, CHIPS)].astype(F32)
    r = r_b[...]
    normed = hid[:, mine].astype(F32) * r
    out[...] = (r * (gain[:, mine] * total - normed * a_b[...])).astype(BF16)

    for c, (first, count) in enumerate(PIECES):
        wait_for(land.at[0 : TOK - ROWS, first * LANES : (first + count) * LANES], ts.at[c])
    wait_for(lse_land.at[0 : TOK - ROWS], ms.at[0])
    wait_for(st_land.at[0 : N - 1], ms.at[1])
    wait_for(fin_land.at[0 : N - 1], ms.at[2])
    wait_for(cx_src, cs.at[0])
    wait_for(rs_src.at[0 : CHIPS - 1], rs)


def finish(grad, loss, grad_out, loss_out):
    grad_out[...] = grad[...]
    loss_out[...] = loss[...]


def on_device(hidden, norm_gain, head_weight, teacher, labels, cotangent):
    vmem = pl.BlockSpec(memory_space=pltpu.VMEM)
    hbm = pl.BlockSpec(memory_space=pl.ANY)
    dma = pltpu.SemaphoreType.DMA
    column = pltpu.VMEM((TOK, LANES), F32)
    grad, loss = pl.pallas_call(
        kernel,
        out_shape=(
            jax.ShapeDtypeStruct((TOK, OWN), BF16),
            jax.ShapeDtypeStruct((1, TOK), F32),
        ),
        in_specs=[hbm, vmem, hbm, hbm, vmem, vmem],
        out_specs=(vmem, vmem),
        scratch_shapes=[
            pltpu.VMEM((TOK, D), BF16),
            pltpu.VMEM((PAD, D), BF16),
            pltpu.VMEM((ROWS, VOCAB), BF16),
            pltpu.VMEM((TOK, PAD + LANES), BF16),
            pltpu.VMEM((TOK, D), BF16),
            pltpu.VMEM((TOK, PAD), F32),
            pltpu.VMEM((TOK, D), F32),
            pltpu.VMEM((TOK, BLOCK), BF16),
            pltpu.VMEM((TOK, BLOCK), BF16),
            pltpu.VMEM((ROWS, LANES), F32),
            column,
            pltpu.VMEM((8, TOK), F32),
            pltpu.VMEM((N, 8, TOK), F32),
            pltpu.VMEM((8, TOK), F32),
            pltpu.VMEM((N, 8, TOK), F32),
            pltpu.VMEM((CHIPS, TOK, OWN), BF16),
            pltpu.VMEM((CHIPS, TOK, OWN), BF16),
            pltpu.VMEM((CHIPS, TOK, OWN), BF16),
            pltpu.VMEM((CHIPS, TOK, OWN), BF16),
            column, column, column, column, column, column,
            column, column, column, column, column,
            pltpu.VMEM((8, TOK), F32),
            dma((2,)), dma((BLOCKS,)), dma((len(PIECES),)), dma((len(PIECES),)),
            dma((3,)), dma((3,)), dma((1,)), dma((CHIPS,)), dma, dma,
        ],
        compiler_params=pltpu.CompilerParams(
            collective_id=0, has_side_effects=True, vmem_limit_bytes=56 * 1024 * 1024
        ),
        cost_estimate=pl.CostEstimate(
            flops=4 * TOK * D * SHARD, bytes_accessed=20_000_000, transcendentals=3_000_000
        ),
    )(
        hidden,
        norm_gain.reshape(1, D),
        head_weight.T,
        teacher,
        labels.reshape(1, TOK),
        cotangent.reshape(1, TOK),
    )
    grad, loss = pl.pallas_call(
        finish,
        out_shape=(
            jax.ShapeDtypeStruct((TOK, OWN), BF16),
            jax.ShapeDtypeStruct((1, TOK), F32),
        ),
        in_specs=[vmem, vmem],
        out_specs=(vmem, vmem),
    )(grad, loss)
    return grad, loss.reshape(TOK)


def solution(mesh):
    return jax.shard_map(
        on_device,
        mesh=mesh,
        in_specs=(P("dp", None), P(), P(None, "vocab"), P(("dp", "vocab"), None), P("dp"), P("dp")),
        out_specs=(P("dp", "vocab"), P("dp")),
        check_vma=False,
    )
```

```python
import jax
import jax.numpy as jnp
from jax import lax
from jax.experimental import pallas as pl
from jax.experimental.pallas import tpu as pltpu
from jax.sharding import PartitionSpec as P

EPSILON = 1e-05
MESH = pl.DeviceIdType.MESH
F32 = jnp.float32
BF16 = jnp.bfloat16

N = 16
TOK = 256
ROWS = TOK // N
D = 2048
VOCAB = 64128
SHARD = VOCAB // N
LANES = 128
TILES = 32
PAD = TILES * LANES
VTILES = VOCAB // LANES
MOST = TILES + 1
VALID = SHARD - (TILES - 1) * LANES
PIECES = ((0, 10), (10, 8), (18, 8), (26, 4), (30, 3))
FIRST_BLOCK = (0, 2, 4, 6, 7)
BLOCK = 512
BLOCKS = PAD // BLOCK
BLOCK_TILES = BLOCK // LANES
FWD = 1024
FWDS = PAD // FWD
LOG2E = 1.4426950408889634
LN2 = 0.6931471805599453
OWN = D // N
CHIPS = N // 2
FULL_W = (SHARD // 16) * 16


def kernel(
    hidden, gain, wt, teacher, labels, cot,
    out, loss,
    hid, w, t_v, land, feats, logits, fg, g_now, g_next,
    lse_src, lse_land, st_src, st_land, fin_src, fin_land,
    cx_src, cx_land, rs_src, rs_land,
    a_b, b_b, c_b, l_b, r_b, mx_b, soft_b, hard_b, pick_b, cross_b, inner_b, rows_v,
    loc_sem, w_sem, ts, tr, ms, mr, cs, cr, rs, rr,
):
    me = lax.axis_index("vocab")
    chip = lax.div(me, 2)
    core = lax.rem(me, 2)
    y = lax.rem(chip, 4)
    z_hi = lax.div(me, 8)
    lane = lax.broadcasted_iota(jnp.int32, (ROWS, LANES), 1)
    places = [(lane + i * LANES).astype(F32) for i in range(BLOCK_TILES)]
    my_rows = pl.ds(pl.multiple_of(me * ROWS, ROWS), ROWS)

    hid_copy = pltpu.make_async_copy(hidden, hid, loc_sem.at[0])
    hid_copy.start()
    t_copy = pltpu.make_async_copy(teacher, t_v, loc_sem.at[1])
    t_copy.start()
    w[FULL_W:PAD, :] = jnp.zeros((PAD - FULL_W, D), BF16)
    w_copies = []
    for c in range(BLOCKS):
        lo, hi = c * BLOCK, min((c + 1) * BLOCK, SHARD)
        w_copies.append(pltpu.make_async_copy(wt.at[lo:hi], w.at[lo:hi], w_sem.at[c]))
    for copy in w_copies[:2]:
        copy.start()

    barrier = pltpu.get_barrier_semaphore()

    def greet(k, _):
        pl.semaphore_signal(
            barrier, inc=1, device_id={"vocab": lax.rem(me + k, N)}, device_id_type=MESH
        )
        return 0

    lax.fori_loop(1, N, greet, 0)
    pl.semaphore_wait(barrier, N - 1)

    def remote(src, dst, send_sem, recv_sem, d):
        return pltpu.make_async_remote_copy(
            src_ref=src, dst_ref=dst, send_sem=send_sem, recv_sem=recv_sem,
            device_id={"vocab": d}, device_id_type=MESH,
        )

    def first_tile(d):
        return jnp.minimum(lax.div(d * SHARD, LANES), VTILES - MOST)

    def piece_refs(d, c):
        first, count = PIECES[c]
        start = pl.multiple_of((first_tile(d) + first) * LANES, LANES)
        return (
            teacher.at[:, pl.ds(start, count * LANES)],
            land.at[my_rows, first * LANES : (first + count) * LANES],
        )

    def send_piece(c):
        for dc in (0, 1):
            for dy, dz in ((0, 1), (1, 0), (3, 0), (2, 1), (1, 1), (2, 0), (3, 1)):
                d = (lax.rem(z_hi + dz, 2) * 4 + lax.rem(y + dy, 4)) * 2 + lax.rem(core + dc, 2)
                src, dst = piece_refs(d, c)
                remote(src, dst, ts.at[c], tr.at[c], d).start()
        sibling = chip * 2 + (1 - core)
        src, dst = piece_refs(sibling, c)
        remote(src, dst, ts.at[c], tr.at[c], sibling).start()
        src, dst = piece_refs(me, c)
        pltpu.make_async_copy(src, dst, tr.at[c]).start()

    send_piece(0)
    for copy in w_copies[2:]:
        copy.start()

    def wait_for(ref, sem):
        pltpu.make_async_copy(ref, ref, sem).wait()

    t_copy.wait()
    wide = 33
    steps = VTILES // wide
    rest = VTILES - steps * wide

    def t_tiles(i, count):
        start = i * (wide * LANES)
        return [
            t_v[:, pl.ds(pl.multiple_of(start + t * LANES, LANES), LANES)] for t in range(count)
        ]

    def tile_max(i, accs, count=wide):
        accs = list(accs)
        for t, x in enumerate(t_tiles(i, count)):
            accs[t % 4] = jnp.maximum(accs[t % 4], x)
        return tuple(accs)

    accs = tile_max(steps, (t_v[:, :LANES],) * 4, rest)
    accs = lax.fori_loop(0, steps, tile_max, accs)
    top = jnp.maximum(jnp.maximum(accs[0], accs[1]), jnp.maximum(accs[2], accs[3]))
    top = (0.5 * LOG2E) * jnp.max(top.astype(F32), axis=1, keepdims=True)

    def tile_sum(i, accs, count=wide):
        accs = list(accs)
        for t, x in enumerate(t_tiles(i, count)):
            accs[t % 4] = accs[t % 4] + jnp.exp2((0.5 * LOG2E) * x.astype(F32) - top)
        return tuple(accs)

    accs = tile_sum(steps, (jnp.zeros((ROWS, LANES), F32),) * 4, rest)
    accs = lax.fori_loop(0, steps, tile_sum, accs)
    total = jnp.sum((accs[0] + accs[1]) + (accs[2] + accs[3]), axis=1, keepdims=True)
    lse_src[...] = jnp.broadcast_to(top + LOG2E * jnp.log(total), (ROWS, LANES))

    def send_lse(k, _):
        remote(
            lse_src, lse_land.at[my_rows, :], ms.at[0], mr.at[0], lax.rem(me + k, N)
        ).start()
        return 0

    pltpu.make_async_copy(lse_src, lse_land.at[my_rows, :], mr.at[0]).start()
    lax.fori_loop(1, N, send_lse, 0)

    send_piece(1)

    local = labels[...] - me * SHARD
    inside = jnp.logical_and(local >= 0, local < SHARD)
    local = jnp.where(inside, local, -1).astype(F32)
    columns = jnp.concatenate(
        [local, cot[...], jnp.zeros((LANES - 2, TOK), F32)], axis=0
    ).T
    l_b[...] = jnp.broadcast_to(columns[:, 0:1], (TOK, LANES))
    c_b[...] = jnp.broadcast_to(columns[:, 1:2], (TOK, LANES))

    hid_copy.wait()

    tall = 64

    def make_features(s, _):
        at = pl.ds(pl.multiple_of(s * tall, tall), tall)
        acc = jnp.zeros((tall, LANES), F32)
        for t in range(D // LANES):
            h = hid[at, t * LANES : (t + 1) * LANES].astype(F32)
            acc = acc + h * h
        r = lax.rsqrt(jnp.sum(acc, axis=1, keepdims=True) * (1.0 / D) + EPSILON)
        r = jnp.broadcast_to(r, (tall, LANES))
        r_b[at, :] = r
        for t in range(D // LANES):
            cols = slice(t * LANES, (t + 1) * LANES)
            feats[at, cols] = ((hid[at, cols].astype(F32) * r) * gain[:, cols]).astype(BF16)
        return 0

    lax.fori_loop(0, TOK // tall, make_features, 0)

    zeros = jnp.zeros((TOK, LANES), F32)
    mx_b[...] = jnp.full((TOK, LANES), -1e30, F32)
    soft_b[...] = zeros
    hard_b[...] = zeros
    pick_b[...] = zeros

    def forward(c):
        for copy in w_copies[c * FWD // BLOCK : (c + 1) * FWD // BLOCK]:
            copy.wait()
        logits[:, c * FWD : (c + 1) * FWD] = lax.dot_general(
            feats[...], w[c * FWD : (c + 1) * FWD, :], (((1,), (1,)), ((), ())),
            preferred_element_type=F32,
        )

    def student_sums(c, s):
        at = slice(s * ROWS, (s + 1) * ROWS)
        tiles = []
        for i in range(FWD // LANES):
            start = c * FWD + i * LANES
            v = logits[at, start : start + LANES]
            if start + LANES > SHARD:
                v = jnp.where(lane < SHARD - start, v, -1e30)
                logits[at, start : start + LANES] = v
            tiles.append(v)
        top = mx_b[at, :]
        label = l_b[at, :]
        new = top
        for v in tiles:
            new = jnp.maximum(new, v)
        mx_b[at, :] = new
        scale = jnp.exp2((0.5 * LOG2E) * (top - new))
        soft = soft_b[at, :] * scale
        hard = hard_b[at, :] * (scale * scale)
        picked = pick_b[at, :]
        for i, v in enumerate(tiles):
            if i % BLOCK_TILES == 0:
                here = label - float(c * FWD + i * LANES)
            e = jnp.exp2((0.5 * LOG2E) * (v - new))
            soft = soft + e
            hard = hard + e * e
            picked = picked + jnp.where(places[i % BLOCK_TILES] == here, v, 0.0)
        soft_b[at, :] = soft
        hard_b[at, :] = hard
        pick_b[at, :] = picked

    for c in range(FWDS + 1):
        if c > 0:
            for s in range(TOK // ROWS):
                student_sums(c - 1, s)
        if c < FWDS:
            forward(c)

    wide_lane = lax.broadcasted_iota(jnp.int32, (TOK, LANES), 1)
    top = mx_b[...]
    m = jnp.max(top, axis=1, keepdims=True)
    scale = jnp.exp2((0.5 * LOG2E) * (top - m))
    soft = jnp.sum(soft_b[...] * scale, axis=1, keepdims=True)
    hard = jnp.sum(hard_b[...] * (scale * scale), axis=1, keepdims=True)
    picked = jnp.sum(pick_b[...], axis=1, keepdims=True)
    stat = jnp.where(wide_lane == 0, m, jnp.where(wide_lane == 1, soft, hard))
    st_src[...] = jnp.where(wide_lane == 3, picked, stat).T[0:8, :]

    def send_stats(k, _):
        remote(
            st_src, st_land.at[me], ms.at[1], mr.at[1], lax.rem(me + k, N)
        ).start()
        return 0

    pltpu.make_async_copy(st_src, st_land.at[me], mr.at[1]).start()
    lax.fori_loop(1, N, send_stats, 0)
    send_piece(2)
    send_piece(3)
    send_piece(4)
    cross_b[...] = zeros
    inner_b[...] = zeros
    fg[...] = jnp.zeros((TOK, D), F32)
    wait_for(st_land, mr.at[1])

    top = st_land[0, 0:1, :]
    for s in range(1, N):
        top = jnp.maximum(top, st_land[s, 0:1, :])
    soft = jnp.zeros((1, TOK), F32)
    hard = jnp.zeros((1, TOK), F32)
    picked = jnp.zeros((1, TOK), F32)
    for s in range(N):
        stat = st_land[s]
        scale = jnp.exp2((0.5 * LOG2E) * (stat[0:1] - top))
        soft = soft + stat[1:2] * scale
        hard = hard + stat[2:3] * (scale * scale)
        picked = picked + stat[3:4]
    lse_soft = 0.5 * top + jnp.log(soft)
    rows_v[0:1, :] = lse_soft
    rows_v[1:2, :] = top + jnp.log(hard)
    rows_v[2:3, :] = picked
    columns = jnp.concatenate(
        [
            LOG2E * lse_soft,
            0.5 * cot[...] * (soft * soft) / hard,
            jnp.zeros((LANES - 2, TOK), F32),
        ],
        axis=0,
    ).T
    a_b[...] = jnp.broadcast_to(columns[:, 0:1], (TOK, LANES))
    b_b[...] = jnp.broadcast_to(columns[:, 1:2], (TOK, LANES))
    wait_for(lse_land, mr.at[0])

    off = lax.rem(me * SHARD, LANES)
    shift = lax.rem(LANES - off, LANES)
    keep = lane < LANES - off
    skip = lax.div(me * SHARD, LANES) - first_tile(me)
    partner = chip * 2 + (1 - core)

    def wait_piece(c):
        first, count = PIECES[c]
        wait_for(land.at[:, first * LANES : (first + count) * LANES], tr.at[c])

    def gradient(c, s, g_v):
        at = pl.ds(s * ROWS, ROWS)
        lse_s, b, ct = a_b[at, :], b_b[at, :], c_b[at, :]
        label = l_b[at, :] - jnp.float32(c * BLOCK)
        lse_t = lse_land[at, :]
        half = 0.5 * ct
        cross, inner = cross_b[at, :], inner_b[at, :]

        def turned(i):
            tile = jnp.minimum(c * BLOCK_TILES + i + skip, MOST - 1)
            start = pl.multiple_of(tile * LANES, LANES)
            return pltpu.roll(land[at, pl.ds(start, LANES)].astype(F32), shift, 1)

        here = turned(0)
        for i in range(BLOCK_TILES):
            after = turned(i + 1)
            x = jnp.where(keep, here, after)
            here = after
            v = logits[at, pl.ds(pl.multiple_of(c * BLOCK + i * LANES, LANES), LANES)]
            p = jnp.exp2((0.5 * LOG2E) * x - lse_t)
            e = jnp.exp2((0.5 * LOG2E) * v - lse_s)
            if i == BLOCK_TILES - 1:
                p = jnp.where(lane < SHARD - i * LANES - c * BLOCK, p, 0.0)
            cross = cross + p * (x - v)
            g = e * (ct + e * b) - ct * p
            g = g - jnp.where(places[i] == label, half, 0.0)
            g = g.astype(BF16)
            g_v[at, i * LANES : (i + 1) * LANES] = g
            inner = inner + g.astype(F32) * v
        cross_b[at, :] = cross
        inner_b[at, :] = inner

    wait_piece(0)
    for s in range(TOK // ROWS):
        gradient(0, s, g_now)

    def step(c, _):
        for p in range(1, len(PIECES)):

            @pl.when(c + 1 == FIRST_BLOCK[p])
            def _():
                wait_piece(p)

        for s in range(TOK // ROWS):
            gradient(c + 1, s, g_next)
        rows = pl.ds(pl.multiple_of(c * BLOCK, BLOCK), BLOCK)
        fg[...] += jnp.dot(g_now[...], w[rows, :], preferred_element_type=F32)
        g_now[...] = g_next[...]
        return 0

    lax.fori_loop(0, BLOCKS - 1, step, 0)

    def half_of(n, c):
        return fg[:, pl.ds(pl.multiple_of((2 * n + c) * OWN, OWN), OWN)]

    for h in range(2):
        cols = slice(h * (D // 2), (h + 1) * (D // 2))
        fg[:, cols] += jnp.dot(
            g_now[...], w[PAD - BLOCK :, cols], preferred_element_type=F32
        )
        for n in range(h * CHIPS // 2, (h + 1) * CHIPS // 2):
            cx_src[n] = half_of(n, 1 - core).astype(BF16)
            remote(cx_src.at[n], cx_land.at[n], cs.at[0], cr.at[n], partner).start()

    cross = jnp.sum(cross_b[...], axis=1, keepdims=True)
    inner = jnp.sum(inner_b[...], axis=1, keepdims=True)
    stat = jnp.where(wide_lane == 0, cross, inner)
    fin_src[...] = jnp.where(wide_lane == 2, LN2 * lse_land[...], stat).T[0:8, :]

    def send_final(k, _):
        remote(
            fin_src, fin_land.at[me], ms.at[2], mr.at[2], lax.rem(me + k, N)
        ).start()
        return 0

    pltpu.make_async_copy(fin_src, fin_land.at[me], mr.at[2]).start()
    lax.fori_loop(1, N, send_final, 0)

    def own_half(n):
        return half_of(n, core) + cx_land[n].astype(F32)

    for dy, dz in ((2, 1), (2, 0), (1, 1), (3, 0), (3, 1), (1, 0), (0, 1)):
        n = lax.rem(z_hi + dz, 2) * 4 + lax.rem(y + dy, 4)
        wait_for(cx_land.at[n], cr.at[n])
        rs_src[n] = own_half(n).astype(BF16)
        remote(rs_src.at[n], rs_land.at[chip], rs, rr, n * 2 + core).start()

    wait_for(cx_land.at[chip], cr.at[chip])

    wait_for(fin_land, mr.at[2])
    cross = jnp.zeros((1, TOK), F32)
    inner = jnp.zeros((1, TOK), F32)
    for s in range(N):
        stat = fin_land[s]
        cross = cross + stat[0:1]
        inner = inner + stat[1:2]
    kl = 0.5 * cross - fin_src[2:3, :] + rows_v[0:1, :]
    loss[...] = 2.0 * kl + 0.5 * (rows_v[1:2, :] - rows_v[2:3, :])
    columns = jnp.concatenate(
        [inner * (1.0 / D), jnp.zeros((LANES - 1, TOK), F32)], axis=0
    ).T
    a_b[...] = jnp.broadcast_to(columns[:, 0:1], (TOK, LANES))

    wait_for(rs_land.at[0 : CHIPS - 1], rr)
    mine = pl.ds(pl.multiple_of(me * OWN, OWN), OWN)
    total = own_half(chip)
    for k in range(1, CHIPS):
        total = total + rs_land[lax.rem(chip + k, CHIPS)].astype(F32)
    r = r_b[...]
    normed = hid[:, mine].astype(F32) * r
    out[...] = (r * (gain[:, mine] * total - normed * a_b[...])).astype(BF16)

    for c, (first, count) in enumerate(PIECES):
        wait_for(land.at[0 : TOK - ROWS, first * LANES : (first + count) * LANES], ts.at[c])
    wait_for(lse_land.at[0 : TOK - ROWS], ms.at[0])
    wait_for(st_land.at[0 : N - 1], ms.at[1])
    wait_for(fin_land.at[0 : N - 1], ms.at[2])
    wait_for(cx_src, cs.at[0])
    wait_for(rs_src.at[0 : CHIPS - 1], rs)


def finish(grad, loss, grad_out, loss_out):
    grad_out[...] = grad[...]
    loss_out[...] = loss[...]


def on_device(hidden, norm_gain, head_weight, teacher, labels, cotangent):
    vmem = pl.BlockSpec(memory_space=pltpu.VMEM)
    hbm = pl.BlockSpec(memory_space=pl.ANY)
    dma = pltpu.SemaphoreType.DMA
    column = pltpu.VMEM((TOK, LANES), F32)
    grad, loss = pl.pallas_call(
        kernel,
        out_shape=(
            jax.ShapeDtypeStruct((TOK, OWN), BF16),
            jax.ShapeDtypeStruct((1, TOK), F32),
        ),
        in_specs=[hbm, vmem, hbm, hbm, vmem, vmem],
        out_specs=(vmem, vmem),
        scratch_shapes=[
            pltpu.VMEM((TOK, D), BF16),
            pltpu.VMEM((PAD, D), BF16),
            pltpu.VMEM((ROWS, VOCAB), BF16),
            pltpu.VMEM((TOK, PAD + LANES), BF16),
            pltpu.VMEM((TOK, D), BF16),
            pltpu.VMEM((TOK, PAD), F32),
            pltpu.VMEM((TOK, D), F32),
            pltpu.VMEM((TOK, BLOCK), BF16),
            pltpu.VMEM((TOK, BLOCK), BF16),
            pltpu.VMEM((ROWS, LANES), F32),
            column,
            pltpu.VMEM((8, TOK), F32),
            pltpu.VMEM((N, 8, TOK), F32),
            pltpu.VMEM((8, TOK), F32),
            pltpu.VMEM((N, 8, TOK), F32),
            pltpu.VMEM((CHIPS, TOK, OWN), BF16),
            pltpu.VMEM((CHIPS, TOK, OWN), BF16),
            pltpu.VMEM((CHIPS, TOK, OWN), BF16),
            pltpu.VMEM((CHIPS, TOK, OWN), BF16),
            column, column, column, column, column, column,
            column, column, column, column, column,
            pltpu.VMEM((8, TOK), F32),
            dma((2,)), dma((BLOCKS,)), dma((len(PIECES),)), dma((len(PIECES),)),
            dma((3,)), dma((3,)), dma((1,)), dma((CHIPS,)), dma, dma,
        ],
        compiler_params=pltpu.CompilerParams(
            collective_id=0, has_side_effects=True, vmem_limit_bytes=56 * 1024 * 1024
        ),
        cost_estimate=pl.CostEstimate(
            flops=4 * TOK * D * SHARD, bytes_accessed=20_000_000, transcendentals=3_000_000
        ),
    )(
        hidden,
        norm_gain.reshape(1, D),
        head_weight.T,
        teacher,
        labels.reshape(1, TOK),
        cotangent.reshape(1, TOK),
    )
    grad, loss = pl.pallas_call(
        finish,
        out_shape=(
            jax.ShapeDtypeStruct((TOK, OWN), BF16),
            jax.ShapeDtypeStruct((1, TOK), F32),
        ),
        in_specs=[vmem, vmem],
        out_specs=(vmem, vmem),
    )(grad, loss)
    return grad, loss.reshape(TOK)


def solution(mesh):
    return jax.shard_map(
        on_device,
        mesh=mesh,
        in_specs=(P("dp", None), P(), P(None, "vocab"), P(("dp", "vocab"), None), P("dp"), P("dp")),
        out_specs=(P("dp", "vocab"), P("dp")),
        check_vma=False,
    )
```
